512 devices in a mesh: lon: 16 (over z, y_hi), lat: 8 (over y_lo, core), lev: 4 (over x).
Axes of the slice: x: 4, y: 8 (y_hi: 2, y_lo: 4; y = y_hi * 4 + y_lo), z: 8, core: 2. Of those that a mesh axis runs over, the one named last changes fastest.
Arguments:
- fields: bfloat16 [8, 48, 192, 192], P('lev', 'lat', 'lon'), may hold values from -7 to 7
- w_qkv: bfloat16 [4, 192, 576], replicated, may hold values from -7 to 7
- w_out: bfloat16 [4, 192, 192], replicated, may hold values from -0.4375 to 0.4375
- w_up: bfloat16 [4, 192, 768], replicated, may hold values from -0.4375 to 0.4375
- w_down: bfloat16 [4, 768, 192], replicated, may hold values from -0.21875 to 0.21875
- gains: float32 [4, 2, 192], replicated, may hold values from 0.25 to 1.75
- bias_table: bfloat16 [4, 4, 8, 6, 3312], P(None, None, 'lat'), may hold values from -4 to 4
- labels: int32 [8, 48, 192], P(None, 'lat', 'lon'), may hold values from 0 to 7, as said below
Outputs:
- fields_out: bfloat16 [8, 48, 192, 192], P('lev', 'lat', 'lon')
The draws below stay inside these ranges and needn't reach their ends.
Inputs may be any that keep to these rules, and one draw needn't show every extreme that they name: labels[z, y, x] = e + 2 f + 4 g, the same for every x, where e is 1 when z >= 7, f is 1 when y >= 45, and g is 1 when the row (y + 3) mod 48 is one of the first n or the last s padding rows of the grid, with n and s between 1 and 3.
All inputs are finite; a program needn't handle non-finite values.
Results may differ from the reference program's by a relative error of at most 0.025.
Values may be sent and summed in bfloat16 or wider, within the bound.
No kernel may reach another device: no remote copies, remote signals or barrier semaphores. Data moves between devices by JAX's collectives and lax.ppermute only.
A program may use at most 64 MiB of HBM per device.

```python
import jax
import jax.numpy as jnp
from jax import lax

D = 192
HEADS = 6
FF = 768
WZ = 2
WY = 6
WX = 12
BLOCKS = 4
HD = 32
LEVW = 4
Z = 8
LATW = 8
LONW = 16
LAT = 48
LON = 192
POS = 3312


def draw_fields(key, part):
    values = jnp.clip(jax.random.normal(key, (Z, LAT, LON, D), jnp.float32), -6.0, 6.0)
    return values.astype(jnp.bfloat16)


def draw_w_qkv(key, part):
    base_key = jax.random.fold_in(key, 0)
    limit_value = 6.0 * D ** (-0.5)
    weights = jnp.clip(jax.random.normal(base_key, (BLOCKS, D, 3 * D), jnp.float32) * D ** (-0.5), -limit_value, limit_value)
    return weights.astype(jnp.bfloat16)


def draw_labels(key, part):
    pad_counts = jax.random.randint(jax.random.fold_in(key, 17), (2,), 1, WY // 2 + 1, dtype=jnp.int32)
    frame_levels = jnp.arange(Z, dtype=jnp.int32)
    frame_rows = jnp.arange(LAT, dtype=jnp.int32)
    level_wrap = (frame_levels >= Z - WZ // 2).astype(jnp.int32)
    row_wrap = (frame_rows >= LAT - WY // 2).astype(jnp.int32)
    grid_rows = (frame_rows + WY // 2) % LAT
    padding = ((grid_rows < pad_counts[0]) | (grid_rows >= LAT - pad_counts[1])).astype(jnp.int32)
    plane = 2 * row_wrap + 4 * padding
    region = level_wrap[:, None] + plane[None, :]
    return jnp.broadcast_to(region[:, :, None], (Z, LAT, LON)).astype(jnp.int32)


def steps_of(own_key, extent, cuts, smallest, top_value):
    loudness = 1.0
    for axis_at, parts in cuts:
        draws = jax.random.uniform(jax.random.fold_in(jax.random.fold_in(own_key, 6), axis_at), (parts,), jnp.float32, smallest / len(cuts), top_value / len(cuts))
        loudness = loudness * jnp.repeat(jnp.exp(draws), extent[axis_at] // parts).reshape((-1,) + (1,) * (len(extent) - 1 - axis_at))
    return loudness


def noise(stream_key, extent, scale, limit, shards=(), held_as=jnp.bfloat16):
    values = jax.random.normal(stream_key, extent, jnp.float32) * scale
    if len(shards) > 0:
        values = steps_of(stream_key, extent, shards, -0.22, 0.18) * values
    return jnp.clip(values, min=-limit, max=limit).astype(held_as)


def setup_inputs(seed: int = 0) -> dict:
    key_list = jax.random.split(jax.random.key(seed), 9)
    fields = draw_fields(jax.random.fold_in(key_list[8], 71), 0)
    w_qkv = draw_w_qkv(jax.random.fold_in(key_list[8], 71), 0)
    w_out = noise(key_list[2], (BLOCKS, D, D), D ** -0.5, 0.4375)
    w_up = noise(key_list[3], (BLOCKS, D, FF), D ** -0.5, 0.4375)
    w_down = noise(key_list[4], (BLOCKS, FF, D), FF ** -0.5, 0.21875)
    gains = jnp.clip(1.0 + 0.15 * jax.random.normal(key_list[5], (BLOCKS, 2, D), jnp.float32), 0.25, 1.75)
    bias_table = noise(key_list[6], (BLOCKS, LEVW, LATW, HEADS, POS), 1.0, 4.0, ((2, 8),))
    labels = draw_labels(jax.random.fold_in(key_list[8], 71), 0)
    return dict(fields=fields, w_qkv=w_qkv, w_out=w_out, w_up=w_up, w_down=w_down, gains=gains, bias_table=bias_table, labels=labels)


def layer_norm(values, gain_row):
    floats = values.astype(jnp.float32)
    center = floats - lax.optimization_barrier(jnp.mean(floats, axis=-1, keepdims=True))
    spread = lax.optimization_barrier(jnp.mean(center * center, axis=-1, keepdims=True))
    return center * lax.rsqrt(spread + 1e-05) * gain_row.astype(jnp.float32)

def expand_bias(bias_rows):
    row_count = bias_rows.shape[0]
    shaped = bias_rows.astype(jnp.float32).reshape(row_count, HEADS, WZ, WZ, WY, WY, 2 * WX - 1)
    offset = jnp.arange(WX, dtype=jnp.int32)[:, None] - jnp.arange(WX, dtype=jnp.int32)[None, :] + (WX - 1)
    selector = (offset[:, :, None] == jnp.arange(2 * WX - 1, dtype=jnp.int32)[None, None, :]).astype(jnp.float32)
    spread_out = jnp.einsum('nhpqrsd,abd->nhpraqsb', shaped, selector, precision=lax.Precision.HIGHEST)
    size_window = WZ * WY * WX
    return spread_out.reshape(row_count, HEADS, size_window, size_window)

def attend(queries, key_part, val_part, bias_full, query_labels, key_labels):
    scores = jnp.einsum('wahd,wbhd->whab', queries.astype(jnp.float32), key_part.astype(jnp.float32))
    scores = scores * HD ** (-0.5)
    groups = bias_full.shape[0]
    scores = (scores.reshape((groups, -1) + scores.shape[1:]) + bias_full[:, None]).reshape(scores.shape)
    if query_labels is None:
        allowed = jnp.ones(scores.shape, dtype=bool)
    else:
        allowed = query_labels[:, None, :, None] == key_labels[:, None, None, :]
    masked = jnp.where(allowed, scores, -1e+30)
    row_max = lax.optimization_barrier(jnp.max(masked, axis=-1, keepdims=True))
    exp_terms = jnp.where(allowed, jnp.exp(masked - row_max), 0.0)
    weights = (exp_terms / lax.optimization_barrier(jnp.sum(exp_terms, axis=-1, keepdims=True))).astype(jnp.bfloat16)
    mixed_heads = jnp.einsum('whab,wbhd->wahd', weights.astype(jnp.float32), val_part.astype(jnp.float32))
    return mixed_heads.astype(jnp.bfloat16)

def attention_layer(frame_grid, qkv_weight, out_weight, bias_rows, labels, use_labels):
    level_windows = Z // WZ
    size_window = WZ * WY * WX
    proj_qkv = jnp.dot(frame_grid.reshape(-1, D), qkv_weight, preferred_element_type=jnp.float32).astype(jnp.bfloat16)
    arranged = proj_qkv.reshape(level_windows, WZ, LATW, WY, LONW, WX, 3 * D).transpose(2, 0, 4, 1, 3, 5, 6)
    arranged = arranged.reshape(LATW, level_windows * LONW, size_window, 3 * D)
    label_grid = labels.reshape(level_windows, WZ, LATW, WY, LONW, WX).transpose(2, 0, 4, 1, 3, 5)
    label_grid = label_grid.reshape(LATW, level_windows * LONW, size_window)
    row_tables = bias_rows.transpose(1, 0, 2, 3)

    def one_row(inputs):
        row_qkv, row_table, row_labels = inputs
        bias_full = expand_bias(row_table)
        queries = row_qkv[:, :, :D].reshape(-1, size_window, HEADS, HD)
        key_part = row_qkv[:, :, D:2 * D].reshape(-1, size_window, HEADS, HD)
        val_part = row_qkv[:, :, 2 * D:].reshape(-1, size_window, HEADS, HD)
        if use_labels:
            mixed_heads = attend(queries, key_part, val_part, bias_full, row_labels, row_labels)
        else:
            mixed_heads = attend(queries, key_part, val_part, bias_full, None, None)
        return mixed_heads.reshape(-1, size_window, D)
    window_out = lax.map(one_row, (arranged, row_tables, label_grid))
    grid_rows = window_out.reshape(LATW, level_windows, LONW, WZ, WY, WX, D).transpose(1, 3, 0, 4, 2, 5, 6).reshape(-1, D)
    projected = jnp.dot(grid_rows, out_weight, preferred_element_type=jnp.float32).astype(jnp.bfloat16)
    return projected.reshape(Z, LAT, LON, D)

def reference(fields, w_qkv, w_out, w_up, w_down, gains, bias_table, labels):
    stream = fields
    half_shift = (WZ // 2, WY // 2, WX // 2)
    for block_idx in range(BLOCKS):
        shifted = block_idx % 2 == 1
        normed = layer_norm(stream, gains[block_idx, 0]).astype(jnp.bfloat16)
        frame_grid = normed
        if shifted:
            frame_grid = jnp.roll(normed, (-half_shift[0], -half_shift[1], -half_shift[2]), axis=(0, 1, 2))
        attended = attention_layer(frame_grid, w_qkv[block_idx], w_out[block_idx], bias_table[block_idx], labels, shifted)
        if shifted:
            attended = jnp.roll(attended, half_shift, axis=(0, 1, 2))
        middle = (stream.astype(jnp.float32) + attended.astype(jnp.float32)).astype(jnp.bfloat16)
        normed_two = layer_norm(middle, gains[block_idx, 1]).astype(jnp.bfloat16)
        hidden = jax.nn.gelu(jnp.dot(normed_two.reshape(-1, D), w_up[block_idx], preferred_element_type=jnp.float32), approximate=False).astype(jnp.bfloat16)
        down_rows = jnp.dot(hidden, w_down[block_idx], preferred_element_type=jnp.float32).reshape(Z, LAT, LON, D)
        stream = (middle.astype(jnp.float32) + down_rows).astype(jnp.bfloat16)
    return stream
```

```python
import functools

import jax
import jax.numpy as jnp
import numpy as np
from jax import lax
from jax.experimental import pallas as pl
from jax.experimental.pallas import tpu as pltpu
from jax.sharding import PartitionSpec as P

HEADS = 6
HD = 32
WZ = 2
WY = 6
WX = 12
BLOCKS = 4
D = 192
FF = 768
T = WZ * WY * WX
OFFS = 2 * WX - 1
POS = 3312
WIDE = 3328
SLOT = 32
QSLOT = 24
NEG = -1e30
MASK_AT = 192
BF = jnp.bfloat16
F32 = jnp.float32


def octant_maps():
    to_oct = np.zeros((8 * SLOT, T), np.float32)
    back = np.zeros((T, 8 * QSLOT), np.float32)
    for z in range(2):
        for y in range(6):
            for x in range(12):
                yh, yl, xh, xl = y // 3, y % 3, x // 6, x % 6
                tok = z * 72 + y * 12 + x
                slot = yl * 6 + xl
                to_oct[((xh * 2 + yh) * 2 + z) * SLOT + slot, tok] = 1.0
                back[tok, ((z * 2 + yh) * 2 + xh) * QSLOT + slot] = 1.0
    return to_oct, back


def selectors():
    regular = np.zeros((2, 256, 256), np.float32)
    for zq in range(2):
        for yq in range(6):
            for xq in range(12):
                regular[zq, yq * OFFS + 11 - xq, zq * 72 + yq * 12 + xq] = 1.0
    shifted = np.zeros((2, 256, 8 * SLOT), np.float32)
    pad = np.full((1, 8 * SLOT), NEG, np.float32)
    for zk in range(2):
        for yk in range(2):
            for xk in range(2):
                for yl in range(3):
                    for xl in range(6):
                        lane = ((zk * 2 + yk) * 2 + xk) * SLOT + yl * 6 + xl
                        yq, xq = yk * 3 + yl, xk * 6 + xl
                        shifted[zk, yq * OFFS + 11 - xq, lane] = 1.0
                        shifted[zk, MASK_AT + yq, lane] = 1.0
                        pad[0, lane] = 0.0
    return regular.reshape(512, 256), shifted.reshape(512, 8 * SLOT), pad


def dot(a, b):
    return jnp.dot(a, b, preferred_element_type=F32)


def dot_t(a, b):
    return lax.dot_general(a, b, (((1,), (1,)), ((), ())), preferred_element_type=F32)


def layer_norm(values, gain):
    center = values - jnp.mean(values, axis=-1, keepdims=True)
    spread = jnp.mean(center * center, axis=-1, keepdims=True)
    return (center * lax.rsqrt(spread + 1e-05) * gain).astype(BF)


def head_mask(rows):
    lane_head = lax.broadcasted_iota(jnp.int32, (rows, D), 1) // HD
    return [lane_head == h for h in range(HEADS)]


def spread_heads(q, masks):
    return jnp.concatenate([jnp.where(m, q, 0.0) for m in masks], axis=0).astype(BF)


def softmax_mix(scores, keys_v, rows, masks):
    top = jnp.max(scores, axis=-1, keepdims=True)
    terms = jnp.exp(scores - top)
    total = 1.0 / jnp.sum(terms, axis=-1, keepdims=True)
    mixed = dot(terms.astype(BF), keys_v) * total
    out = mixed[0:rows]
    for h in range(1, HEADS):
        out = jnp.where(masks[h], mixed[h * rows : (h + 1) * rows], out)
    return out


def feed_forward(middle, gain, w_up, w_down):
    normed = layer_norm(middle.astype(F32), gain)
    up = dot(normed, w_up)
    hidden = (0.5 * up * (1.0 + lax.erf(up * np.float32(0.5**0.5)))).astype(BF)
    return (middle.astype(F32) + dot(hidden, w_down)).astype(BF)


def regular_block(stream, gain0, gain1, w_qkv, w_out, w_up, w_down, bias):
    normed = layer_norm(stream.astype(F32), gain0)
    qkv = dot(normed, w_qkv)
    q = qkv[:, :D].astype(BF).astype(F32) * np.float32(HD**-0.5)
    k = qkv[:, D : 2 * D].astype(BF)
    v = qkv[:, 2 * D :].astype(BF)
    masks = head_mask(T)
    scores = dot_t(spread_heads(q, masks), k) + jnp.concatenate([bias[0], bias[1, :, : T - 128]], 1)
    heads_out = softmax_mix(scores, v, T, masks).astype(BF)
    attended = dot(heads_out, w_out).astype(BF)
    middle = (stream.astype(F32) + attended.astype(F32)).astype(BF)
    return feed_forward(middle, gain1, w_up, w_down)


def shifted_block(stream, slabs, gain1, w_qkv, w_out, w_up, w_down, bias_ref, back, k_ref, v_ref):
    for i, slab in enumerate(slabs):
        kv = dot(slab[...], w_qkv[:, D:])
        k_ref[i] = kv[:, :D].astype(BF).reshape(4, 4, SLOT, D)
        v_ref[i] = kv[:, D:].astype(BF).reshape(4, 4, SLOT, D)
    own = []
    for z in range(2):
        for yh in range(2):
            row = ((1 + yh) * 4 + 1) * SLOT
            own.append(slabs[1 + z][row : row + 2 * SLOT, :])
    q = dot(jnp.concatenate(own, axis=0), w_qkv[:, :D]).astype(BF).astype(F32) * np.float32(
        HD**-0.5
    )
    masks = head_mask(QSLOT)
    outs = []
    for z in range(2):
        for yh in range(2):
            for xh in range(2):
                w = (z * 2 + yh) * 2 + xh
                ks = k_ref[2 * z : 2 * z + 2, 2 * yh : 2 * yh + 2, 2 * xh : 2 * xh + 2]
                vs = v_ref[2 * z : 2 * z + 2, 2 * yh : 2 * yh + 2, 2 * xh : 2 * xh + 2]
                scores = dot_t(
                    spread_heads(q[w * SLOT : w * SLOT + QSLOT], masks),
                    ks.reshape(8 * SLOT, D),
                )
                rows = slice(w * 144, (w + 1) * 144)
                scores = scores + jnp.concatenate([bias_ref[0, rows], bias_ref[1, rows]], 1)
                outs.append(softmax_mix(scores, vs.reshape(8 * SLOT, D), QSLOT, masks))
    heads_out = jnp.concatenate(outs, axis=0).astype(BF)
    attended = dot(heads_out, w_out).astype(BF)
    attended = dot(back, attended)
    middle = (stream.astype(F32) + attended).astype(BF)
    return feed_forward(middle, gain1, w_up, w_down)


def bias_rolls(lhs_ref, sel):
    parts = [jnp.concatenate([lhs_ref[k, 0], lhs_ref[k, 1]], axis=1) for k in range(2)]
    lane = lax.broadcasted_iota(jnp.int32, parts[0].shape, 1)
    fixed = [jnp.where(lane >= MASK_AT, p, 0.0) for p in parts]
    moving = [jnp.where(lane < MASK_AT, p, 0.0) for p in parts]
    for xp in range(WX):
        rows = [
            (pltpu.roll(m, 256 - xp, 1) if xp else m) + f for m, f in zip(moving, fixed)
        ]
        yield xp, dot(jnp.concatenate(rows, axis=1).astype(BF), sel)


def put(ref, rows, value):
    for k in range(2):
        ref[k, rows, :] = value[:, k * 128 : (k + 1) * 128]


def widened(table, extra):
    wide = jnp.concatenate([table, jnp.zeros((HEADS, 256 - 6 * OFFS), F32)], axis=1)
    return wide if extra is None else wide + extra


def bias_regular_kernel(at, table_ref, sel_ref, out_ref, table, lhs):
    table[...] = table_ref[at].astype(F32)
    for zp in range(2):
        for zq in range(2):
            for yp in range(6):
                start = ((zp * 2 + zq) * 6 + yp) * 6 * OFFS
                part = widened(table[:, start : start + 6 * OFFS], None)
                put(lhs.at[zq], pl.ds(zp * 6 + yp, HEADS, stride=12), part)
    for xp, rows in bias_rolls(lhs, sel_ref[...]):
        put(out_ref, pl.ds(xp, 72, stride=WX), rows)


def bias_shifted_kernel(at, own_ref, south_ref, sel_ref, pad_ref, out_ref, table, lhs):
    lane = lax.broadcasted_iota(jnp.int32, (1, 128), 1)
    in_mask = (lane >= MASK_AT - 128) & (lane < MASK_AT - 122)
    lhs[...] = jnp.zeros_like(lhs)
    for z in range(2):
        for yh in range(2):
            source = own_ref if yh else south_ref
            table[...] = source[at, z].astype(F32)
            tags = table[0:1, WIDE - 128 : WIDE]
            first = POS - (WIDE - 128)
            zp = 1 - z
            for zq in range(2):
                turn = (MASK_AT - 128 - first - zq * 6) % 128
                keys = pltpu.roll(tags, turn, 1)
                for yl in range(3):
                    yp = yl if yh else yl + 3
                    mine = jnp.sum(
                        jnp.where(lane == first + zp * 6 + yp, tags, 0.0), axis=1, keepdims=True
                    )
                    mask = jnp.where(in_mask & (keys != mine), NEG, 0.0)
                    mask = jnp.concatenate([jnp.zeros((1, 128), F32), mask], axis=1)
                    start = ((zp * 2 + zq) * 6 + yp) * 6 * OFFS
                    part = widened(table[:, start : start + 6 * OFFS], mask)
                    put(lhs.at[zq], pl.ds((z * 2 + yh) * QSLOT + yl, HEADS, stride=4), part)
    for xp, rows in bias_rolls(lhs, sel_ref[...]):
        rows = rows + pad_ref[...]
        x = (xp + 6) % 12
        xh, xl = x // 6, x % 6
        for zy in range(4):
            base = (zy * 2 + xh) * 144 + xl
            put(out_ref, pl.ds(base, QSLOT, stride=6), rows[zy * QSLOT : (zy + 1) * QSLOT])


def first_kernel(x, gains, w_qkv, w_out, w_up, w_down, bias, to_oct, stream_out, west, east):
    stream = regular_block(
        x[...], gains[0, 0:1], gains[0, 1:2], w_qkv[0], w_out[0], w_up[0], w_down[0], bias
    )
    stream_out[...] = stream
    normed = layer_norm(stream.astype(F32), gains[1, 0:1])
    octs = dot(to_oct[...], normed).astype(BF)
    west[...] = octs[: 4 * SLOT]
    east[...] = octs[4 * SLOT :]


def middle_kernel(
    stream_in, z0, z1, z2, z3, gains, w_qkv, w_out, w_up, w_down, bias1, bias2, to_oct, back,
    stream_out, west, east, k_ref, v_ref,
):
    stream = shifted_block(
        stream_in[...], (z0, z1, z2, z3), gains[1, 1:2], w_qkv[1], w_out[1], w_up[1], w_down[1],
        bias1, back[...], k_ref, v_ref,
    )
    stream = regular_block(
        stream, gains[2, 0:1], gains[2, 1:2], w_qkv[2], w_out[2], w_up[2], w_down[2], bias2
    )
    stream_out[...] = stream
    normed = layer_norm(stream.astype(F32), gains[3, 0:1])
    octs = dot(to_oct[...], normed).astype(BF)
    west[...] = octs[: 4 * SLOT]
    east[...] = octs[4 * SLOT :]


def last_kernel(
    stream_in, z0, z1, z2, z3, gains, w_qkv, w_out, w_up, w_down, bias3, back, out, k_ref, v_ref
):
    out[...] = shifted_block(
        stream_in[...], (z0, z1, z2, z3), gains[3, 1:2], w_qkv[3], w_out[3], w_up[3], w_down[3],
        bias3, back[...], k_ref, v_ref,
    )


def lat_pack_kernel(recv_w, own_w, own_e, recv_e, south, north):
    for xk, ref in enumerate((recv_w, own_w, own_e, recv_e)):
        half = 2 * SLOT
        south[xk * half : (xk + 1) * half] = ref[:half]
        north[xk * half : (xk + 1) * half] = ref[half:]


def lev_pack_kernel(recv_s, south, north, recv_n, down, up):
    for yk, ref in enumerate((recv_s, south, north, recv_n)):
        for xk in range(4):
            at = (yk * 4 + xk) * SLOT
            down[at : at + SLOT] = ref[2 * xk * SLOT : (2 * xk + 1) * SLOT]
            up[at : at + SLOT] = ref[(2 * xk + 1) * SLOT : (2 * xk + 2) * SLOT]


def call(kernel, outs, *args, scratch=(), flops=0, limit=20):
    return pl.pallas_call(
        kernel,
        out_shape=outs,
        scratch_shapes=list(scratch),
        compiler_params=pltpu.CompilerParams(vmem_limit_bytes=limit << 20),
        cost_estimate=pl.CostEstimate(flops=flops, bytes_accessed=1 << 20, transcendentals=0),
    )(*args)


def shape(*dims, dtype=BF):
    return jax.ShapeDtypeStruct(dims, dtype)


def move(value, axis, steps):
    count = lax.axis_size(axis)
    return lax.ppermute(value, axis, [(i, (i + steps) % count) for i in range(count)])


def halo(west, east):
    recv_e = move(west, "lon", -1)
    recv_w = move(east, "lon", 1)
    south, north = call(
        lat_pack_kernel, [shape(8 * SLOT, D)] * 2, recv_w, west, east, recv_e, limit=4
    )
    recv_n = move(south, "lat", -1)
    recv_s = move(north, "lat", 1)
    down, up = call(
        lev_pack_kernel, [shape(16 * SLOT, D)] * 2, recv_s, south, north, recv_n, limit=4
    )
    recv_u = move(down, "lev", -1)
    recv_d = move(up, "lev", 1)
    return recv_d, down, up, recv_u


def per_device(fields, w_qkv, w_out, w_up, w_down, gains, bias_table, labels):
    level = lax.axis_index("lev")
    below = (level + 3) % 4
    to_oct_np, back_np = octant_maps()
    sel_reg, sel_shift, pad = selectors()
    to_oct = jnp.asarray(to_oct_np, BF)
    back = jnp.asarray(back_np, BF)
    sel_reg = jnp.asarray(sel_reg, BF)
    sel_shift = jnp.asarray(sel_shift, BF)
    pad = jnp.asarray(pad, F32)

    lab = labels[:, :, 0].astype(BF).reshape(4, 2 * WY)
    picked = []
    for window in (below, level):
        rows = lax.dynamic_index_in_dim(bias_table[:, :, 0], window, 1, keepdims=False)
        tags = lax.dynamic_index_in_dim(lab, window, 0, keepdims=False)
        tags = jnp.broadcast_to(tags, (BLOCKS, HEADS, 2 * WY))
        rows = jnp.concatenate([rows, tags], axis=-1)
        picked.append(jnp.pad(rows, ((0, 0), (0, 0), (0, WIDE - POS - 2 * WY))))
    own = picked[1]
    shifted_own = jnp.stack([jnp.stack([p[b] for p in picked]) for b in (1, 3)])
    shifted_south = move(shifted_own, "lat", 1)

    table_scratch = pltpu.VMEM((HEADS, WIDE), F32)

    def regular_bias(block):
        return call(
            functools.partial(bias_regular_kernel, block),
            shape(2, HEADS * T, 128, dtype=F32), own, sel_reg,
            scratch=[table_scratch, pltpu.VMEM((2, 2, 72, 128), F32)], flops=1 << 30,
        )

    def shifted_bias(at):
        return call(
            functools.partial(bias_shifted_kernel, at),
            shape(2, 8 * 144, 128, dtype=F32), shifted_own, shifted_south, sel_shift, pad,
            scratch=[table_scratch, pltpu.VMEM((2, 2, 96, 128), F32)], flops=1 << 30,
        )

    kv_scratch = [pltpu.VMEM((4, 4, 4, SLOT, D), BF)] * 2
    weights = (gains, w_qkv, w_out, w_up, w_down)
    stream, west, east = call(
        first_kernel, [shape(T, D), shape(4 * SLOT, D), shape(4 * SLOT, D)],
        fields.reshape(T, D), *weights, regular_bias(0), to_oct, flops=1 << 31,
    )
    slabs = halo(west, east)
    stream, west, east = call(
        middle_kernel, [shape(T, D), shape(4 * SLOT, D), shape(4 * SLOT, D)],
        stream, *slabs, *weights, shifted_bias(0), regular_bias(2), to_oct, back,
        scratch=kv_scratch, flops=1 << 31,
    )
    slabs = halo(west, east)
    stream = call(
        last_kernel, shape(T, D), stream, *slabs, *weights, shifted_bias(1), back,
        scratch=kv_scratch, flops=1 << 31,
    )
    return stream.reshape(2, 6, 12, D)


def solution(mesh):
    in_specs = (
        P("lev", "lat", "lon", None),
        P(),
        P(),
        P(),
        P(),
        P(),
        P(None, None, "lat", None, None),
        P(None, "lat", "lon"),
    )
    return jax.shard_map(
        per_device,
        mesh=mesh,
        in_specs=in_specs,
        out_specs=P("lev", "lat", "lon", None),
        check_vma=False,
    )
```

```python
import functools

import jax
import jax.numpy as jnp
import numpy as np
from jax import lax
from jax.experimental import pallas as pl
from jax.experimental.pallas import tpu as pltpu
from jax.sharding import PartitionSpec as P

HEADS = 6
HD = 32
WZ = 2
WY = 6
WX = 12
BLOCKS = 4
D = 192
FF = 768
T = WZ * WY * WX
OFFS = 2 * WX - 1
POS = 3312
SLOT = 24
PAIR = 2 * SLOT
NEG = -1e30
MASK_AT = 192
BF = jnp.bfloat16
F32 = jnp.float32


def octant_maps():
    to_oct = np.zeros((8 * SLOT, T), np.float32)
    back = np.zeros((T, 8 * SLOT), np.float32)
    for z in range(2):
        for y in range(6):
            for x in range(12):
                yh, yl, xh, xl = y // 3, y % 3, x // 6, x % 6
                tok = z * 72 + y * 12 + x
                slot = yl * 6 + xl
                to_oct[((xh * 2 + yh) * 2 + z) * SLOT + slot, tok] = 1.0
                back[tok, ((z * 2 + yh) * 2 + xh) * SLOT + slot] = 1.0
    return to_oct, back


def selectors():
    regular = np.zeros((2, 256, 256), np.float32)
    for zq in range(2):
        for yq in range(6):
            for xq in range(12):
                regular[zq, yq * OFFS + 11 - xq, zq * 72 + yq * 12 + xq] = 1.0
    shifted = np.zeros((2, 256, 256), np.float32)
    pad = np.full((1, 256), NEG, np.float32)
    for zk in range(2):
        for yk in range(2):
            for xk in range(2):
                for yl in range(3):
                    for xl in range(6):
                        lane = ((zk * 2 + yk) * 2 + xk) * SLOT + yl * 6 + xl
                        yq, xq = yk * 3 + yl, xk * 6 + xl
                        shifted[zk, yq * OFFS + 11 - xq, lane] = 1.0
                        shifted[zk, MASK_AT + yq, lane] = 1.0
                        pad[0, lane] = 0.0
    return regular.reshape(512, 256), shifted.reshape(512, 256), pad


def dot(a, b):
    return jnp.dot(a, b, preferred_element_type=F32)


def dot_t(a, b):
    return lax.dot_general(a, b, (((1,), (1,)), ((), ())), preferred_element_type=F32)


def layer_norm(values, gain):
    center = values - jnp.mean(values, axis=-1, keepdims=True)
    spread = jnp.mean(center * center, axis=-1, keepdims=True)
    return (center * lax.rsqrt(spread + 1e-05) * gain).astype(BF)


def head_mask(rows):
    lane_head = lax.broadcasted_iota(jnp.int32, (rows, D), 1) // HD
    return [lane_head == h for h in range(HEADS)]


def spread_heads(q, masks):
    return jnp.concatenate([jnp.where(m, q, 0.0) for m in masks], axis=0).astype(BF)


def softmax_mix(scores, keys_v, rows, masks):
    top = jnp.max(scores, axis=-1, keepdims=True)
    terms = jnp.exp(scores - top)
    total = 1.0 / jnp.sum(terms, axis=-1, keepdims=True)
    mixed = dot(terms.astype(BF), keys_v) * total
    out = mixed[0:rows]
    for h in range(1, HEADS):
        out = jnp.where(masks[h], mixed[h * rows : (h + 1) * rows], out)
    return out


def feed_forward(middle, gain, w_up, w_down):
    normed = layer_norm(middle.astype(F32), gain)
    up = dot(normed, w_up)
    hidden = (0.5 * up * (1.0 + lax.erf(up * np.float32(0.5**0.5)))).astype(BF)
    return (middle.astype(F32) + dot_t(hidden, w_down)).astype(BF)


def regular_block(stream, gain0, gain1, w_qkv, w_out, w_up, w_down, bias):
    normed = layer_norm(stream.astype(F32), gain0)
    qkv = dot(normed, w_qkv)
    q = qkv[:, :D].astype(BF).astype(F32) * np.float32(HD**-0.5)
    k = qkv[:, D : 2 * D].astype(BF)
    v = qkv[:, 2 * D :].astype(BF)
    masks = head_mask(T)
    bias = jnp.concatenate([bias[0], bias[1, :, : T - 128]], axis=1)
    scores = dot_t(spread_heads(q, masks), k) + bias
    heads_out = softmax_mix(scores, v, T, masks).astype(BF)
    attended = dot(heads_out, w_out).astype(BF)
    middle = (stream.astype(F32) + attended.astype(F32)).astype(BF)
    return feed_forward(middle, gain1, w_up, w_down)


def pack(tokens):
    half = tokens.shape[0] // 2
    tails = jnp.concatenate([tokens[:half, 128:], tokens[half:, 128:]], axis=1)
    return jnp.concatenate([tokens[:, :128], tails], axis=0).astype(BF)


def unpack(packed):
    values = packed.astype(F32)
    rows = values.shape[0] // 3 * 2
    tails = jnp.concatenate([values[rows:, :64], values[rows:, 64:]], axis=0)
    return jnp.concatenate([values[:rows], tails], axis=1)


def keys_values(tokens, w_qkv, k_ref, v_ref):
    kv = dot(tokens.astype(BF), w_qkv[:, D:])
    k_ref[...] = kv[:, :D].astype(BF).reshape(k_ref.shape)
    v_ref[...] = kv[:, D:].astype(BF).reshape(v_ref.shape)


def own_keys_kernel(block, down, up, w_qkv, q_ref, k_ref, v_ref):
    own = []
    for z, ref in enumerate((down, up)):
        tokens = unpack(ref[...])
        keys_values(tokens, w_qkv[block], k_ref.at[z], v_ref.at[z])
        for yh in range(2):
            row = (1 + yh) * 4 * SLOT + SLOT
            own.append(tokens[row : row + PAIR])
    q = dot(jnp.concatenate(own, axis=0).astype(BF), w_qkv[block, :, :D]).astype(BF)
    q_ref[...] = q.astype(F32) * np.float32(HD**-0.5)


def shifted_block(
    stream, below, above, q_ref, k_own, v_own, gain1, w_qkv, w_out, w_up, w_down, bias, back,
    k_ref, v_ref,
):
    for i, ref in enumerate((below, above)):
        keys_values(unpack(ref[...]), w_qkv, k_ref.at[i], v_ref.at[i])
    masks = head_mask(SLOT)
    outs = []
    for z in range(2):
        for yh in range(2):
            for xh in range(2):
                w = (z * 2 + yh) * 2 + xh
                sides = ((k_ref, v_ref, 0), (k_own, v_own, 0))
                if z:
                    sides = ((k_own, v_own, 1), (k_ref, v_ref, 1))
                ks, vs = [
                    jnp.concatenate(
                        [s[i][s[2], 2 * yh : 2 * yh + 2, xh].reshape(2 * PAIR, D) for s in sides],
                        axis=0,
                    )
                    for i in range(2)
                ]
                q = spread_heads(q_ref[w * SLOT : (w + 1) * SLOT], masks)
                rows = slice(w * 144, (w + 1) * 144)
                scores = dot_t(q, ks) + jnp.concatenate([bias[0, rows], bias[1, rows, :64]], 1)
                outs.append(softmax_mix(scores, vs, SLOT, masks))
    heads_out = jnp.concatenate(outs, axis=0).astype(BF)
    attended = dot(back, dot(heads_out, w_out).astype(BF))
    middle = (stream.astype(F32) + attended).astype(BF)
    return feed_forward(middle, gain1, w_up, w_down)


def pick_table(table_ref, block, window, table):
    rows = table_ref[block].astype(F32)
    at = lax.broadcasted_iota(jnp.int32, rows.shape, 1)
    table[...] = jnp.sum(jnp.where(at == window, rows, 0.0), axis=1)


def put(ref, rows, value):
    for k in range(2):
        ref[k, rows, :] = value[:, k * 128 : (k + 1) * 128]


def widened(table, start, extra):
    part = table[:, start : start + 6 * OFFS]
    wide = jnp.concatenate([part, jnp.zeros((HEADS, 256 - 6 * OFFS), F32)], axis=1)
    return wide if extra is None else wide + extra


def bias_rolls(parts, sel):
    lane = lax.broadcasted_iota(jnp.int32, parts[0].shape, 1)
    fixed = [jnp.where(lane >= MASK_AT, p, 0.0) for p in parts]
    moving = [jnp.where(lane < MASK_AT, p, 0.0) for p in parts]
    for xp in range(WX):
        rows = [
            (pltpu.roll(m, 256 - xp, 1) if xp else m) + f for m, f in zip(moving, fixed)
        ]
        yield xp, dot(jnp.concatenate(rows, axis=1).astype(BF), sel)


def bias_regular(table, sel, lhs, out_ref):
    for zp in range(2):
        for zq in range(2):
            for yp in range(6):
                start = ((zp * 2 + zq) * 6 + yp) * 6 * OFFS
                rows = pl.ds(zp * 6 + yp, HEADS, stride=12)
                put(lhs.at[zq], rows, widened(table, start, None))
    parts = [jnp.concatenate([lhs[k, 0], lhs[k, 1]], axis=1) for k in range(2)]
    for xp, rows in bias_rolls(parts, sel):
        put(out_ref, pl.ds(xp, 72, stride=WX), rows)


def tables_kernel(
    lev_ref, table_ref, label_ref, sel_ref, bias2, keep1, send1, keep3, send3, table, lhs, half
):
    pick_table(table_ref, 2, lev_ref[1], table)
    bias_regular(table, sel_ref[...], lhs, bias2)
    lane = lax.broadcasted_iota(jnp.int32, (8, 128), 1)
    level = lax.broadcasted_iota(jnp.int32, (8, 128), 0)
    first = MASK_AT - 128
    tags = jnp.zeros((8, 128), F32)
    for y in range(6):
        column = label_ref[y].astype(F32)[:, 0:1]
        tags = jnp.where(lane == first + y, column, tags)
    in_mask = (lane[0:1] >= first) & (lane[0:1] < first + 6)
    half[...] = jnp.zeros_like(half)
    for block, keep, send in ((1, keep1, send1), (3, keep3, send3)):
        for z in range(2):
            window = lev_ref[z]
            pick_table(table_ref, block, window, table)
            keys = [
                jnp.sum(jnp.where(level == window * 2 + zq, tags, 0.0), axis=0, keepdims=True)
                for zq in range(2)
            ]
            zp = 1 - z
            for yp in range(6):
                mine = jnp.sum(
                    jnp.where(lane[0:1] == first + yp, keys[zp], 0.0), axis=1, keepdims=True
                )
                for zq in range(2):
                    mask = jnp.where(in_mask & (keys[zq] != mine), NEG, 0.0)
                    mask = jnp.concatenate([jnp.zeros((1, 128), F32), mask], axis=1)
                    start = ((zp * 2 + zq) * 6 + yp) * 6 * OFFS
                    rows = pl.ds(z * 24 + yp % 3, HEADS, stride=4)
                    put(half.at[yp // 3, zq], rows, widened(table, start, mask))
        keep[...] = half[0].astype(BF)
        send[...] = half[1].astype(BF).reshape(192, 128)


def bias_shifted_kernel(keep, south, sel_ref, pad_ref, out_ref):
    moved = south[288:].reshape(2, 2, 48, 128)
    parts = []
    for zq in range(2):
        rows = [jnp.concatenate([src[zq, 0], src[zq, 1]], axis=1) for src in (moved, keep)]
        parts.append(jnp.concatenate(rows, axis=0).astype(F32))
    for xp, rows in bias_rolls(parts, sel_ref[...]):
        rows = rows + pad_ref[...]
        x = (xp + 6) % 12
        xh, xl = x // 6, x % 6
        for yh in range(2):
            for z in range(2):
                base = ((z * 2 + yh) * 2 + xh) * 144 + xl
                at = (yh * 2 + z) * 24
                put(out_ref, pl.ds(base, 24, stride=6), rows[at : at + 24])


def halves(stream, gain, to_oct, west, east):
    octs = dot(to_oct, layer_norm(stream.astype(F32), gain))
    west[...] = pack(octs[: 4 * SLOT])
    east[...] = pack(octs[4 * SLOT :])


def first_kernel(
    lev_ref, x, gains, w_qkv, w_out, w_up, w_down, table_ref, sel_ref, to_oct,
    stream_out, west, east, table, lhs, bias,
):
    pick_table(table_ref, 0, lev_ref[1], table)
    bias_regular(table, sel_ref[...], lhs, bias)
    stream = regular_block(
        x[...], gains[0, 0:1], gains[0, 1:2], w_qkv[0], w_out[0], w_up[0], w_down[0], bias
    )
    stream_out[...] = stream
    halves(stream, gains[1, 0:1], to_oct[...], west, east)


def middle_kernel(
    stream_in, below, above, q, k_own, v_own, gains, w_qkv, w_out, w_up, w_down, bias1, bias2,
    to_oct, back, stream_out, west, east, k_ref, v_ref,
):
    stream = shifted_block(
        stream_in[...], below, above, q, k_own, v_own, gains[1, 1:2], w_qkv[1], w_out[1], w_up[1],
        w_down[1], bias1, back[...], k_ref, v_ref,
    )
    stream = regular_block(
        stream, gains[2, 0:1], gains[2, 1:2], w_qkv[2], w_out[2], w_up[2], w_down[2], bias2
    )
    stream_out[...] = stream
    halves(stream, gains[3, 0:1], to_oct[...], west, east)


def last_kernel(
    stream_in, below, above, q, k_own, v_own, gains, w_qkv, w_out, w_up, w_down, bias3, back, out,
    k_ref, v_ref,
):
    out[...] = shifted_block(
        stream_in[...], below, above, q, k_own, v_own, gains[3, 1:2], w_qkv[3], w_out[3], w_up[3],
        w_down[3], bias3, back[...], k_ref, v_ref,
    )


def lat_pack_kernel(recv_w, own_w, own_e, recv_e, table_rows, south, north):
    parts = [unpack(ref[...]) for ref in (recv_w, own_w, own_e, recv_e)]
    for yh, ref in ((0, south), (1, north)):
        rows = [
            part[(yh * 2 + z) * SLOT : (yh * 2 + z + 1) * SLOT] for z in range(2) for part in parts
        ]
        ref[:288] = pack(jnp.concatenate(rows, axis=0))
    north[288:] = table_rows[...]


def lev_pack_kernel(recv_s, south, north, recv_n, down, up):
    parts = [unpack(ref[:288]) for ref in (recv_s, south, north, recv_n)]
    for z, ref in ((0, down), (1, up)):
        rows = [part[z * 4 * SLOT : (z + 1) * 4 * SLOT] for part in parts]
        ref[...] = pack(jnp.concatenate(rows, axis=0))


def call(kernel, outs, *args, scratch=(), flops=0, limit=20, scalars=0):
    specs = [pl.BlockSpec(memory_space=pltpu.SMEM)] * scalars
    specs += [pl.BlockSpec(memory_space=pltpu.VMEM)] * (len(args) - scalars)
    return pl.pallas_call(
        kernel,
        out_shape=outs,
        in_specs=specs,
        scratch_shapes=list(scratch),
        compiler_params=pltpu.CompilerParams(vmem_limit_bytes=limit << 20),
        cost_estimate=pl.CostEstimate(flops=flops, bytes_accessed=1 << 20, transcendentals=0),
    )(*args)


def shape(*dims, dtype=BF):
    return jax.ShapeDtypeStruct(dims, dtype)


def move(value, axis, steps):
    count = lax.axis_size(axis)
    return lax.ppermute(value, axis, [(i, (i + steps) % count) for i in range(count)])


def halo(block, west, east, keep, send, w_qkv, sel_shift, pad):
    recv_e = move(west, "lon", -1)
    recv_w = move(east, "lon", 1)
    south, north = call(
        lat_pack_kernel, [shape(288, 128), shape(480, 128)], recv_w, west, east, recv_e, send,
        limit=4,
    )
    recv_n = move(south, "lat", -1)
    recv_s = move(north, "lat", 1)
    down, up = call(
        lev_pack_kernel, [shape(576, 128)] * 2, recv_s, south, north, recv_n, limit=4
    )
    above = move(down, "lev", -1)
    below = move(up, "lev", 1)
    q, k, v = call(
        functools.partial(own_keys_kernel, block),
        [shape(8 * SLOT, D, dtype=F32), shape(2, 4, 2, PAIR, D), shape(2, 4, 2, PAIR, D)],
        down, up, w_qkv, flops=1 << 30, limit=8,
    )
    bias = call(
        bias_shifted_kernel, shape(2, 8 * 144, 128, dtype=F32), keep, recv_s, sel_shift, pad,
        flops=1 << 30, limit=8,
    )
    return below, above, q, k, v, bias


def per_device(fields, w_qkv, w_out, w_up, w_down, gains, bias_table, labels):
    level = lax.axis_index("lev")
    levels = jnp.stack([(level + 3) % 4, level]).astype(jnp.int32)
    to_oct, back = [jnp.asarray(m, BF) for m in octant_maps()]
    sel_reg, sel_shift, pad = selectors()
    sel_reg, sel_shift = jnp.asarray(sel_reg, BF), jnp.asarray(sel_shift, BF)
    pad = jnp.asarray(pad, F32)
    tables = bias_table[:, :, 0].transpose(0, 2, 1, 3)
    tags = labels.transpose(1, 0, 2)
    weights = (gains, w_qkv, w_out, w_up, w_down.transpose(0, 2, 1))

    bias_shape = (2, HEADS * T, 128)
    table_scratch = [pltpu.VMEM((HEADS, POS), F32), pltpu.VMEM((2, 2, 72, 128), F32)]
    kv_scratch = [pltpu.VMEM((2, 4, 2, PAIR, D), BF)] * 2
    streams = [shape(T, D), shape(144, 128), shape(144, 128)]
    stream, west, east = call(
        first_kernel, streams, levels, fields.reshape(T, D), *weights, tables, sel_reg, to_oct,
        scratch=[*table_scratch, pltpu.VMEM(bias_shape, F32)], flops=1 << 31, scalars=1,
    )
    rows = [shape(2, 2, 48, 128), shape(192, 128)]
    bias2, keep1, send1, keep3, send3 = call(
        tables_kernel, [shape(*bias_shape, dtype=F32), *rows, *rows], levels, tables, tags, sel_reg,
        scratch=[*table_scratch, pltpu.VMEM((2, 2, 2, 48, 128), F32)], flops=1 << 31, scalars=1,
    )
    *ready, bias1 = halo(1, west, east, keep1, send1, w_qkv, sel_shift, pad)
    stream, west, east = call(
        middle_kernel, streams, stream, *ready, *weights, bias1, bias2, to_oct, back,
        scratch=kv_scratch, flops=1 << 31,
    )
    *ready, bias3 = halo(3, west, east, keep3, send3, w_qkv, sel_shift, pad)
    stream = call(
        last_kernel, shape(T, D), stream, *ready, *weights, bias3, back,
        scratch=kv_scratch, flops=1 << 31,
    )
    return stream.reshape(2, 6, 12, D)


def solution(mesh):
    in_specs = (
        P("lev", "lat", "lon", None),
        P(),
        P(),
        P(),
        P(),
        P(),
        P(None, None, "lat", None, None),
        P(None, "lat", "lon"),
    )
    return jax.shard_map(
        per_device,
        mesh=mesh,
        in_specs=in_specs,
        out_specs=P("lev", "lat", "lon", None),
        check_vma=False,
    )
```

```python
import functools

import jax
import jax.numpy as jnp
import numpy as np
from jax import lax
from jax.experimental import pallas as pl
from jax.experimental.pallas import tpu as pltpu
from jax.sharding import PartitionSpec as P

HEADS = 6
HD = 32
WZ = 2
WY = 6
WX = 12
BLOCKS = 4
D = 192
FF = 768
T = WZ * WY * WX
OFFS = 2 * WX - 1
POS = 3312
SLOT = 24
PAIR = 2 * SLOT
FIRST_LIMIT = 62.0
NEG = -1e30
MASK_AT = 192
BF = jnp.bfloat16
F32 = jnp.float32


def octant_maps():
    to_oct = np.zeros((8 * SLOT, T), np.float32)
    back = np.zeros((T, 8 * SLOT), np.float32)
    for z in range(2):
        for y in range(6):
            for x in range(12):
                yh, yl, xh, xl = y // 3, y % 3, x // 6, x % 6
                tok = (y * 12 + x) * 2 + z
                slot = yl * 6 + xl
                to_oct[((xh * 2 + yh) * 2 + z) * SLOT + slot, tok] = 1.0
                back[tok, ((z * 2 + yh) * 2 + xh) * SLOT + slot] = 1.0
    return to_oct, back


def selectors():
    regular = np.zeros((2, 256, 256), np.float32)
    for zq in range(2):
        for yq in range(6):
            for xq in range(12):
                regular[zq, yq * OFFS + 11 - xq, (yq * 12 + xq) * 2 + zq] = 1.0
    shifted = np.zeros((2, 256, 256), np.float32)
    pad = np.full((1, 256), NEG, np.float32)
    for zk in range(2):
        for yk in range(2):
            for xk in range(2):
                for yl in range(3):
                    for xl in range(6):
                        lane = ((zk * 2 + yk) * 2 + xk) * SLOT + yl * 6 + xl
                        yq, xq = yk * 3 + yl, xk * 6 + xl
                        shifted[zk, yq * OFFS + 11 - xq, lane] = 1.0
                        shifted[zk, MASK_AT + yq, lane] = 1.0
                        pad[0, lane] = 0.0
    return regular.reshape(512, 256), shifted.reshape(512, 256), pad


def dot(a, b):
    return jnp.dot(a, b, preferred_element_type=F32)


def dot_t(a, b):
    return lax.dot_general(a, b, (((1,), (1,)), ((), ())), preferred_element_type=F32)


def layer_norm(values, gain):
    center = values - jnp.mean(values, axis=-1, keepdims=True)
    spread = jnp.mean(center * center, axis=-1, keepdims=True)
    return (center * lax.rsqrt(spread + 1e-05) * gain).astype(BF)


def head_mask(rows):
    lane_head = lax.broadcasted_iota(jnp.int32, (rows, D), 1) // HD
    return [lane_head == h for h in range(HEADS)]


def spread_heads(q, masks):
    return jnp.concatenate([jnp.where(m, q, 0.0) for m in masks], axis=0).astype(BF)


def softmax_mix(scores, keys_v, rows, masks):
    top = jnp.max(scores, axis=-1, keepdims=True)
    terms = jnp.exp(scores - top)
    total = 1.0 / jnp.sum(terms, axis=-1, keepdims=True)
    mixed = dot(terms.astype(BF), keys_v) * total
    out = mixed[0:rows]
    for h in range(1, HEADS):
        out = jnp.where(masks[h], mixed[h * rows : (h + 1) * rows], out)
    return out


def feed_forward(middle, gain, w_up, w_down):
    normed = layer_norm(middle.astype(F32), gain)
    up = dot(normed, w_up)
    hidden = (0.5 * up * (1.0 + lax.erf(up * np.float32(0.5**0.5)))).astype(BF)
    return (middle.astype(F32) + dot_t(hidden, w_down)).astype(BF)


def regular_block(stream, gain0, gain1, w_qkv, w_out, w_up, w_down, bias):
    normed = layer_norm(stream.astype(F32), gain0)
    qkv = dot(normed, w_qkv)
    q = qkv[:, :D].astype(BF).astype(F32) * np.float32(HD**-0.5)
    k = qkv[:, D : 2 * D].astype(BF)
    v = qkv[:, 2 * D :].astype(BF)
    masks = head_mask(T)
    bias = jnp.concatenate([bias[0], bias[1, :, : T - 128]], axis=1)
    scores = dot_t(spread_heads(q, masks), k) + bias
    heads_out = softmax_mix(scores, v, T, masks).astype(BF)
    attended = dot(heads_out, w_out).astype(BF)
    middle = (stream.astype(F32) + attended.astype(F32)).astype(BF)
    return feed_forward(middle, gain1, w_up, w_down)


def pack(tokens):
    half = tokens.shape[0] // 2
    tails = jnp.concatenate([tokens[:half, 128:], tokens[half:, 128:]], axis=1)
    return jnp.concatenate([tokens[:, :128], tails], axis=0).astype(BF)


def unpack(packed):
    values = packed.astype(F32)
    rows = values.shape[0] // 3 * 2
    tails = jnp.concatenate([values[rows:, :64], values[rows:, 64:]], axis=0)
    return jnp.concatenate([values[:rows], tails], axis=1)


def keys_values(tokens, w_qkv, k_ref, v_ref):
    kv = dot(tokens.astype(BF), w_qkv[:, D:])
    k_ref[...] = kv[:, :D].astype(BF).reshape(k_ref.shape)
    v_ref[...] = kv[:, D:].astype(BF).reshape(v_ref.shape)


def own_keys_kernel(block, down, up, w_qkv, q_ref, k_ref, v_ref):
    own = []
    for z, ref in enumerate((down, up)):
        tokens = unpack(ref[...])
        keys_values(tokens, w_qkv[block], k_ref.at[z], v_ref.at[z])
        for yh in range(2):
            row = (1 + yh) * 4 * SLOT + SLOT
            own.append(tokens[row : row + PAIR])
    q = dot(jnp.concatenate(own, axis=0).astype(BF), w_qkv[block, :, :D]).astype(BF)
    q_ref[...] = q.astype(F32) * np.float32(HD**-0.5)


def shifted_block(
    stream, below, above, q_ref, k_own, v_own, gain1, w_qkv, w_out, w_up, w_down, bias, back,
    k_ref, v_ref,
):
    for i, ref in enumerate((below, above)):
        keys_values(unpack(ref[...]), w_qkv, k_ref.at[i], v_ref.at[i])
    masks = head_mask(SLOT)
    outs = []
    for z in range(2):
        for yh in range(2):
            for xh in range(2):
                w = (z * 2 + yh) * 2 + xh
                sides = ((k_ref, v_ref, 0), (k_own, v_own, 0))
                if z:
                    sides = ((k_own, v_own, 1), (k_ref, v_ref, 1))
                ks, vs = [
                    jnp.concatenate(
                        [s[i][s[2], 2 * yh : 2 * yh + 2, xh].reshape(2 * PAIR, D) for s in sides],
                        axis=0,
                    )
                    for i in range(2)
                ]
                q = spread_heads(q_ref[w * SLOT : (w + 1) * SLOT], masks)
                rows = slice(w * 144, (w + 1) * 144)
                scores = dot_t(q, ks) + jnp.concatenate([bias[0, rows], bias[1, rows, :64]], 1)
                outs.append(softmax_mix(scores, vs, SLOT, masks))
    heads_out = jnp.concatenate(outs, axis=0).astype(BF)
    attended = dot(back, dot(heads_out, w_out).astype(BF))
    middle = (stream.astype(F32) + attended).astype(BF)
    return feed_forward(middle, gain1, w_up, w_down)


def pick_table(table_ref, block, window, table):
    rows = table_ref[block].astype(F32)
    at = lax.broadcasted_iota(jnp.int32, rows.shape, 1)
    table[...] = jnp.sum(jnp.where(at == window, rows, 0.0), axis=1)


def put(ref, rows, value):
    for k in range(2):
        ref[k, rows, :] = value[:, k * 128 : (k + 1) * 128]


def widened(table, start, extra):
    part = table[:, start : start + 6 * OFFS]
    wide = jnp.concatenate([part, jnp.zeros((HEADS, 256 - 6 * OFFS), F32)], axis=1)
    return wide if extra is None else wide + extra


def bias_rolls(parts, sel):
    lane = lax.broadcasted_iota(jnp.int32, parts[0].shape, 1)
    fixed = [jnp.where(lane >= MASK_AT, p, 0.0) for p in parts]
    moving = [jnp.where(lane < MASK_AT, p, 0.0) for p in parts]
    for xp in range(WX):
        rows = [
            (pltpu.roll(m, 256 - xp, 1) if xp else m) + f for m, f in zip(moving, fixed)
        ]
        yield xp, dot(jnp.concatenate(rows, axis=1).astype(BF), sel)


def bias_regular(table, sel, lhs, out_ref):
    for zp in range(2):
        for zq in range(2):
            for yp in range(6):
                start = ((zp * 2 + zq) * 6 + yp) * 6 * OFFS
                rows = pl.ds(zp * 40 + yp, HEADS, stride=6)
                put(lhs.at[zq], rows, widened(table, start, None))
    parts = [jnp.concatenate([lhs[k, 0], lhs[k, 1]], axis=1) for k in range(2)]
    for xp, rows in bias_rolls(parts, sel):
        for zp in range(2):
            put(out_ref, pl.ds(2 * xp + zp, 36, stride=24), rows[zp * 40 : zp * 40 + 36])


def tables_kernel(
    lev_ref, table_ref, label_ref, sel_ref, bias2, keep1, send1, keep3, send3, table, lhs, half
):
    pick_table(table_ref, 2, lev_ref[1], table)
    lhs[...] = jnp.zeros_like(lhs)
    bias_regular(table, sel_ref[...], lhs, bias2)
    lane = lax.broadcasted_iota(jnp.int32, (8, 128), 1)
    level = lax.broadcasted_iota(jnp.int32, (8, 128), 0)
    first = MASK_AT - 128
    tags = jnp.zeros((8, 128), F32)
    for y in range(6):
        column = label_ref[y].astype(F32)[:, 0:1]
        tags = jnp.where(lane == first + y, column, tags)
    in_mask = (lane[0:1] >= first) & (lane[0:1] < first + 6)
    half[...] = jnp.zeros_like(half)
    for block, keep, send in ((1, keep1, send1), (3, keep3, send3)):
        for z in range(2):
            window = lev_ref[z]
            pick_table(table_ref, block, window, table)
            keys = [
                jnp.sum(jnp.where(level == window * 2 + zq, tags, 0.0), axis=0, keepdims=True)
                for zq in range(2)
            ]
            zp = 1 - z
            for yp in range(6):
                mine = jnp.sum(
                    jnp.where(lane[0:1] == first + yp, keys[zp], 0.0), axis=1, keepdims=True
                )
                for zq in range(2):
                    mask = jnp.where(in_mask & (keys[zq] != mine), NEG, 0.0)
                    mask = jnp.concatenate([jnp.zeros((1, 128), F32), mask], axis=1)
                    start = ((zp * 2 + zq) * 6 + yp) * 6 * OFFS
                    rows = pl.ds(z * 24 + yp % 3, HEADS, stride=4)
                    put(half.at[yp // 3, zq], rows, widened(table, start, mask))
        keep[...] = half[0].astype(BF)
        send[...] = half[1].astype(BF).reshape(192, 128)


def bias_shifted_kernel(keep, south, sel_ref, pad_ref, out_ref):
    moved = south[288:].reshape(2, 2, 48, 128)
    parts = []
    for zq in range(2):
        rows = [jnp.concatenate([src[zq, 0], src[zq, 1]], axis=1) for src in (moved, keep)]
        parts.append(jnp.concatenate(rows, axis=0).astype(F32))
    for xp, rows in bias_rolls(parts, sel_ref[...]):
        rows = rows + pad_ref[...]
        x = (xp + 6) % 12
        xh, xl = x // 6, x % 6
        for yh in range(2):
            for z in range(2):
                base = ((z * 2 + yh) * 2 + xh) * 144 + xl
                at = (yh * 2 + z) * 24
                put(out_ref, pl.ds(base, 24, stride=6), rows[at : at + 24])


def halves(stream, gain, to_oct, west, east):
    octs = dot(to_oct, layer_norm(stream.astype(F32), gain))
    west[...] = pack(octs[: 4 * SLOT])
    east[...] = pack(octs[4 * SLOT :])


def first_kernel(
    lev_ref, x_hbm, gains_hbm, w_qkv_hbm, w_out_hbm, w_up_hbm, w_down_hbm, table_hbm, sel_hbm,
    oct_hbm, stream_out, west, east, table, lhs, bias, x, gains, w_qkv, w_out, w_up, w_down,
    rows, sel, to_oct, sems,
):
    pairs = (
        (table_hbm.at[pl.ds(0, 1)], rows), (sel_hbm, sel), (x_hbm, x), (gains_hbm, gains),
        (w_qkv_hbm.at[0], w_qkv), (w_out_hbm.at[0], w_out), (w_up_hbm.at[0], w_up),
        (w_down_hbm.at[0], w_down), (oct_hbm, to_oct),
    )
    copies = [pltpu.make_async_copy(a, b, sems.at[i]) for i, (a, b) in enumerate(pairs)]
    for copy in copies:
        copy.start()
    copies[0].wait()
    pick_table(rows, 0, lev_ref[1], table)
    lhs[...] = jnp.zeros_like(lhs)
    copies[1].wait()
    bias_regular(table, sel[...], lhs, bias)
    for copy in copies[2:]:
        copy.wait()
    stream = regular_block(
        x[...].astype(F32).reshape(T, D).astype(BF), gains[0, 0:1], gains[0, 1:2], w_qkv[...],
        w_out[...], w_up[...], w_down[...], bias,
    )
    stream_out[...] = stream
    halves(stream, gains[1, 0:1], to_oct[...], west, east)


def middle_kernel(
    stream_in, below, above, q, k_own, v_own, gains, w_qkv, w_out, w_up, w_down, bias1, bias2,
    to_oct, back, stream_out, west, east, k_ref, v_ref,
):
    stream = shifted_block(
        stream_in[...], below, above, q, k_own, v_own, gains[1, 1:2], w_qkv[1], w_out[1], w_up[1],
        w_down[1], bias1, back[...], k_ref, v_ref,
    )
    stream = regular_block(
        stream, gains[2, 0:1], gains[2, 1:2], w_qkv[2], w_out[2], w_up[2], w_down[2], bias2
    )
    stream_out[...] = stream
    halves(stream, gains[3, 0:1], to_oct[...], west, east)


def last_kernel(
    stream_in, below, above, q, k_own, v_own, gains, w_qkv, w_out, w_up, w_down, bias3, back, out,
    k_ref, v_ref,
):
    stream = shifted_block(
        stream_in[...], below, above, q, k_own, v_own, gains[3, 1:2], w_qkv[3], w_out[3], w_up[3],
        w_down[3], bias3, back[...], k_ref, v_ref,
    )
    out[...] = stream.astype(F32).reshape(T // 2, 2, D).astype(BF)


def lat_pack_kernel(recv_w, own_w, own_e, recv_e, table_rows, south, north):
    parts = [unpack(ref[...]) for ref in (recv_w, own_w, own_e, recv_e)]
    for yh, ref in ((0, south), (1, north)):
        rows = [
            part[(yh * 2 + z) * SLOT : (yh * 2 + z + 1) * SLOT] for z in range(2) for part in parts
        ]
        ref[:288] = pack(jnp.concatenate(rows, axis=0))
    north[288:] = table_rows[...]


def lev_pack_kernel(recv_s, south, north, recv_n, down, up):
    parts = [unpack(ref[:288]) for ref in (recv_s, south, north, recv_n)]
    for z, ref in ((0, down), (1, up)):
        rows = [part[z * 4 * SLOT : (z + 1) * 4 * SLOT] for part in parts]
        ref[...] = pack(jnp.concatenate(rows, axis=0))


def call(kernel, outs, *args, scratch=(), flops=0, limit=20, scalars=0, place=pltpu.VMEM):
    specs = [pl.BlockSpec(memory_space=pltpu.SMEM)] * scalars
    specs += [pl.BlockSpec(memory_space=place)] * (len(args) - scalars)
    return pl.pallas_call(
        kernel,
        out_shape=outs,
        in_specs=specs,
        scratch_shapes=list(scratch),
        compiler_params=pltpu.CompilerParams(vmem_limit_bytes=int(limit * (1 << 20))),
        cost_estimate=pl.CostEstimate(flops=flops, bytes_accessed=1 << 20, transcendentals=0),
    )(*args)


def shape(*dims, dtype=BF):
    return jax.ShapeDtypeStruct(dims, dtype)


def move(value, axis, steps):
    count = lax.axis_size(axis)
    return lax.ppermute(value, axis, [(i, (i + steps) % count) for i in range(count)])


def halo(block, west, east, keep, send, w_qkv, sel_shift, pad):
    recv_e = move(west, "lon", -1)
    recv_w = move(east, "lon", 1)
    south, north = call(
        lat_pack_kernel, [shape(288, 128), shape(480, 128)], recv_w, west, east, recv_e, send,
        limit=4,
    )
    recv_n = move(south, "lat", -1)
    recv_s = move(north, "lat", 1)
    down, up = call(
        lev_pack_kernel, [shape(576, 128)] * 2, recv_s, south, north, recv_n, limit=4
    )
    above = move(down, "lev", -1)
    below = move(up, "lev", 1)
    q, k, v = call(
        functools.partial(own_keys_kernel, block),
        [shape(8 * SLOT, D, dtype=F32), shape(2, 4, 2, PAIR, D), shape(2, 4, 2, PAIR, D)],
        down, up, w_qkv, flops=1 << 30, limit=8,
    )
    bias = call(
        bias_shifted_kernel, shape(2, 8 * 144, 128, dtype=F32), keep, recv_s, sel_shift, pad,
        flops=1 << 30, limit=8,
    )
    return below, above, q, k, v, bias


def per_device(fields, w_qkv, w_out, w_up, w_down, gains, bias_table, labels):
    level = lax.axis_index("lev")
    levels = jnp.stack([(level + 3) % 4, level]).astype(jnp.int32)
    to_oct, back = [jnp.asarray(m, BF) for m in octant_maps()]
    sel_reg, sel_shift, pad = selectors()
    sel_reg, sel_shift = jnp.asarray(sel_reg, BF), jnp.asarray(sel_shift, BF)
    pad = jnp.asarray(pad, F32)
    tables = bias_table[:, :, 0].transpose(0, 2, 1, 3)
    tags = labels.transpose(1, 0, 2)
    weights = (gains, w_qkv, w_out, w_up, w_down.transpose(0, 2, 1))

    bias_shape = (2, HEADS * T, 128)
    table_scratch = [pltpu.VMEM((HEADS, POS), F32), pltpu.VMEM((2, 2, 80, 128), F32)]
    kv_scratch = [pltpu.VMEM((2, 4, 2, PAIR, D), BF)] * 2
    streams = [shape(T, D), shape(144, 128), shape(144, 128)]
    stream, west, east = call(
        first_kernel, streams, levels, fields.transpose(1, 2, 0, 3).reshape(T // 2, 2, D), *weights,
        tables, sel_reg, to_oct,
        scratch=[
            *table_scratch, pltpu.VMEM(bias_shape, F32), pltpu.VMEM((T // 2, 2, D), BF),
            pltpu.VMEM((BLOCKS, 2, D), F32), pltpu.VMEM((D, 3 * D), BF), pltpu.VMEM((D, D), BF),
            pltpu.VMEM((D, FF), BF), pltpu.VMEM((D, FF), BF), pltpu.VMEM((1, HEADS, 4, POS), BF),
            pltpu.VMEM((512, 256), BF), pltpu.VMEM((8 * SLOT, T), BF), pltpu.SemaphoreType.DMA((9,)),
        ],
        flops=1 << 31, scalars=1, place=pltpu.HBM, limit=FIRST_LIMIT,
    )
    rows = [shape(2, 2, 48, 128), shape(192, 128)]
    bias2, keep1, send1, keep3, send3 = call(
        tables_kernel, [shape(*bias_shape, dtype=F32), *rows, *rows], levels, tables, tags, sel_reg,
        scratch=[*table_scratch, pltpu.VMEM((2, 2, 2, 48, 128), F32)], flops=1 << 31, scalars=1,
    )
    *ready, bias1 = halo(1, west, east, keep1, send1, w_qkv, sel_shift, pad)
    stream, west, east = call(
        middle_kernel, streams, stream, *ready, *weights, bias1, bias2, to_oct, back,
        scratch=kv_scratch, flops=1 << 31,
    )
    *ready, bias3 = halo(3, west, east, keep3, send3, w_qkv, sel_shift, pad)
    stream = call(
        last_kernel, shape(T // 2, 2, D), stream, *ready, *weights, bias3, back,
        scratch=kv_scratch, flops=1 << 31,
    )
    return stream.reshape(6, 12, 2, D).transpose(2, 0, 1, 3)


def solution(mesh):
    in_specs = (
        P("lev", "lat", "lon", None),
        P(),
        P(),
        P(),
        P(),
        P(),
        P(None, None, "lat", None, None),
        P(None, "lat", "lon"),
    )
    return jax.shard_map(
        per_device,
        mesh=mesh,
        in_specs=in_specs,
        out_specs=P("lev", "lat", "lon", None),
        check_vma=False,
    )
```

```python
import functools

import jax
import jax.numpy as jnp
import numpy as np
from jax import lax
from jax.experimental import pallas as pl
from jax.experimental.pallas import tpu as pltpu
from jax.sharding import PartitionSpec as P

HEADS = 6
HD = 32
WZ = 2
WY = 6
WX = 12
BLOCKS = 4
D = 192
FF = 768
T = WZ * WY * WX
OFFS = 2 * WX - 1
POS = 3312
SLOT = 24
PAIR = 2 * SLOT
FIRST_LIMIT = 62.0
NEG = -1e30
MASK_AT = 192
BF = jnp.bfloat16
F32 = jnp.float32


def octant_maps():
    to_oct = np.zeros((8 * SLOT, T), np.float32)
    back = np.zeros((T, 8 * SLOT), np.float32)
    for z in range(2):
        for y in range(6):
            for x in range(12):
                yh, yl, xh, xl = y // 3, y % 3, x // 6, x % 6
                tok = (y * 12 + x) * 2 + z
                slot = yl * 6 + xl
                to_oct[((xh * 2 + yh) * 2 + z) * SLOT + slot, tok] = 1.0
                back[tok, ((z * 2 + yh) * 2 + xh) * SLOT + slot] = 1.0
    return to_oct, back


def selectors():
    regular = np.zeros((2, 256, 256), np.float32)
    for zq in range(2):
        for yq in range(6):
            for xq in range(12):
                regular[zq, yq * OFFS + 11 - xq, (yq * 12 + xq) * 2 + zq] = 1.0
    shifted = np.zeros((2, 256, 256), np.float32)
    pad = np.full((1, 256), NEG, np.float32)
    for zk in range(2):
        for yk in range(2):
            for xk in range(2):
                for yl in range(3):
                    for xl in range(6):
                        lane = ((zk * 2 + yk) * 2 + xk) * SLOT + yl * 6 + xl
                        yq, xq = yk * 3 + yl, xk * 6 + xl
                        shifted[zk, yq * OFFS + 11 - xq, lane] = 1.0
                        shifted[zk, MASK_AT + yq, lane] = 1.0
                        pad[0, lane] = 0.0
    return regular.reshape(512, 256), shifted.reshape(512, 256), pad


def dot(a, b):
    return jnp.dot(a, b, preferred_element_type=F32)


def dot_t(a, b):
    return lax.dot_general(a, b, (((1,), (1,)), ((), ())), preferred_element_type=F32)


def layer_norm(values, gain):
    center = values - jnp.mean(values, axis=-1, keepdims=True)
    spread = jnp.mean(center * center, axis=-1, keepdims=True)
    return (center * lax.rsqrt(spread + 1e-05) * gain).astype(BF)


def head_mask(rows):
    lane_head = lax.broadcasted_iota(jnp.int32, (rows, D), 1) // HD
    return [lane_head == h for h in range(HEADS)]


def spread_heads(q, masks):
    return jnp.concatenate([jnp.where(m, q, 0.0) for m in masks], axis=0).astype(BF)


def softmax_mix(scores, keys_v, rows, masks):
    top = jnp.max(scores, axis=-1, keepdims=True)
    terms = jnp.exp(scores - top)
    total = 1.0 / jnp.sum(terms, axis=-1, keepdims=True)
    mixed = dot(terms.astype(BF), keys_v) * total
    out = mixed[0:rows]
    for h in range(1, HEADS):
        out = jnp.where(masks[h], mixed[h * rows : (h + 1) * rows], out)
    return out


def feed_forward(middle, gain, w_up, w_down):
    normed = layer_norm(middle.astype(F32), gain)
    up = dot(normed, w_up)
    hidden = (0.5 * up * (1.0 + lax.erf(up * np.float32(0.5**0.5)))).astype(BF)
    return (middle.astype(F32) + dot_t(hidden, w_down)).astype(BF)


def regular_block(stream, gain0, gain1, w_qkv, w_out, w_up, w_down, bias):
    normed = layer_norm(stream.astype(F32), gain0)
    qkv = dot(normed, w_qkv)
    q = qkv[:, :D].astype(BF).astype(F32) * np.float32(HD**-0.5)
    k = qkv[:, D : 2 * D].astype(BF)
    v = qkv[:, 2 * D :].astype(BF)
    masks = head_mask(T)
    bias = jnp.concatenate([bias[0], bias[1, :, : T - 128]], axis=1)
    scores = dot_t(spread_heads(q, masks), k) + bias
    heads_out = softmax_mix(scores, v, T, masks).astype(BF)
    attended = dot(heads_out, w_out).astype(BF)
    middle = (stream.astype(F32) + attended.astype(F32)).astype(BF)
    return feed_forward(middle, gain1, w_up, w_down)


def pack(tokens):
    half = tokens.shape[0] // 2
    tails = jnp.concatenate([tokens[:half, 128:], tokens[half:, 128:]], axis=1)
    return jnp.concatenate([tokens[:, :128], tails], axis=0).astype(BF)


def unpack(packed):
    values = packed.astype(F32)
    rows = values.shape[0] // 3 * 2
    tails = jnp.concatenate([values[rows:, :64], values[rows:, 64:]], axis=0)
    return jnp.concatenate([values[:rows], tails], axis=1)


def keys_values(tokens, w_qkv, k_ref, v_ref):
    kv = dot(tokens.astype(BF), w_qkv[:, D:])
    k_ref[...] = kv[:, :D].astype(BF).reshape(k_ref.shape)
    v_ref[...] = kv[:, D:].astype(BF).reshape(v_ref.shape)


def own_keys_kernel(block, down, up, w_qkv, q_ref, k_ref, v_ref):
    own = []
    for z, ref in enumerate((down, up)):
        tokens = unpack(ref[...])
        keys_values(tokens, w_qkv[block], k_ref.at[z], v_ref.at[z])
        for yh in range(2):
            row = (1 + yh) * 4 * SLOT + SLOT
            own.append(tokens[row : row + PAIR])
    q = dot(jnp.concatenate(own, axis=0).astype(BF), w_qkv[block, :, :D]).astype(BF)
    q_ref[...] = q.astype(F32) * np.float32(HD**-0.5)


def shifted_block(
    stream, below, above, q_ref, k_own, v_own, gain1, w_qkv, w_out, w_up, w_down, bias, back,
    k_ref, v_ref,
):
    for i, ref in enumerate((below, above)):
        keys_values(unpack(ref[...]), w_qkv, k_ref.at[i], v_ref.at[i])
    masks = head_mask(SLOT)
    outs = []
    for z in range(2):
        for yh in range(2):
            for xh in range(2):
                w = (z * 2 + yh) * 2 + xh
                sides = ((k_ref, v_ref, 0), (k_own, v_own, 0))
                if z:
                    sides = ((k_own, v_own, 1), (k_ref, v_ref, 1))
                ks, vs = [
                    jnp.concatenate(
                        [s[i][s[2], 2 * yh : 2 * yh + 2, xh].reshape(2 * PAIR, D) for s in sides],
                        axis=0,
                    )
                    for i in range(2)
                ]
                q = spread_heads(q_ref[w * SLOT : (w + 1) * SLOT], masks)
                rows = slice(w * 144, (w + 1) * 144)
                scores = dot_t(q, ks) + jnp.concatenate([bias[0, rows], bias[1, rows, :64]], 1)
                outs.append(softmax_mix(scores, vs, SLOT, masks))
    heads_out = jnp.concatenate(outs, axis=0).astype(BF)
    attended = dot(back, dot(heads_out, w_out).astype(BF))
    middle = (stream.astype(F32) + attended).astype(BF)
    return feed_forward(middle, gain1, w_up, w_down)


def pick_table(table_ref, block, window, table):
    rows = table_ref[block].astype(F32)
    at = lax.broadcasted_iota(jnp.int32, rows.shape, 1)
    table[...] = jnp.sum(jnp.where(at == window, rows, 0.0), axis=1)


def put(ref, rows, value):
    for k in range(2):
        ref[k, rows, :] = value[:, k * 128 : (k + 1) * 128]


def widened(table, start, extra):
    part = table[:, start : start + 6 * OFFS]
    wide = jnp.concatenate([part, jnp.zeros((HEADS, 256 - 6 * OFFS), F32)], axis=1)
    return wide if extra is None else wide + extra


def bias_rolls(parts, sel):
    lane = lax.broadcasted_iota(jnp.int32, parts[0].shape, 1)
    fixed = [jnp.where(lane >= MASK_AT, p, 0.0) for p in parts]
    moving = [jnp.where(lane < MASK_AT, p, 0.0) for p in parts]
    for xp in range(WX):
        rows = [
            (pltpu.roll(m, 256 - xp, 1) if xp else m) + f for m, f in zip(moving, fixed)
        ]
        yield xp, dot(jnp.concatenate(rows, axis=1).astype(BF), sel)


def bias_regular(table, sel, lhs, out_ref):
    for zp in range(2):
        for zq in range(2):
            for yp in range(6):
                start = ((zp * 2 + zq) * 6 + yp) * 6 * OFFS
                rows = pl.ds(zp * 40 + yp, HEADS, stride=6)
                put(lhs.at[zq], rows, widened(table, start, None))
    parts = [jnp.concatenate([lhs[k, 0], lhs[k, 1]], axis=1) for k in range(2)]
    for xp, rows in bias_rolls(parts, sel):
        for zp in range(2):
            put(out_ref, pl.ds(2 * xp + zp, 36, stride=24), rows[zp * 40 : zp * 40 + 36])


def tables_kernel(
    lev_ref, table_ref, label_ref, sel_ref, bias2, keep1, send1, keep3, send3, table, lhs, half
):
    pick_table(table_ref, 2, lev_ref[1], table)
    lhs[...] = jnp.zeros_like(lhs)
    bias_regular(table, sel_ref[...], lhs, bias2)
    lane = lax.broadcasted_iota(jnp.int32, (8, 128), 1)
    level = lax.broadcasted_iota(jnp.int32, (8, 128), 0)
    first = MASK_AT - 128
    tags = jnp.zeros((8, 128), F32)
    for y in range(6):
        column = label_ref[y].astype(F32)[:, 0:1]
        tags = jnp.where(lane == first + y, column, tags)
    in_mask = (lane[0:1] >= first) & (lane[0:1] < first + 6)
    half[...] = jnp.zeros_like(half)
    for block, keep, send in ((1, keep1, send1), (3, keep3, send3)):
        for z in range(2):
            window = lev_ref[z]
            pick_table(table_ref, block, window, table)
            keys = [
                jnp.sum(jnp.where(level == window * 2 + zq, tags, 0.0), axis=0, keepdims=True)
                for zq in range(2)
            ]
            zp = 1 - z
            for yp in range(6):
                mine = jnp.sum(
                    jnp.where(lane[0:1] == first + yp, keys[zp], 0.0), axis=1, keepdims=True
                )
                for zq in range(2):
                    mask = jnp.where(in_mask & (keys[zq] != mine), NEG, 0.0)
                    mask = jnp.concatenate([jnp.zeros((1, 128), F32), mask], axis=1)
                    start = ((zp * 2 + zq) * 6 + yp) * 6 * OFFS
                    rows = pl.ds(z * 24 + yp % 3, HEADS, stride=4)
                    put(half.at[yp // 3, zq], rows, widened(table, start, mask))
        keep[...] = half[0].astype(BF)
        send[...] = half[1].astype(BF).reshape(192, 128)


def bias_shifted_kernel(lev_ref, keep, far, near, sel_ref, pad_ref, out_ref):
    moved = choose(lev_ref[2], near[288:], far[288:]).reshape(2, 2, 48, 128)
    parts = []
    for zq in range(2):
        rows = [jnp.concatenate([src[zq, 0], src[zq, 1]], axis=1) for src in (moved, keep)]
        parts.append(jnp.concatenate(rows, axis=0).astype(F32))
    for xp, rows in bias_rolls(parts, sel_ref[...]):
        rows = rows + pad_ref[...]
        x = (xp + 6) % 12
        xh, xl = x // 6, x % 6
        for yh in range(2):
            for z in range(2):
                base = ((z * 2 + yh) * 2 + xh) * 144 + xl
                at = (yh * 2 + z) * 24
                put(out_ref, pl.ds(base, 24, stride=6), rows[at : at + 24])


def choose(odd, value_odd, value_even):
    return jnp.where(odd == 1, value_odd, value_even)


def halves(lev_ref, stream, gain, to_oct, far, near):
    octs = dot(to_oct, layer_norm(stream.astype(F32), gain))
    west, east = pack(octs[: 4 * SLOT]), pack(octs[4 * SLOT :])
    far[...] = choose(lev_ref[3], east, west)
    near[...] = choose(lev_ref[3], west, east)


def first_kernel(
    lev_ref, x_hbm, gains_hbm, w_qkv_hbm, w_out_hbm, w_up_hbm, w_down_hbm, table_hbm, sel_hbm,
    oct_hbm, stream_out, far, near, table, lhs, bias, x, gains, w_qkv, w_out, w_up, w_down,
    rows, sel, to_oct, sems,
):
    pairs = (
        (table_hbm.at[pl.ds(0, 1)], rows), (sel_hbm, sel), (x_hbm, x), (gains_hbm, gains),
        (w_qkv_hbm.at[0], w_qkv), (w_out_hbm.at[0], w_out), (w_up_hbm.at[0], w_up),
        (w_down_hbm.at[0], w_down), (oct_hbm, to_oct),
    )
    copies = [pltpu.make_async_copy(a, b, sems.at[i]) for i, (a, b) in enumerate(pairs)]
    for copy in copies:
        copy.start()
    copies[0].wait()
    pick_table(rows, 0, lev_ref[1], table)
    lhs[...] = jnp.zeros_like(lhs)
    copies[1].wait()
    bias_regular(table, sel[...], lhs, bias)
    for copy in copies[2:]:
        copy.wait()
    stream = regular_block(
        x[...].astype(F32).reshape(T, D).astype(BF), gains[0, 0:1], gains[0, 1:2], w_qkv[...],
        w_out[...], w_up[...], w_down[...], bias,
    )
    stream_out[...] = stream
    halves(lev_ref, stream, gains[1, 0:1], to_oct[...], far, near)


def middle_kernel(
    lev_ref, stream_in, below, above, q, k_own, v_own, gains, w_qkv, w_out, w_up, w_down, bias1,
    bias2, to_oct, back, stream_out, far, near, k_ref, v_ref,
):
    stream = shifted_block(
        stream_in[...], below, above, q, k_own, v_own, gains[1, 1:2], w_qkv[1], w_out[1], w_up[1],
        w_down[1], bias1, back[...], k_ref, v_ref,
    )
    stream = regular_block(
        stream, gains[2, 0:1], gains[2, 1:2], w_qkv[2], w_out[2], w_up[2], w_down[2], bias2
    )
    stream_out[...] = stream
    halves(lev_ref, stream, gains[3, 0:1], to_oct[...], far, near)


def last_kernel(
    stream_in, below, above, q, k_own, v_own, gains, w_qkv, w_out, w_up, w_down, bias3, back, out,
    k_ref, v_ref,
):
    stream = shifted_block(
        stream_in[...], below, above, q, k_own, v_own, gains[3, 1:2], w_qkv[3], w_out[3], w_up[3],
        w_down[3], bias3, back[...], k_ref, v_ref,
    )
    out[...] = stream.astype(F32).reshape(T // 2, 2, D).astype(BF)


def lat_pack_kernel(lev_ref, recv_far, own_far, own_near, recv_near, table_rows, far, near):
    parts = [unpack(ref[...]) for ref in (recv_far, own_far, own_near, recv_near)]
    parts = [choose(lev_ref[3], parts[3 - i], parts[i]) for i in range(4)]
    packed = []
    for yh in range(2):
        rows = [
            part[(yh * 2 + z) * SLOT : (yh * 2 + z + 1) * SLOT] for z in range(2) for part in parts
        ]
        packed.append(pack(jnp.concatenate(rows, axis=0)))
    far[:288] = choose(lev_ref[2], packed[1], packed[0])
    near[:288] = choose(lev_ref[2], packed[0], packed[1])
    far[288:] = table_rows[...]
    near[288:] = table_rows[...]


def lev_pack_kernel(lev_ref, recv_far, own_far, own_near, recv_near, down, up):
    parts = [unpack(ref[:288]) for ref in (recv_far, own_far, own_near, recv_near)]
    parts = [choose(lev_ref[2], parts[3 - i], parts[i]) for i in range(4)]
    for z, ref in ((0, down), (1, up)):
        rows = [part[z * 4 * SLOT : (z + 1) * 4 * SLOT] for part in parts]
        ref[...] = pack(jnp.concatenate(rows, axis=0))


def call(kernel, outs, *args, scratch=(), flops=0, limit=20, scalars=0, place=pltpu.VMEM):
    specs = [pl.BlockSpec(memory_space=pltpu.SMEM)] * scalars
    specs += [pl.BlockSpec(memory_space=place)] * (len(args) - scalars)
    return pl.pallas_call(
        kernel,
        out_shape=outs,
        in_specs=specs,
        scratch_shapes=list(scratch),
        compiler_params=pltpu.CompilerParams(vmem_limit_bytes=int(limit * (1 << 20))),
        cost_estimate=pl.CostEstimate(flops=flops, bytes_accessed=1 << 20, transcendentals=0),
    )(*args)


def shape(*dims, dtype=BF):
    return jax.ShapeDtypeStruct(dims, dtype)


def move(value, axis, steps):
    count = lax.axis_size(axis)
    return lax.ppermute(value, axis, [(i, (i + steps) % count) for i in range(count)])


def swap(value, axis, far):
    count = lax.axis_size(axis)
    steps = (-1, 1) if far else (1, -1)
    return lax.ppermute(value, axis, [(i, (i + steps[i % 2]) % count) for i in range(count)])


def halo(block, levels, far, near, keep, send, w_qkv, sel_shift, pad):
    recv_far = swap(far, "lon", True)
    recv_near = swap(near, "lon", False)
    far, near = call(
        lat_pack_kernel, [shape(480, 128)] * 2, levels, recv_far, far, near, recv_near, send,
        limit=4, scalars=1,
    )
    recv_far = swap(far, "lat", True)
    recv_near = swap(near, "lat", False)
    down, up = call(
        lev_pack_kernel, [shape(576, 128)] * 2, levels, recv_far, far, near, recv_near,
        limit=4, scalars=1,
    )
    above = move(down, "lev", -1)
    below = move(up, "lev", 1)
    q, k, v = call(
        functools.partial(own_keys_kernel, block),
        [shape(8 * SLOT, D, dtype=F32), shape(2, 4, 2, PAIR, D), shape(2, 4, 2, PAIR, D)],
        down, up, w_qkv, flops=1 << 30, limit=8,
    )
    bias = call(
        bias_shifted_kernel, shape(2, 8 * 144, 128, dtype=F32), levels, keep, recv_far, recv_near,
        sel_shift, pad, flops=1 << 30, limit=8, scalars=1,
    )
    return below, above, q, k, v, bias


def per_device(fields, w_qkv, w_out, w_up, w_down, gains, bias_table, labels):
    level = lax.axis_index("lev")
    odd = [lax.axis_index(axis) % 2 for axis in ("lat", "lon")]
    levels = jnp.stack([(level + 3) % 4, level, *odd]).astype(jnp.int32)
    to_oct, back = [jnp.asarray(m, BF) for m in octant_maps()]
    sel_reg, sel_shift, pad = selectors()
    sel_reg, sel_shift = jnp.asarray(sel_reg, BF), jnp.asarray(sel_shift, BF)
    pad = jnp.asarray(pad, F32)
    tables = bias_table[:, :, 0].transpose(0, 2, 1, 3)
    tags = labels.transpose(1, 0, 2)
    weights = (gains, w_qkv, w_out, w_up, w_down.transpose(0, 2, 1))

    bias_shape = (2, HEADS * T, 128)
    table_scratch = [pltpu.VMEM((HEADS, POS), F32), pltpu.VMEM((2, 2, 80, 128), F32)]
    kv_scratch = [pltpu.VMEM((2, 4, 2, PAIR, D), BF)] * 2
    streams = [shape(T, D), shape(144, 128), shape(144, 128)]
    stream, far, near = call(
        first_kernel, streams, levels, fields.transpose(1, 2, 0, 3).reshape(T // 2, 2, D), *weights,
        tables, sel_reg, to_oct,
        scratch=[
            *table_scratch, pltpu.VMEM(bias_shape, F32), pltpu.VMEM((T // 2, 2, D), BF),
            pltpu.VMEM((BLOCKS, 2, D), F32), pltpu.VMEM((D, 3 * D), BF), pltpu.VMEM((D, D), BF),
            pltpu.VMEM((D, FF), BF), pltpu.VMEM((D, FF), BF), pltpu.VMEM((1, HEADS, 4, POS), BF),
            pltpu.VMEM((512, 256), BF), pltpu.VMEM((8 * SLOT, T), BF), pltpu.SemaphoreType.DMA((9,)),
        ],
        flops=1 << 31, scalars=1, place=pltpu.HBM, limit=FIRST_LIMIT,
    )
    rows = [shape(2, 2, 48, 128), shape(192, 128)]
    bias2, keep1, send1, keep3, send3 = call(
        tables_kernel, [shape(*bias_shape, dtype=F32), *rows, *rows], levels, tables, tags, sel_reg,
        scratch=[*table_scratch, pltpu.VMEM((2, 2, 2, 48, 128), F32)], flops=1 << 31, scalars=1,
    )
    *ready, bias1 = halo(1, levels, far, near, keep1, send1, w_qkv, sel_shift, pad)
    stream, far, near = call(
        middle_kernel, streams, levels, stream, *ready, *weights, bias1, bias2, to_oct, back,
        scratch=kv_scratch, flops=1 << 31, scalars=1,
    )
    *ready, bias3 = halo(3, levels, far, near, keep3, send3, w_qkv, sel_shift, pad)
    stream = call(
        last_kernel, shape(T // 2, 2, D), stream, *ready, *weights, bias3, back,
        scratch=kv_scratch, flops=1 << 31,
    )
    return stream.reshape(6, 12, 2, D).transpose(2, 0, 1, 3)


def solution(mesh):
    in_specs = (
        P("lev", "lat", "lon", None),
        P(),
        P(),
        P(),
        P(),
        P(),
        P(None, None, "lat", None, None),
        P(None, "lat", "lon"),
    )
    return jax.shard_map(
        per_device,
        mesh=mesh,
        in_specs=in_specs,
        out_specs=P("lev", "lat", "lon", None),
        check_vma=False,
    )
```

```python
import functools

import jax
import jax.numpy as jnp
import numpy as np
from jax import lax
from jax.experimental import pallas as pl
from jax.experimental.pallas import tpu as pltpu
from jax.sharding import PartitionSpec as P

HEADS = 6
HD = 32
WZ = 2
WY = 6
WX = 12
BLOCKS = 4
D = 192
FF = 768
T = WZ * WY * WX
OFFS = 2 * WX - 1
POS = 3312
SLOT = 24
PAIR = 2 * SLOT
FIRST_LIMIT = 62.0
NEG = -1e30
MASK_AT = 192
BF = jnp.bfloat16
F32 = jnp.float32


def octant_maps():
    to_oct = np.zeros((8 * SLOT, T), np.float32)
    back = np.zeros((T, 8 * SLOT), np.float32)
    for z in range(2):
        for y in range(6):
            for x in range(12):
                yh, yl, xh, xl = y // 3, y % 3, x // 6, x % 6
                tok = (y * 12 + x) * 2 + z
                slot = yl * 6 + xl
                to_oct[((xh * 2 + yh) * 2 + z) * SLOT + slot, tok] = 1.0
                back[tok, ((z * 2 + yh) * 2 + xh) * SLOT + slot] = 1.0
    return to_oct, back


def selectors():
    regular = np.zeros((2, 256, 256), np.float32)
    for zq in range(2):
        for yq in range(6):
            for xq in range(12):
                regular[zq, yq * OFFS + 11 - xq, (yq * 12 + xq) * 2 + zq] = 1.0
    shifted = np.zeros((2, 256, 256), np.float32)
    pad = np.full((1, 256), NEG, np.float32)
    for zk in range(2):
        for yk in range(2):
            for xk in range(2):
                for yl in range(3):
                    for xl in range(6):
                        lane = ((zk * 2 + yk) * 2 + xk) * SLOT + yl * 6 + xl
                        yq, xq = yk * 3 + yl, xk * 6 + xl
                        shifted[zk, yq * OFFS + 11 - xq, lane] = 1.0
                        shifted[zk, MASK_AT + yq, lane] = 1.0
                        pad[0, lane] = 0.0
    return regular.reshape(512, 256), shifted.reshape(512, 256), pad


def dot(a, b):
    return jnp.dot(a, b, preferred_element_type=F32)


def dot_t(a, b):
    return lax.dot_general(a, b, (((1,), (1,)), ((), ())), preferred_element_type=F32)


def layer_norm(values, gain):
    center = values - jnp.mean(values, axis=-1, keepdims=True)
    spread = jnp.mean(center * center, axis=-1, keepdims=True)
    return (center * lax.rsqrt(spread + 1e-05) * gain).astype(BF)


def head_mask(rows):
    lane_head = lax.broadcasted_iota(jnp.int32, (rows, D), 1) // HD
    return [lane_head == h for h in range(HEADS)]


def spread_heads(q, masks):
    return jnp.concatenate([jnp.where(m, q, 0.0) for m in masks], axis=0).astype(BF)


def softmax_mix(scores, keys_v, rows, masks):
    top = jnp.max(scores, axis=-1, keepdims=True)
    terms = jnp.exp(scores - top)
    total = 1.0 / jnp.sum(terms, axis=-1, keepdims=True)
    mixed = dot(terms.astype(BF), keys_v) * total
    out = mixed[0:rows]
    for h in range(1, HEADS):
        out = jnp.where(masks[h], mixed[h * rows : (h + 1) * rows], out)
    return out


def feed_forward(middle, gain, w_up, w_down):
    normed = layer_norm(middle.astype(F32), gain)
    up = dot(normed, w_up)
    hidden = (0.5 * up * (1.0 + lax.erf(up * np.float32(0.5**0.5)))).astype(BF)
    return (middle.astype(F32) + dot_t(hidden, w_down)).astype(BF)


def regular_block(stream, gain0, gain1, w_qkv, w_out, w_up, w_down, bias):
    normed = layer_norm(stream.astype(F32), gain0)
    qkv = dot(normed, w_qkv)
    q = qkv[:, :D].astype(BF).astype(F32) * np.float32(HD**-0.5)
    k = qkv[:, D : 2 * D].astype(BF)
    v = qkv[:, 2 * D :].astype(BF)
    masks = head_mask(T)
    bias = jnp.concatenate([bias[0], bias[1, :, : T - 128]], axis=1)
    scores = dot_t(spread_heads(q, masks), k) + bias
    heads_out = softmax_mix(scores, v, T, masks).astype(BF)
    attended = dot(heads_out, w_out).astype(BF)
    middle = (stream.astype(F32) + attended.astype(F32)).astype(BF)
    return feed_forward(middle, gain1, w_up, w_down)


def pack(tokens):
    half = tokens.shape[0] // 2
    tails = jnp.concatenate([tokens[:half, 128:], tokens[half:, 128:]], axis=1)
    return jnp.concatenate([tokens[:, :128], tails], axis=0).astype(BF)


def unpack(packed):
    values = packed.astype(F32)
    rows = values.shape[0] // 3 * 2
    tails = jnp.concatenate([values[rows:, :64], values[rows:, 64:]], axis=0)
    return jnp.concatenate([values[:rows], tails], axis=1)


def keys_values(tokens, w_qkv, k_ref, v_ref):
    kv = dot(tokens.astype(BF), w_qkv[:, D:])
    k_ref[...] = kv[:, :D].astype(BF).reshape(k_ref.shape)
    v_ref[...] = kv[:, D:].astype(BF).reshape(v_ref.shape)


def own_keys_kernel(block, down, up, w_qkv, q_ref, k_ref, v_ref):
    own = []
    for z, ref in enumerate((down, up)):
        tokens = unpack(ref[...])
        keys_values(tokens, w_qkv[block], k_ref.at[z], v_ref.at[z])
        for yh in range(2):
            row = (1 + yh) * 4 * SLOT + SLOT
            own.append(tokens[row : row + PAIR])
    q = dot(jnp.concatenate(own, axis=0).astype(BF), w_qkv[block, :, :D]).astype(BF)
    q_ref[...] = q.astype(F32) * np.float32(HD**-0.5)


def shifted_block(
    stream, below, above, q_ref, k_own, v_own, gain1, w_qkv, w_out, w_up, w_down, bias, back,
    k_ref, v_ref,
):
    for i, ref in enumerate((below, above)):
        keys_values(unpack(ref[...]), w_qkv, k_ref.at[i], v_ref.at[i])
    masks = head_mask(SLOT)
    outs = []
    for z in range(2):
        for yh in range(2):
            for xh in range(2):
                w = (z * 2 + yh) * 2 + xh
                sides = ((k_ref, v_ref, 0), (k_own, v_own, 0))
                if z:
                    sides = ((k_own, v_own, 1), (k_ref, v_ref, 1))
                ks, vs = [
                    jnp.concatenate(
                        [s[i][s[2], 2 * yh : 2 * yh + 2, xh].reshape(2 * PAIR, D) for s in sides],
                        axis=0,
                    )
                    for i in range(2)
                ]
                q = spread_heads(q_ref[w * SLOT : (w + 1) * SLOT], masks)
                rows = slice(w * 144, (w + 1) * 144)
                scores = dot_t(q, ks) + jnp.concatenate([bias[0, rows], bias[1, rows, :64]], 1)
                outs.append(softmax_mix(scores, vs, SLOT, masks))
    heads_out = jnp.concatenate(outs, axis=0).astype(BF)
    attended = dot(back, dot(heads_out, w_out).astype(BF))
    middle = (stream.astype(F32) + attended).astype(BF)
    return feed_forward(middle, gain1, w_up, w_down)


def pick_table(table_ref, block, window, table):
    rows = table_ref[block].astype(F32)
    at = lax.broadcasted_iota(jnp.int32, rows.shape, 1)
    table[...] = jnp.sum(jnp.where(at == window, rows, 0.0), axis=1)


def put(ref, rows, value):
    for k in range(2):
        ref[k, rows, :] = value[:, k * 128 : (k + 1) * 128]


def widened(table, start, extra):
    part = table[:, start : start + 6 * OFFS]
    wide = jnp.concatenate([part, jnp.zeros((HEADS, 256 - 6 * OFFS), F32)], axis=1)
    return wide if extra is None else wide + extra


def bias_rolls(parts, sel):
    lane = lax.broadcasted_iota(jnp.int32, parts[0].shape, 1)
    fixed = [jnp.where(lane >= MASK_AT, p, 0.0) for p in parts]
    moving = [jnp.where(lane < MASK_AT, p, 0.0) for p in parts]
    for xp in range(WX):
        rows = [
            (pltpu.roll(m, 256 - xp, 1) if xp else m) + f for m, f in zip(moving, fixed)
        ]
        yield xp, dot(jnp.concatenate(rows, axis=1).astype(BF), sel)


def bias_regular(table, sel, lhs, out_ref):
    for zp in range(2):
        for zq in range(2):
            for yp in range(6):
                start = ((zp * 2 + zq) * 6 + yp) * 6 * OFFS
                rows = pl.ds(zp * 40 + yp, HEADS, stride=6)
                put(lhs.at[zq], rows, widened(table, start, None))
    parts = [jnp.concatenate([lhs[k, 0], lhs[k, 1]], axis=1) for k in range(2)]
    for xp, rows in bias_rolls(parts, sel):
        for zp in range(2):
            put(out_ref, pl.ds(2 * xp + zp, 36, stride=24), rows[zp * 40 : zp * 40 + 36])


def tables_kernel(
    table_ref, label_ref, sel_ref, bias2, keep1, send1, keep3, send3, table, lhs, half
):
    pick_table(table_ref, 2, level_at(0), table)
    lhs[...] = jnp.zeros_like(lhs)
    bias_regular(table, sel_ref[...], lhs, bias2)
    lane = lax.broadcasted_iota(jnp.int32, (8, 128), 1)
    level = lax.broadcasted_iota(jnp.int32, (8, 128), 0)
    first = MASK_AT - 128
    tags = jnp.zeros((8, 128), F32)
    for y in range(6):
        column = label_ref[y].astype(F32)[:, 0:1]
        tags = jnp.where(lane == first + y, column, tags)
    in_mask = (lane[0:1] >= first) & (lane[0:1] < first + 6)
    half[...] = jnp.zeros_like(half)
    for block, keep, send in ((1, keep1, send1), (3, keep3, send3)):
        for z in range(2):
            window = level_at(z - 1)
            pick_table(table_ref, block, window, table)
            keys = [
                jnp.sum(jnp.where(level == window * 2 + zq, tags, 0.0), axis=0, keepdims=True)
                for zq in range(2)
            ]
            zp = 1 - z
            for yp in range(6):
                mine = jnp.sum(
                    jnp.where(lane[0:1] == first + yp, keys[zp], 0.0), axis=1, keepdims=True
                )
                for zq in range(2):
                    mask = jnp.where(in_mask & (keys[zq] != mine), NEG, 0.0)
                    mask = jnp.concatenate([jnp.zeros((1, 128), F32), mask], axis=1)
                    start = ((zp * 2 + zq) * 6 + yp) * 6 * OFFS
                    rows = pl.ds(z * 24 + yp % 3, HEADS, stride=4)
                    put(half.at[yp // 3, zq], rows, widened(table, start, mask))
        keep[...] = half[0].astype(BF)
        send[...] = half[1].astype(BF).reshape(192, 128)


def bias_shifted_kernel(keep, far, near, sel_ref, pad_ref, out_ref):
    moved = choose(parity("lat"), near[288:], far[288:]).reshape(2, 2, 48, 128)
    parts = []
    for zq in range(2):
        rows = [jnp.concatenate([src[zq, 0], src[zq, 1]], axis=1) for src in (moved, keep)]
        parts.append(jnp.concatenate(rows, axis=0).astype(F32))
    for xp, rows in bias_rolls(parts, sel_ref[...]):
        rows = rows + pad_ref[...]
        x = (xp + 6) % 12
        xh, xl = x // 6, x % 6
        for yh in range(2):
            for z in range(2):
                base = ((z * 2 + yh) * 2 + xh) * 144 + xl
                at = (yh * 2 + z) * 24
                put(out_ref, pl.ds(base, 24, stride=6), rows[at : at + 24])


def parity(axis):
    return lax.rem(lax.axis_index(axis), 2)


def level_at(steps):
    return lax.rem(lax.axis_index("lev") + 4 + steps, 4)


def choose(odd, value_odd, value_even):
    return jnp.where(odd == 1, value_odd, value_even)


def halves(stream, gain, to_oct, far, near):
    octs = dot(to_oct, layer_norm(stream.astype(F32), gain))
    west, east = pack(octs[: 4 * SLOT]), pack(octs[4 * SLOT :])
    far[...] = choose(parity("lon"), east, west)
    near[...] = choose(parity("lon"), west, east)


def first_kernel(
    x_hbm, gains_hbm, w_qkv_hbm, w_out_hbm, w_up_hbm, w_down_hbm, table_hbm, sel_hbm,
    oct_hbm, stream_out, far, near, table, lhs, bias, x, gains, w_qkv, w_out, w_up, w_down,
    rows, sel, to_oct, sems,
):
    pairs = (
        (table_hbm.at[pl.ds(0, 1)], rows), (sel_hbm, sel), (x_hbm, x), (gains_hbm, gains),
        (w_qkv_hbm.at[0], w_qkv), (w_out_hbm.at[0], w_out), (w_up_hbm.at[0], w_up),
        (w_down_hbm.at[0], w_down), (oct_hbm, to_oct),
    )
    copies = [pltpu.make_async_copy(a, b, sems.at[i]) for i, (a, b) in enumerate(pairs)]
    for copy in copies:
        copy.start()
    copies[0].wait()
    pick_table(rows, 0, level_at(0), table)
    lhs[...] = jnp.zeros_like(lhs)
    copies[1].wait()
    bias_regular(table, sel[...], lhs, bias)
    for copy in copies[2:]:
        copy.wait()
    stream = regular_block(
        x[...].astype(F32).reshape(T, D).astype(BF), gains[0, 0:1], gains[0, 1:2], w_qkv[...],
        w_out[...], w_up[...], w_down[...], bias,
    )
    stream_out[...] = stream
    halves(stream, gains[1, 0:1], to_oct[...], far, near)


def middle_kernel(
    stream_in, below, above, q, k_own, v_own, gains, w_qkv, w_out, w_up, w_down, bias1,
    bias2, to_oct, back, stream_out, far, near, k_ref, v_ref,
):
    stream = shifted_block(
        stream_in[...], below, above, q, k_own, v_own, gains[1, 1:2], w_qkv[1], w_out[1], w_up[1],
        w_down[1], bias1, back[...], k_ref, v_ref,
    )
    stream = regular_block(
        stream, gains[2, 0:1], gains[2, 1:2], w_qkv[2], w_out[2], w_up[2], w_down[2], bias2
    )
    stream_out[...] = stream
    halves(stream, gains[3, 0:1], to_oct[...], far, near)


def last_kernel(
    stream_in, below, above, q, k_own, v_own, gains, w_qkv, w_out, w_up, w_down, bias3, back, out,
    k_ref, v_ref,
):
    stream = shifted_block(
        stream_in[...], below, above, q, k_own, v_own, gains[3, 1:2], w_qkv[3], w_out[3], w_up[3],
        w_down[3], bias3, back[...], k_ref, v_ref,
    )
    out[...] = stream.astype(F32).reshape(T // 2, 2, D).astype(BF)


def lat_pack_kernel(recv_far, own_far, own_near, recv_near, table_rows, far, near):
    parts = [unpack(ref[...]) for ref in (recv_far, own_far, own_near, recv_near)]
    parts = [choose(parity("lon"), parts[3 - i], parts[i]) for i in range(4)]
    packed = []
    for yh in range(2):
        rows = [
            part[(yh * 2 + z) * SLOT : (yh * 2 + z + 1) * SLOT] for z in range(2) for part in parts
        ]
        packed.append(pack(jnp.concatenate(rows, axis=0)))
    far[:288] = choose(parity("lat"), packed[1], packed[0])
    near[:288] = choose(parity("lat"), packed[0], packed[1])
    far[288:] = table_rows[...]
    near[288:] = table_rows[...]


def lev_pack_kernel(recv_far, own_far, own_near, recv_near, down, up):
    parts = [unpack(ref[:288]) for ref in (recv_far, own_far, own_near, recv_near)]
    parts = [choose(parity("lat"), parts[3 - i], parts[i]) for i in range(4)]
    for z, ref in ((0, down), (1, up)):
        rows = [part[z * 4 * SLOT : (z + 1) * 4 * SLOT] for part in parts]
        ref[...] = pack(jnp.concatenate(rows, axis=0))


def call(kernel, outs, *args, scratch=(), flops=0, limit=20, place=pltpu.VMEM):
    specs = [pl.BlockSpec(memory_space=place)] * len(args)
    return pl.pallas_call(
        kernel,
        out_shape=outs,
        in_specs=specs,
        scratch_shapes=list(scratch),
        compiler_params=pltpu.CompilerParams(vmem_limit_bytes=int(limit * (1 << 20))),
        cost_estimate=pl.CostEstimate(flops=flops, bytes_accessed=1 << 20, transcendentals=0),
    )(*args)


def shape(*dims, dtype=BF):
    return jax.ShapeDtypeStruct(dims, dtype)


def move(value, axis, steps):
    count = lax.axis_size(axis)
    return lax.ppermute(value, axis, [(i, (i + steps) % count) for i in range(count)])


def swap(value, axis, far):
    count = lax.axis_size(axis)
    steps = (-1, 1) if far else (1, -1)
    return lax.ppermute(value, axis, [(i, (i + steps[i % 2]) % count) for i in range(count)])


def halo(block, far, near, keep, send, w_qkv, sel_shift, pad):
    recv_far = swap(far, "lon", True)
    recv_near = swap(near, "lon", False)
    far, near = call(
        lat_pack_kernel, [shape(480, 128)] * 2, recv_far, far, near, recv_near, send,
        limit=4,
    )
    recv_far = swap(far, "lat", True)
    recv_near = swap(near, "lat", False)
    down, up = call(
        lev_pack_kernel, [shape(576, 128)] * 2, recv_far, far, near, recv_near,
        limit=4,
    )
    above = move(down, "lev", -1)
    below = move(up, "lev", 1)
    q, k, v = call(
        functools.partial(own_keys_kernel, block),
        [shape(8 * SLOT, D, dtype=F32), shape(2, 4, 2, PAIR, D), shape(2, 4, 2, PAIR, D)],
        down, up, w_qkv, flops=1 << 30, limit=8,
    )
    bias = call(
        bias_shifted_kernel, shape(2, 8 * 144, 128, dtype=F32), keep, recv_far, recv_near,
        sel_shift, pad, flops=1 << 30, limit=8,
    )
    return below, above, q, k, v, bias


def per_device(fields, w_qkv, w_out, w_up, w_down, gains, bias_table, labels):
    to_oct, back = [jnp.asarray(m, BF) for m in octant_maps()]
    sel_reg, sel_shift, pad = selectors()
    sel_reg, sel_shift = jnp.asarray(sel_reg, BF), jnp.asarray(sel_shift, BF)
    pad = jnp.asarray(pad, F32)
    tables = bias_table[:, :, 0].transpose(0, 2, 1, 3)
    tags = labels.transpose(1, 0, 2)
    weights = (gains, w_qkv, w_out, w_up, w_down.transpose(0, 2, 1))

    bias_shape = (2, HEADS * T, 128)
    table_scratch = [pltpu.VMEM((HEADS, POS), F32), pltpu.VMEM((2, 2, 80, 128), F32)]
    kv_scratch = [pltpu.VMEM((2, 4, 2, PAIR, D), BF)] * 2
    streams = [shape(T, D), shape(144, 128), shape(144, 128)]
    stream, far, near = call(
        first_kernel, streams, fields.transpose(1, 2, 0, 3).reshape(T // 2, 2, D), *weights,
        tables, sel_reg, to_oct,
        scratch=[
            *table_scratch, pltpu.VMEM(bias_shape, F32), pltpu.VMEM((T // 2, 2, D), BF),
            pltpu.VMEM((BLOCKS, 2, D), F32), pltpu.VMEM((D, 3 * D), BF), pltpu.VMEM((D, D), BF),
            pltpu.VMEM((D, FF), BF), pltpu.VMEM((D, FF), BF), pltpu.VMEM((1, HEADS, 4, POS), BF),
            pltpu.VMEM((512, 256), BF), pltpu.VMEM((8 * SLOT, T), BF), pltpu.SemaphoreType.DMA((9,)),
        ],
        flops=1 << 31, place=pltpu.HBM, limit=FIRST_LIMIT,
    )
    rows = [shape(2, 2, 48, 128), shape(192, 128)]
    bias2, keep1, send1, keep3, send3 = call(
        tables_kernel, [shape(*bias_shape, dtype=F32), *rows, *rows], tables, tags, sel_reg,
        scratch=[*table_scratch, pltpu.VMEM((2, 2, 2, 48, 128), F32)], flops=1 << 31,
    )
    *ready, bias1 = halo(1, far, near, keep1, send1, w_qkv, sel_shift, pad)
    stream, far, near = call(
        middle_kernel, streams, stream, *ready, *weights, bias1, bias2, to_oct, back,
        scratch=kv_scratch, flops=1 << 31,
    )
    *ready, bias3 = halo(3, far, near, keep3, send3, w_qkv, sel_shift, pad)
    stream = call(
        last_kernel, shape(T // 2, 2, D), stream, *ready, *weights, bias3, back,
        scratch=kv_scratch, flops=1 << 31,
    )
    return stream.reshape(6, 12, 2, D).transpose(2, 0, 1, 3)


def solution(mesh):
    in_specs = (
        P("lev", "lat", "lon", None),
        P(),
        P(),
        P(),
        P(),
        P(),
        P(None, None, "lat", None, None),
        P(None, "lat", "lon"),
    )
    return jax.shard_map(
        per_device,
        mesh=mesh,
        in_specs=in_specs,
        out_specs=P("lev", "lat", "lon", None),
        check_vma=False,
    )
```

```python
import functools

import jax
import jax.numpy as jnp
import numpy as np
from jax import lax
from jax.experimental import pallas as pl
from jax.experimental.pallas import tpu as pltpu
from jax.sharding import PartitionSpec as P

HEADS = 6
HD = 32
WZ = 2
WY = 6
WX = 12
BLOCKS = 4
D = 192
FF = 768
T = WZ * WY * WX
OFFS = 2 * WX - 1
POS = 3312
SLOT = 24
PAIR = 2 * SLOT
NEG = -1e30
MASK_AT = 192
BF = jnp.bfloat16
F32 = jnp.float32


def octant_maps():
    to_oct = np.zeros((8 * SLOT, T), np.float32)
    back = np.zeros((T, 8 * SLOT), np.float32)
    for z in range(2):
        for y in range(6):
            for x in range(12):
                yh, yl, xh, xl = y // 3, y % 3, x // 6, x % 6
                tok = (y * 12 + x) * 2 + z
                slot = yl * 6 + xl
                to_oct[((xh * 2 + yh) * 2 + z) * SLOT + slot, tok] = 1.0
                back[tok, ((z * 2 + yh) * 2 + xh) * SLOT + slot] = 1.0
    return to_oct, back


def selectors():
    regular = np.zeros((2, 256, 256), np.float32)
    for zq in range(2):
        for yq in range(6):
            for xq in range(12):
                regular[zq, yq * OFFS + 11 - xq, (yq * 12 + xq) * 2 + zq] = 1.0
    shifted = np.zeros((2, 256, 256), np.float32)
    pad = np.full((1, 256), NEG, np.float32)
    for zk in range(2):
        for yk in range(2):
            for xk in range(2):
                for yl in range(3):
                    for xl in range(6):
                        lane = ((zk * 2 + yk) * 2 + xk) * SLOT + yl * 6 + xl
                        yq, xq = yk * 3 + yl, xk * 6 + xl
                        shifted[zk, yq * OFFS + 11 - xq, lane] = 1.0
                        shifted[zk, MASK_AT + yq, lane] = 1.0
                        pad[0, lane] = 0.0
    return regular.reshape(512, 256), shifted.reshape(512, 256), pad


def dot(a, b):
    return jnp.dot(a, b, preferred_element_type=F32)


def dot_t(a, b):
    return lax.dot_general(a, b, (((1,), (1,)), ((), ())), preferred_element_type=F32)


def layer_norm(values, gain):
    center = values - jnp.mean(values, axis=-1, keepdims=True)
    spread = jnp.mean(center * center, axis=-1, keepdims=True)
    return (center * lax.rsqrt(spread + 1e-05) * gain).astype(BF)


def head_mask(rows):
    lane_head = lax.broadcasted_iota(jnp.int32, (rows, D), 1) // HD
    return [lane_head == h for h in range(HEADS)]


def spread_heads(q, masks):
    return jnp.concatenate([jnp.where(m, q, 0.0) for m in masks], axis=0).astype(BF)


def softmax_mix(scores, keys_v, rows, masks):
    top = jnp.max(scores, axis=-1, keepdims=True)
    terms = jnp.exp(scores - top)
    total = 1.0 / jnp.sum(terms, axis=-1, keepdims=True)
    mixed = dot(terms.astype(BF), keys_v) * total
    out = mixed[0:rows]
    for h in range(1, HEADS):
        out = jnp.where(masks[h], mixed[h * rows : (h + 1) * rows], out)
    return out


def feed_forward(middle, gain, w_up, w_down):
    normed = layer_norm(middle.astype(F32), gain)
    up = dot(normed, w_up)
    hidden = (0.5 * up * (1.0 + lax.erf(up * np.float32(0.5**0.5)))).astype(BF)
    return (middle.astype(F32) + dot_t(hidden, w_down)).astype(BF)


def regular_block(stream, gain0, gain1, w_qkv, w_out, w_up, w_down, bias):
    normed = layer_norm(stream.astype(F32), gain0)
    qkv = dot(normed, w_qkv)
    q = qkv[:, :D].astype(BF).astype(F32) * np.float32(HD**-0.5)
    k = qkv[:, D : 2 * D].astype(BF)
    v = qkv[:, 2 * D :].astype(BF)
    masks = head_mask(T)
    bias = jnp.concatenate([bias[0], bias[1, :, : T - 128]], axis=1)
    scores = dot_t(spread_heads(q, masks), k) + bias
    heads_out = softmax_mix(scores, v, T, masks).astype(BF)
    attended = dot(heads_out, w_out).astype(BF)
    middle = (stream.astype(F32) + attended.astype(F32)).astype(BF)
    return feed_forward(middle, gain1, w_up, w_down)


def pack(tokens):
    half = tokens.shape[0] // 2
    tails = jnp.concatenate([tokens[:half, 128:], tokens[half:, 128:]], axis=1)
    return jnp.concatenate([tokens[:, :128], tails], axis=0).astype(BF)


def unpack(packed):
    values = packed.astype(F32)
    rows = values.shape[0] // 3 * 2
    tails = jnp.concatenate([values[rows:, :64], values[rows:, 64:]], axis=0)
    return jnp.concatenate([values[:rows], tails], axis=1)


def keys_values(tokens, w_qkv, k_ref, v_ref):
    kv = dot(tokens.astype(BF), w_qkv[:, D:])
    k_ref[...] = kv[:, :D].astype(BF).reshape(k_ref.shape)
    v_ref[...] = kv[:, D:].astype(BF).reshape(v_ref.shape)


def own_keys_kernel(block, down, up, w_qkv, q_ref, k_ref, v_ref):
    own = []
    for z, ref in enumerate((down, up)):
        tokens = unpack(ref[...])
        keys_values(tokens, w_qkv[block], k_ref.at[z], v_ref.at[z])
        for yh in range(2):
            row = (1 + yh) * 4 * SLOT + SLOT
            own.append(tokens[row : row + PAIR])
    q = dot(jnp.concatenate(own, axis=0).astype(BF), w_qkv[block, :, :D]).astype(BF)
    q_ref[...] = q.astype(F32) * np.float32(HD**-0.5)


def level_windows(z, halo, q_ref, k_own, v_own, w_qkv, bias, k_ref, v_ref):
    keys_values(unpack(halo[...]), w_qkv, k_ref, v_ref)
    masks = head_mask(SLOT)
    outs = []
    for yh in range(2):
        for xh in range(2):
            sides = ((k_ref, v_ref), (k_own.at[z], v_own.at[z]))
            if z:
                sides = sides[::-1]
            ks, vs = [
                jnp.concatenate(
                    [side[i][2 * yh : 2 * yh + 2, xh].reshape(2 * PAIR, D) for side in sides], axis=0
                )
                for i in range(2)
            ]
            w = (z * 2 + yh) * 2 + xh
            q = spread_heads(q_ref[w * SLOT : (w + 1) * SLOT], masks)
            rows = slice(w * 144, (w + 1) * 144)
            scores = dot_t(q, ks) + jnp.concatenate([bias[0, rows], bias[1, rows, :64]], 1)
            outs.append(softmax_mix(scores, vs, SLOT, masks))
    return jnp.concatenate(outs, axis=0).astype(BF)


def lower_kernel(block, below, q, k_own, v_own, w_qkv, bias, out, k_ref, v_ref):
    out[...] = level_windows(0, below, q, k_own, v_own, w_qkv[block], bias, k_ref, v_ref)


def shifted_block(
    stream, lower, above, q, k_own, v_own, gain1, w_qkv, w_out, w_up, w_down, bias, back,
    k_ref, v_ref,
):
    upper = level_windows(1, above, q, k_own, v_own, w_qkv, bias, k_ref, v_ref)
    heads_out = jnp.concatenate([lower, upper], axis=0)
    attended = dot(back, dot(heads_out, w_out).astype(BF))
    middle = (stream.astype(F32) + attended).astype(BF)
    return feed_forward(middle, gain1, w_up, w_down)


def pick_table(table_ref, block, window, table):
    rows = table_ref[block].astype(F32)
    at = lax.broadcasted_iota(jnp.int32, rows.shape, 1)
    table[...] = jnp.sum(jnp.where(at == window, rows, 0.0), axis=1)


def put(ref, rows, value):
    for k in range(2):
        ref[k, rows, :] = value[:, k * 128 : (k + 1) * 128]


def widened(table, start, extra):
    part = table[:, start : start + 6 * OFFS]
    wide = jnp.concatenate([part, jnp.zeros((HEADS, 256 - 6 * OFFS), F32)], axis=1)
    return wide if extra is None else wide + extra


def bias_rolls(parts, sel):
    lane = lax.broadcasted_iota(jnp.int32, parts[0].shape, 1)
    fixed = [jnp.where(lane >= MASK_AT, p, 0.0) for p in parts]
    moving = [jnp.where(lane < MASK_AT, p, 0.0) for p in parts]
    for xp in range(WX):
        rows = [
            (pltpu.roll(m, 256 - xp, 1) if xp else m) + f for m, f in zip(moving, fixed)
        ]
        yield xp, dot(jnp.concatenate(rows, axis=1).astype(BF), sel)


def bias_regular(table, sel, lhs, out_ref):
    for zp in range(2):
        for zq in range(2):
            for yp in range(6):
                start = ((zp * 2 + zq) * 6 + yp) * 6 * OFFS
                rows = pl.ds(zp * 40 + yp, HEADS, stride=6)
                put(lhs.at[zq], rows, widened(table, start, None))
    parts = [jnp.concatenate([lhs[k, 0], lhs[k, 1]], axis=1) for k in range(2)]
    for xp, rows in bias_rolls(parts, sel):
        for zp in range(2):
            put(out_ref, pl.ds(2 * xp + zp, 36, stride=24), rows[zp * 40 : zp * 40 + 36])


def tables_kernel(
    table_ref, label_ref, sel_ref, bias2, keep1, send1, keep3, send3, table, lhs, half
):
    pick_table(table_ref, 2, level_at(0), table)
    lhs[...] = jnp.zeros_like(lhs)
    bias_regular(table, sel_ref[...], lhs, bias2)
    lane = lax.broadcasted_iota(jnp.int32, (8, 128), 1)
    level = lax.broadcasted_iota(jnp.int32, (8, 128), 0)
    first = MASK_AT - 128
    tags = jnp.zeros((8, 128), F32)
    for y in range(6):
        column = label_ref[y].astype(F32)[:, 0:1]
        tags = jnp.where(lane == first + y, column, tags)
    in_mask = (lane[0:1] >= first) & (lane[0:1] < first + 6)
    half[...] = jnp.zeros_like(half)
    for block, keep, send in ((1, keep1, send1), (3, keep3, send3)):
        for z in range(2):
            window = level_at(z - 1)
            pick_table(table_ref, block, window, table)
            keys = [
                jnp.sum(jnp.where(level == window * 2 + zq, tags, 0.0), axis=0, keepdims=True)
                for zq in range(2)
            ]
            zp = 1 - z
            for yp in range(6):
                mine = jnp.sum(
                    jnp.where(lane[0:1] == first + yp, keys[zp], 0.0), axis=1, keepdims=True
                )
                for zq in range(2):
                    mask = jnp.where(in_mask & (keys[zq] != mine), NEG, 0.0)
                    mask = jnp.concatenate([jnp.zeros((1, 128), F32), mask], axis=1)
                    start = ((zp * 2 + zq) * 6 + yp) * 6 * OFFS
                    rows = pl.ds(z * 24 + yp % 3, HEADS, stride=4)
                    put(half.at[yp // 3, zq], rows, widened(table, start, mask))
        keep[...] = half[0].astype(BF)
        send[...] = half[1].astype(BF).reshape(192, 128)


def bias_shifted_kernel(keep, far, near, sel_ref, pad_ref, out_ref):
    moved = choose(parity("lat"), near[288:], far[288:]).reshape(2, 2, 48, 128)
    parts = []
    for zq in range(2):
        rows = [jnp.concatenate([src[zq, 0], src[zq, 1]], axis=1) for src in (moved, keep)]
        parts.append(jnp.concatenate(rows, axis=0).astype(F32))
    for xp, rows in bias_rolls(parts, sel_ref[...]):
        rows = rows + pad_ref[...]
        x = (xp + 6) % 12
        xh, xl = x // 6, x % 6
        for yh in range(2):
            for z in range(2):
                base = ((z * 2 + yh) * 2 + xh) * 144 + xl
                at = (yh * 2 + z) * 24
                put(out_ref, pl.ds(base, 24, stride=6), rows[at : at + 24])


def parity(axis):
    return lax.rem(lax.axis_index(axis), 2)


def level_at(steps):
    return lax.rem(lax.axis_index("lev") + 4 + steps, 4)


def choose(odd, value_odd, value_even):
    return jnp.where(odd == 1, value_odd, value_even)


def halves(stream, gain, to_oct, far, near):
    octs = dot(to_oct, layer_norm(stream.astype(F32), gain))
    west, east = pack(octs[: 4 * SLOT]), pack(octs[4 * SLOT :])
    far[...] = choose(parity("lon"), east, west)
    near[...] = choose(parity("lon"), west, east)


def first_kernel(
    x_hbm, gains_hbm, w_qkv_hbm, w_out_hbm, w_up_hbm, w_down_hbm, table_hbm, sel_hbm,
    oct_hbm, stream_out, far, near, table, lhs, bias, x, gains, w_qkv, w_out, w_up, w_down,
    rows, sel, to_oct, sems,
):
    pairs = (
        (table_hbm.at[pl.ds(0, 1)], rows), (sel_hbm, sel), (x_hbm, x), (gains_hbm, gains),
        (w_qkv_hbm.at[0], w_qkv), (w_out_hbm.at[0], w_out), (w_up_hbm.at[0], w_up),
        (w_down_hbm.at[0], w_down), (oct_hbm, to_oct),
    )
    copies = [pltpu.make_async_copy(a, b, sems.at[i]) for i, (a, b) in enumerate(pairs)]
    for copy in copies:
        copy.start()
    copies[0].wait()
    pick_table(rows, 0, level_at(0), table)
    lhs[...] = jnp.zeros_like(lhs)
    copies[1].wait()
    bias_regular(table, sel[...], lhs, bias)
    for copy in copies[2:]:
        copy.wait()
    stream = regular_block(
        x[...].reshape(T, D), gains[0, 0:1], gains[0, 1:2], w_qkv[...],
        w_out[...], w_up[...], w_down[...], bias,
    )
    stream_out[...] = stream
    halves(stream, gains[1, 0:1], to_oct[...], far, near)


def middle_kernel(
    stream_in, lower, above, q, k_own, v_own, gains, w_qkv, w_out, w_up, w_down, bias1,
    bias2, to_oct, back, stream_out, far, near, k_ref, v_ref,
):
    stream = shifted_block(
        stream_in[...], lower[...], above, q, k_own, v_own, gains[1, 1:2], w_qkv[1], w_out[1], w_up[1],
        w_down[1], bias1, back[...], k_ref, v_ref,
    )
    stream = regular_block(
        stream, gains[2, 0:1], gains[2, 1:2], w_qkv[2], w_out[2], w_up[2], w_down[2], bias2
    )
    stream_out[...] = stream
    halves(stream, gains[3, 0:1], to_oct[...], far, near)


def last_kernel(
    stream_in, lower, above, q, k_own, v_own, gains, w_qkv, w_out, w_up, w_down, bias3, back, out,
    k_ref, v_ref,
):
    stream = shifted_block(
        stream_in[...], lower[...], above, q, k_own, v_own, gains[3, 1:2], w_qkv[3], w_out[3], w_up[3],
        w_down[3], bias3, back[...], k_ref, v_ref,
    )
    out[...] = stream.reshape(T // 2, 2, D)


def lat_pack_kernel(recv_far, own_far, own_near, recv_near, table_rows, far, near):
    parts = [unpack(ref[...]) for ref in (recv_far, own_far, own_near, recv_near)]
    parts = [choose(parity("lon"), parts[3 - i], parts[i]) for i in range(4)]
    packed = []
    for yh in range(2):
        rows = [
            part[(yh * 2 + z) * SLOT : (yh * 2 + z + 1) * SLOT] for z in range(2) for part in parts
        ]
        packed.append(pack(jnp.concatenate(rows, axis=0)))
    far[:288] = choose(parity("lat"), packed[1], packed[0])
    near[:288] = choose(parity("lat"), packed[0], packed[1])
    far[288:] = table_rows[...]
    near[288:] = table_rows[...]


def lev_pack_kernel(recv_far, own_far, own_near, recv_near, down, up):
    parts = [unpack(ref[:288]) for ref in (recv_far, own_far, own_near, recv_near)]
    parts = [choose(parity("lat"), parts[3 - i], parts[i]) for i in range(4)]
    for z, ref in ((0, down), (1, up)):
        rows = [part[z * 4 * SLOT : (z + 1) * 4 * SLOT] for part in parts]
        ref[...] = pack(jnp.concatenate(rows, axis=0))


def call(kernel, outs, *args, scratch=(), flops=0, limit=20, place=pltpu.VMEM):
    specs = [pl.BlockSpec(memory_space=place)] * len(args)
    if place == pltpu.HBM:
        args = [pltpu.with_memory_space_constraint(arg, place) for arg in args]
    return pl.pallas_call(
        kernel,
        out_shape=outs,
        in_specs=specs,
        scratch_shapes=list(scratch),
        compiler_params=pltpu.CompilerParams(vmem_limit_bytes=int(limit * (1 << 20))),
        cost_estimate=pl.CostEstimate(flops=flops, bytes_accessed=1 << 20, transcendentals=0),
    )(*args)


def shape(*dims, dtype=BF):
    return jax.ShapeDtypeStruct(dims, dtype)


def move(value, axis, steps):
    count = lax.axis_size(axis)
    return lax.ppermute(value, axis, [(i, (i + steps) % count) for i in range(count)])


def swap(value, axis, far):
    count = lax.axis_size(axis)
    steps = (-1, 1) if far else (1, -1)
    return lax.ppermute(value, axis, [(i, (i + steps[i % 2]) % count) for i in range(count)])


def kv_scratch():
    return [pltpu.VMEM((4, 2, PAIR, D), BF)] * 2


def halo(block, far, near, keep, send, w_qkv, sel_shift, pad):
    recv_far = swap(far, "lon", True)
    recv_near = swap(near, "lon", False)
    far, near = call(
        lat_pack_kernel, [shape(480, 128)] * 2, recv_far, far, near, recv_near, send,
        limit=4,
    )
    recv_far = swap(far, "lat", True)
    recv_near = swap(near, "lat", False)
    down, up = call(
        lev_pack_kernel, [shape(576, 128)] * 2, recv_far, far, near, recv_near,
        limit=4,
    )
    above = move(down, "lev", -1)
    below = move(up, "lev", 1)
    q, k, v = call(
        functools.partial(own_keys_kernel, block),
        [shape(8 * SLOT, D, dtype=F32), shape(2, 4, 2, PAIR, D), shape(2, 4, 2, PAIR, D)],
        down, up, w_qkv, flops=1 << 30, limit=8,
    )
    bias = call(
        bias_shifted_kernel, shape(2, 8 * 144, 128, dtype=F32), keep, recv_far, recv_near,
        sel_shift, pad, flops=1 << 30, limit=8,
    )
    lower = call(
        functools.partial(lower_kernel, block), shape(4 * SLOT, D), below, q, k, v, w_qkv, bias,
        scratch=kv_scratch(), flops=1 << 30, limit=8,
    )
    return lower, above, q, k, v, bias


def per_device(fields, w_qkv, w_out, w_up, w_down, gains, bias_table, labels):
    to_oct, back = [jnp.asarray(m, BF) for m in octant_maps()]
    sel_reg, sel_shift, pad = selectors()
    sel_reg, sel_shift = jnp.asarray(sel_reg, BF), jnp.asarray(sel_shift, BF)
    pad = jnp.asarray(pad, F32)
    tables = bias_table[:, :, 0].transpose(0, 2, 1, 3)
    tags = labels.transpose(1, 0, 2)
    weights = (gains, w_qkv, w_out, w_up, w_down.transpose(0, 2, 1))

    bias_shape = (2, HEADS * T, 128)
    table_scratch = [pltpu.VMEM((HEADS, POS), F32), pltpu.VMEM((2, 2, 80, 128), F32)]
    streams = [shape(T, D), shape(144, 128), shape(144, 128)]
    stream, far, near = call(
        first_kernel, streams, fields.transpose(1, 2, 0, 3).reshape(T // 2, 2, D), *weights,
        tables, sel_reg, to_oct,
        scratch=[
            *table_scratch, pltpu.VMEM(bias_shape, F32), pltpu.VMEM((T // 2, 2, D), BF),
            pltpu.VMEM((BLOCKS, 2, D), F32), pltpu.VMEM((D, 3 * D), BF), pltpu.VMEM((D, D), BF),
            pltpu.VMEM((D, FF), BF), pltpu.VMEM((D, FF), BF), pltpu.VMEM((1, HEADS, 4, POS), BF),
            pltpu.VMEM((512, 256), BF), pltpu.VMEM((8 * SLOT, T), BF), pltpu.SemaphoreType.DMA((9,)),
        ],
        flops=1 << 31, place=pltpu.HBM,
    )
    rows = [shape(2, 2, 48, 128), shape(192, 128)]
    bias2, keep1, send1, keep3, send3 = call(
        tables_kernel, [shape(*bias_shape, dtype=F32), *rows, *rows], tables, tags, sel_reg,
        scratch=[*table_scratch, pltpu.VMEM((2, 2, 2, 48, 128), F32)], flops=1 << 31,
    )
    *ready, bias1 = halo(1, far, near, keep1, send1, w_qkv, sel_shift, pad)
    stream, far, near = call(
        middle_kernel, streams, stream, *ready, *weights, bias1, bias2, to_oct, back,
        scratch=kv_scratch(), flops=1 << 31,
    )
    *ready, bias3 = halo(3, far, near, keep3, send3, w_qkv, sel_shift, pad)
    stream = call(
        last_kernel, shape(T // 2, 2, D), stream, *ready, *weights, bias3, back,
        scratch=kv_scratch(), flops=1 << 31,
    )
    return stream.reshape(6, 12, 2, D).transpose(2, 0, 1, 3)


def solution(mesh):
    in_specs = (
        P("lev", "lat", "lon", None),
        P(),
        P(),
        P(),
        P(),
        P(),
        P(None, None, "lat", None, None),
        P(None, "lat", "lon"),
    )
    return jax.shard_map(
        per_device,
        mesh=mesh,
        in_specs=in_specs,
        out_specs=P("lev", "lat", "lon", None),
        check_vma=False,
    )
```

```python
import functools

import jax
import jax.numpy as jnp
import numpy as np
from jax import lax
from jax.experimental import pallas as pl
from jax.experimental.pallas import tpu as pltpu
from jax.sharding import PartitionSpec as P

HEADS = 6
HD = 32
WZ = 2
WY = 6
WX = 12
BLOCKS = 4
D = 192
FF = 768
T = WZ * WY * WX
OFFS = 2 * WX - 1
POS = 3312
SLOT = 24
PAIR = 2 * SLOT
NEG = -1e30
MASK_AT = 192
BF = jnp.bfloat16
F32 = jnp.float32


def octant_maps():
    to_oct = np.zeros((8 * SLOT, T), np.float32)
    back = np.zeros((T, 8 * SLOT), np.float32)
    for z in range(2):
        for y in range(6):
            for x in range(12):
                yh, yl, xh, xl = y // 3, y % 3, x // 6, x % 6
                tok = (y * 12 + x) * 2 + z
                slot = yl * 6 + xl
                to_oct[((xh * 2 + yh) * 2 + z) * SLOT + slot, tok] = 1.0
                back[tok, ((z * 2 + yh) * 2 + xh) * SLOT + slot] = 1.0
    return to_oct, back


def selectors():
    regular = np.zeros((2, 256, 256), np.float32)
    for zq in range(2):
        for yq in range(6):
            for xq in range(12):
                regular[zq, yq * OFFS + 11 - xq, (yq * 12 + xq) * 2 + zq] = 1.0
    shifted = np.zeros((2, 256, 256), np.float32)
    pad = np.full((1, 256), NEG, np.float32)
    for zk in range(2):
        for yk in range(2):
            for xk in range(2):
                for yl in range(3):
                    for xl in range(6):
                        lane = ((zk * 2 + yk) * 2 + xk) * SLOT + yl * 6 + xl
                        yq, xq = yk * 3 + yl, xk * 6 + xl
                        shifted[zk, yq * OFFS + 11 - xq, lane] = 1.0
                        shifted[zk, MASK_AT + yq, lane] = 1.0
                        pad[0, lane] = 0.0
    return regular.reshape(512, 256), shifted.reshape(512, 256), pad


def dot(a, b):
    return jnp.dot(a, b, preferred_element_type=F32)


def dot_t(a, b):
    return lax.dot_general(a, b, (((1,), (1,)), ((), ())), preferred_element_type=F32)


def layer_norm(values, gain):
    center = values - jnp.mean(values, axis=-1, keepdims=True)
    spread = jnp.mean(center * center, axis=-1, keepdims=True)
    return (center * lax.rsqrt(spread + 1e-05) * gain).astype(BF)


def head_mask(rows):
    lane_head = lax.broadcasted_iota(jnp.int32, (rows, D), 1) // HD
    return [lane_head == h for h in range(HEADS)]


def spread_heads(q, masks):
    return jnp.concatenate([jnp.where(m, q, 0.0) for m in masks], axis=0).astype(BF)


def softmax_mix(scores, values, rows, masks):
    tops = [jnp.max(score, axis=-1, keepdims=True) for score in scores]
    terms = [jnp.exp(score - top) for score, top in zip(scores, tops)]
    totals = [1.0 / jnp.sum(term, axis=-1, keepdims=True) for term in terms]
    mixed = [dot(term.astype(BF), v) for term, v in zip(terms, values)]
    outs = []
    for part, total in zip(mixed, totals):
        part = part * total
        out = part[0:rows]
        for h in range(1, HEADS):
            out = jnp.where(masks[h], part[h * rows : (h + 1) * rows], out)
        outs.append(out)
    return outs


def feed_forward(middle, gain, w_up, w_down):
    normed = layer_norm(middle.astype(F32), gain)
    up = dot(normed, w_up)
    hidden = (0.5 * up * (1.0 + lax.erf(up * np.float32(0.5**0.5)))).astype(BF)
    return (middle.astype(F32) + dot_t(hidden, w_down)).astype(BF)


def regular_block(stream, gain0, gain1, w_qkv, w_out, w_up, w_down, bias):
    normed = layer_norm(stream.astype(F32), gain0)
    qkv = dot(normed, w_qkv)
    q = qkv[:, :D].astype(BF).astype(F32) * np.float32(HD**-0.5)
    masks = head_mask(T)
    bias = jnp.concatenate([bias[0], bias[1, :, : T - 128]], axis=1)
    scores, values = [], []
    for at in range(0, stream.shape[0], T):
        k = qkv[at : at + T, D : 2 * D].astype(BF)
        values.append(qkv[at : at + T, 2 * D :].astype(BF))
        scores.append(dot_t(spread_heads(q[at : at + T], masks), k) + bias)
    heads_out = jnp.concatenate(softmax_mix(scores, values, T, masks), axis=0).astype(BF)
    attended = dot(heads_out, w_out).astype(BF)
    middle = (stream.astype(F32) + attended.astype(F32)).astype(BF)
    return feed_forward(middle, gain1, w_up, w_down)


def pack(tokens):
    half = tokens.shape[0] // 2
    tails = jnp.concatenate([tokens[:half, 128:], tokens[half:, 128:]], axis=1)
    return jnp.concatenate([tokens[:, :128], tails], axis=0).astype(BF)


def unpack(packed):
    values = packed.astype(F32)
    rows = values.shape[0] // 3 * 2
    tails = jnp.concatenate([values[rows:, :64], values[rows:, 64:]], axis=0)
    return jnp.concatenate([values[:rows], tails], axis=1)


def keys_values(tokens, w_qkv, k_ref, v_ref):
    kv = dot(tokens.astype(BF), w_qkv[:, D:])
    k_ref[...] = kv[:, :D].astype(BF).reshape(k_ref.shape)
    v_ref[...] = kv[:, D:].astype(BF).reshape(v_ref.shape)


def own_keys_kernel(block, down, up, w_qkv, q_ref, k_ref, v_ref):
    across = k_ref.shape[2] * 2
    own = []
    for z, ref in enumerate((down, up)):
        tokens = unpack(ref[...])
        keys_values(tokens, w_qkv[block], k_ref.at[z], v_ref.at[z])
        for yh in range(2):
            row = ((1 + yh) * across + 1) * SLOT
            own.append(tokens[row : row + (across - 2) * SLOT])
    q = dot(jnp.concatenate(own, axis=0).astype(BF), w_qkv[block, :, :D]).astype(BF)
    q_ref[...] = q.astype(F32) * np.float32(HD**-0.5)


def level_windows(z, halo, q_ref, k_own, v_own, w_qkv, bias, k_ref, v_ref):
    pairs = k_own.shape[2]
    windows = pairs - 1
    keys_values(unpack(halo[...]), w_qkv, k_ref, v_ref)
    masks = head_mask(SLOT)
    sides = ((k_ref, v_ref), (k_own.at[z], v_own.at[z]))
    if z:
        sides = sides[::-1]
    names, scores, values = [], [], []
    for yh in range(2):
        for pair in range(pairs):
            ks, vs = [
                jnp.concatenate(
                    [side[i][2 * yh : 2 * yh + 2, pair].reshape(2 * PAIR, D) for side in sides],
                    axis=0,
                )
                for i in range(2)
            ]
            for half in (2 * pair - 1, 2 * pair):
                if half < 0 or half >= 2 * windows:
                    continue
                at = ((z * 2 + yh) * 2 * windows + half) * SLOT
                q = spread_heads(q_ref[at : at + SLOT], masks)
                at = ((z * 2 + yh) * 2 + half % 2) * 144
                added = jnp.concatenate([bias[0, at : at + 144], bias[1, at : at + 144, :64]], 1)
                names.append((half // 2, yh, half % 2))
                scores.append(dot_t(q, ks) + added)
                values.append(vs)
    outs = dict(zip(names, softmax_mix(scores, values, SLOT, masks)))
    return jnp.concatenate([outs[key] for key in sorted(outs)], axis=0).astype(BF)


def lower_kernel(block, below, q, k_own, v_own, w_qkv, bias, out, k_ref, v_ref):
    out[...] = level_windows(0, below, q, k_own, v_own, w_qkv[block], bias, k_ref, v_ref)


def shifted_block(
    stream, lower, above, q, k_own, v_own, gain1, w_qkv, w_out, w_up, w_down, bias, back,
    k_ref, v_ref,
):
    upper = level_windows(1, above, q, k_own, v_own, w_qkv, bias, k_ref, v_ref)
    rows = 4 * SLOT
    starts = range(0, upper.shape[0], rows)
    heads_out = [half[at : at + rows] for at in starts for half in (lower, upper)]
    projected = dot(jnp.concatenate(heads_out, axis=0), w_out).astype(BF)
    attended = [dot(back, projected[2 * at : 2 * at + 2 * rows]) for at in starts]
    middle = (stream.astype(F32) + jnp.concatenate(attended, axis=0)).astype(BF)
    return feed_forward(middle, gain1, w_up, w_down)


def pick_table(table_ref, block, window, table):
    rows = table_ref[block].astype(F32)
    at = lax.broadcasted_iota(jnp.int32, rows.shape, 1)
    table[...] = jnp.sum(jnp.where(at == window, rows, 0.0), axis=1)


def put(ref, rows, value):
    for k in range(2):
        ref[k, rows, :] = value[:, k * 128 : (k + 1) * 128]


def widened(table, start, extra):
    part = table[:, start : start + 6 * OFFS]
    wide = jnp.concatenate([part, jnp.zeros((HEADS, 256 - 6 * OFFS), F32)], axis=1)
    return wide if extra is None else wide + extra


def bias_rolls(parts, sel):
    lane = lax.broadcasted_iota(jnp.int32, parts[0].shape, 1)
    fixed = [jnp.where(lane >= MASK_AT, p, 0.0) for p in parts]
    moving = [jnp.where(lane < MASK_AT, p, 0.0) for p in parts]
    for xp in range(WX):
        rows = [
            (pltpu.roll(m, 256 - xp, 1) if xp else m) + f for m, f in zip(moving, fixed)
        ]
        yield xp, dot(jnp.concatenate(rows, axis=1).astype(BF), sel)


def bias_regular(table, sel, lhs, out_ref):
    for zp in range(2):
        for zq in range(2):
            for yp in range(6):
                start = ((zp * 2 + zq) * 6 + yp) * 6 * OFFS
                rows = pl.ds(zp * 40 + yp, HEADS, stride=6)
                put(lhs.at[zq], rows, widened(table, start, None))
    parts = [jnp.concatenate([lhs[k, 0], lhs[k, 1]], axis=1) for k in range(2)]
    for xp, rows in bias_rolls(parts, sel):
        for zp in range(2):
            put(out_ref, pl.ds(2 * xp + zp, 36, stride=24), rows[zp * 40 : zp * 40 + 36])


def tables_kernel(
    table_ref, label_ref, sel_ref, bias2, keep1, send1, keep3, send3, table, lhs, half
):
    pick_table(table_ref, 2, level_at(0), table)
    lhs[...] = jnp.zeros_like(lhs)
    bias_regular(table, sel_ref[...], lhs, bias2)
    lane = lax.broadcasted_iota(jnp.int32, (8, 128), 1)
    level = lax.broadcasted_iota(jnp.int32, (8, 128), 0)
    first = MASK_AT - 128
    tags = jnp.zeros((8, 128), F32)
    for y in range(6):
        column = label_ref[y].astype(F32)[:, 0:1]
        tags = jnp.where(lane == first + y, column, tags)
    in_mask = (lane[0:1] >= first) & (lane[0:1] < first + 6)
    half[...] = jnp.zeros_like(half)
    for block, keep, send in ((1, keep1, send1), (3, keep3, send3)):
        for z in range(2):
            window = level_at(z - 1)
            pick_table(table_ref, block, window, table)
            keys = [
                jnp.sum(jnp.where(level == window * 2 + zq, tags, 0.0), axis=0, keepdims=True)
                for zq in range(2)
            ]
            zp = 1 - z
            for yp in range(6):
                mine = jnp.sum(
                    jnp.where(lane[0:1] == first + yp, keys[zp], 0.0), axis=1, keepdims=True
                )
                for zq in range(2):
                    mask = jnp.where(in_mask & (keys[zq] != mine), NEG, 0.0)
                    mask = jnp.concatenate([jnp.zeros((1, 128), F32), mask], axis=1)
                    start = ((zp * 2 + zq) * 6 + yp) * 6 * OFFS
                    rows = pl.ds(z * 24 + yp % 3, HEADS, stride=4)
                    put(half.at[yp // 3, zq], rows, widened(table, start, mask))
        keep[...] = half[0].astype(BF)
        send[...] = half[1].astype(BF).reshape(192, 128)


def bias_shifted_kernel(keep, far, near, sel_ref, pad_ref, out_ref):
    moved = choose(parity("lat"), near[-192:], far[-192:]).reshape(2, 2, 48, 128)
    parts = []
    for zq in range(2):
        rows = [jnp.concatenate([src[zq, 0], src[zq, 1]], axis=1) for src in (moved, keep)]
        parts.append(jnp.concatenate(rows, axis=0).astype(F32))
    for xp, rows in bias_rolls(parts, sel_ref[...]):
        rows = rows + pad_ref[...]
        x = (xp + 6) % 12
        xh, xl = x // 6, x % 6
        for yh in range(2):
            for z in range(2):
                base = ((z * 2 + yh) * 2 + xh) * 144 + xl
                at = (yh * 2 + z) * 24
                put(out_ref, pl.ds(base, 24, stride=6), rows[at : at + 24])


def parity(axis):
    return lax.rem(lax.axis_index(axis), 2)


def level_at(steps):
    return lax.rem(lax.axis_index("lev") + 4 + steps, 4)


def choose(odd, value_odd, value_even):
    return jnp.where(odd == 1, value_odd, value_even)


def halves(stream, gain, to_oct, odd, far, near):
    octs = dot(to_oct, layer_norm(stream.astype(F32), gain))
    west, east = pack(octs[: 4 * SLOT]), pack(octs[4 * SLOT :])
    far[...] = choose(odd, east, west)
    near[...] = choose(odd, west, east)


def first_kernel(
    x_hbm, gains_hbm, w_qkv_hbm, w_out_hbm, w_up_hbm, w_down_hbm, table_hbm, sel_hbm,
    oct_hbm, stream_out, far, near, table, lhs, bias, x, gains, w_qkv, w_out, w_up, w_down,
    rows, sel, to_oct, sems,
):
    pairs = (
        (table_hbm.at[pl.ds(0, 1)], rows), (sel_hbm, sel), (x_hbm, x), (gains_hbm, gains),
        (w_qkv_hbm.at[0], w_qkv), (w_out_hbm.at[0], w_out), (w_up_hbm.at[0], w_up),
        (w_down_hbm.at[0], w_down), (oct_hbm, to_oct),
    )
    copies = [pltpu.make_async_copy(a, b, sems.at[i]) for i, (a, b) in enumerate(pairs)]
    for copy in copies:
        copy.start()
    copies[0].wait()
    pick_table(rows, 0, level_at(0), table)
    lhs[...] = jnp.zeros_like(lhs)
    copies[1].wait()
    bias_regular(table, sel[...], lhs, bias)
    for copy in copies[2:]:
        copy.wait()
    stream = regular_block(
        x[...].reshape(T, D), gains[0, 0:1], gains[0, 1:2], w_qkv[...],
        w_out[...], w_up[...], w_down[...], bias,
    )
    stream_out[...] = pack(stream.astype(F32))
    halves(stream, gains[1, 0:1], to_oct[...], parity("lon"), far, near)


def join_kernel(other, near, joined):
    joined[:216] = other[...]
    joined[216:] = near[...]


def partner_kernel(other, gains, to_oct, far, near):
    halves(unpack(other[...]), gains[1, 0:1], to_oct[...], 1 - parity("lon"), far, near)


def third_kernel(third, gains, to_oct, far, near, beyond):
    halves(unpack(third[:216]), gains[1, 0:1], to_oct[...], 1 - parity("lon"), far, near)
    beyond[...] = third[216:]


def middle_kernel(
    own_in, other_in, third_in, lower, above, q, k_own, v_own, gains, w_qkv, w_out, w_up, w_down,
    bias1, bias2, to_oct, back, stream_out, beside_w, west, east, beside_e, k_ref, v_ref,
):
    odd = parity("lon")
    other, third = unpack(other_in[...]), unpack(third_in[:216])
    stream = [choose(odd, other, third), unpack(own_in[...]), choose(odd, third, other)]
    stream = shifted_block(
        jnp.concatenate(stream, axis=0).astype(BF), lower[...], above, q, k_own, v_own, gains[1, 1:2],
        w_qkv[1], w_out[1], w_up[1], w_down[1], bias1, back[...], k_ref, v_ref,
    )
    stream = regular_block(
        stream, gains[2, 0:1], gains[2, 1:2], w_qkv[2], w_out[2], w_up[2], w_down[2], bias2
    )
    stream_out[...] = stream[T : 2 * T]
    normed = layer_norm(stream.astype(F32), gains[3, 0:1])
    beside_w[...] = pack(dot(to_oct[4 * SLOT :], normed[:T]))
    octs = dot(to_oct[...], normed[T : 2 * T])
    west[...] = pack(octs[: 4 * SLOT])
    east[...] = pack(octs[4 * SLOT :])
    beside_e[...] = pack(dot(to_oct[: 4 * SLOT], normed[2 * T :]))


def last_kernel(
    stream_in, lower, above, q, k_own, v_own, gains, w_qkv, w_out, w_up, w_down, bias3, back, out,
    k_ref, v_ref,
):
    stream = shifted_block(
        stream_in[...], lower[...], above, q, k_own, v_own, gains[3, 1:2], w_qkv[3], w_out[3], w_up[3],
        w_down[3], bias3, back[...], k_ref, v_ref,
    )
    out[...] = stream.reshape(T // 2, 2, D)


def lat_pack_kernel(mirrored, *refs):
    *columns, table_rows, far, near = refs
    count = len(columns)
    parts = [unpack(ref[...]) for ref in columns]
    if mirrored:
        parts = [choose(parity("lon"), parts[count - 1 - i], parts[i]) for i in range(count)]
    packed = []
    for yh in range(2):
        rows = [
            part[(yh * 2 + z) * SLOT : (yh * 2 + z + 1) * SLOT] for z in range(2) for part in parts
        ]
        packed.append(pack(jnp.concatenate(rows, axis=0)))
    size = packed[0].shape[0]
    far[:size] = choose(parity("lat"), packed[1], packed[0])
    near[:size] = choose(parity("lat"), packed[0], packed[1])
    far[size:] = table_rows[...]
    near[size:] = table_rows[...]


def lev_pack_kernel(recv_far, own_far, own_near, recv_near, down, up):
    parts = [unpack(ref[:-192]) for ref in (recv_far, own_far, own_near, recv_near)]
    parts = [choose(parity("lat"), parts[3 - i], parts[i]) for i in range(4)]
    half = parts[0].shape[0] // 2
    for z, ref in ((0, down), (1, up)):
        ref[...] = pack(jnp.concatenate([part[z * half : (z + 1) * half] for part in parts], axis=0))


def call(kernel, outs, *args, scratch=(), flops=0, limit=20, place=pltpu.VMEM):
    specs = [pl.BlockSpec(memory_space=place)] * len(args)
    if place == pltpu.HBM:
        args = [pltpu.with_memory_space_constraint(arg, place) for arg in args]
    return pl.pallas_call(
        kernel,
        out_shape=outs,
        in_specs=specs,
        scratch_shapes=list(scratch),
        compiler_params=pltpu.CompilerParams(vmem_limit_bytes=int(limit * (1 << 20))),
        cost_estimate=pl.CostEstimate(flops=flops, bytes_accessed=1 << 20, transcendentals=0),
    )(*args)


def shape(*dims, dtype=BF):
    return jax.ShapeDtypeStruct(dims, dtype)


def move(value, axis, steps):
    count = lax.axis_size(axis)
    return lax.ppermute(value, axis, [(i, (i + steps) % count) for i in range(count)])


def swap(value, axis, steps):
    count = lax.axis_size(axis)
    pairs = [(i, (i + (-steps if i % 2 else steps)) % count) for i in range(count)]
    return lax.ppermute(value, axis, pairs)


def kv_scratch(pairs):
    return [pltpu.VMEM((4, pairs, PAIR, D), BF)] * 2


def halo(block, columns, keep, send, w_qkv, sel_shift, pad):
    across = len(columns)
    far, near = call(
        functools.partial(lat_pack_kernel, block == 1), [shape(across * 72 + 192, 128)] * 2,
        *columns, send, limit=4,
    )
    recv_far = swap(far, "lat", -1)
    recv_near = swap(near, "lat", 1)
    down, up = call(
        lev_pack_kernel, [shape(across * 144, 128)] * 2, recv_far, far, near, recv_near, limit=4
    )
    above = move(down, "lev", -1)
    below = move(up, "lev", 1)
    kv = shape(2, 4, across // 2, PAIR, D)
    q, k, v = call(
        functools.partial(own_keys_kernel, block),
        [shape((across - 2) * 4 * SLOT, D, dtype=F32), kv, kv],
        down, up, w_qkv, flops=1 << 30, limit=8,
    )
    bias = call(
        bias_shifted_kernel, shape(2, 8 * 144, 128, dtype=F32), keep, recv_far, recv_near,
        sel_shift, pad, flops=1 << 30, limit=8,
    )
    lower = call(
        functools.partial(lower_kernel, block), shape((across - 2) * 2 * SLOT, D), below, q, k, v,
        w_qkv, bias, scratch=kv_scratch(across // 2), flops=1 << 30, limit=8,
    )
    return lower, above, q, k, v, bias


def per_device(fields, w_qkv, w_out, w_up, w_down, gains, bias_table, labels):
    to_oct, back = [jnp.asarray(m, BF) for m in octant_maps()]
    sel_reg, sel_shift, pad = selectors()
    sel_reg, sel_shift = jnp.asarray(sel_reg, BF), jnp.asarray(sel_shift, BF)
    pad = jnp.asarray(pad, F32)
    tables = bias_table[:, :, 0].transpose(0, 2, 1, 3)
    tags = labels.transpose(1, 0, 2)
    weights = (gains, w_qkv, w_out, w_up, w_down.transpose(0, 2, 1))

    bias_shape = (2, HEADS * T, 128)
    table_scratch = [pltpu.VMEM((HEADS, POS), F32), pltpu.VMEM((2, 2, 80, 128), F32)]
    half = shape(144, 128)
    stream, far, near = call(
        first_kernel, [shape(216, 128), half, half], fields.transpose(1, 2, 0, 3).reshape(T // 2, 2, D), *weights,
        tables, sel_reg, to_oct,
        scratch=[
            *table_scratch, pltpu.VMEM(bias_shape, F32), pltpu.VMEM((T // 2, 2, D), BF),
            pltpu.VMEM((BLOCKS, 2, D), F32), pltpu.VMEM((D, 3 * D), BF), pltpu.VMEM((D, D), BF),
            pltpu.VMEM((D, FF), BF), pltpu.VMEM((D, FF), BF), pltpu.VMEM((1, HEADS, 4, POS), BF),
            pltpu.VMEM((512, 256), BF), pltpu.VMEM((8 * SLOT, T), BF), pltpu.SemaphoreType.DMA((9,)),
        ],
        flops=1 << 31, place=pltpu.HBM,
    )
    other = swap(stream, "lon", 1)
    outer_own = swap(far, "lon", -2)
    rows = [shape(2, 2, 48, 128), shape(192, 128)]
    bias2, keep1, send1, keep3, send3 = call(
        tables_kernel, [shape(*bias_shape, dtype=F32), *rows, *rows], tables, tags, sel_reg,
        scratch=[*table_scratch, pltpu.VMEM((2, 2, 2, 48, 128), F32)], flops=1 << 31,
    )
    other, send1, outer_own = lax.optimization_barrier((other, send1, outer_own))
    joined = call(join_kernel, shape(360, 128), other, near, limit=4)
    third = swap(joined, "lon", 2)
    other_far, other_near = call(
        partner_kernel, [half, half], other, gains, to_oct, flops=1 << 28, limit=4
    )
    third_far, third_near, beyond = call(
        third_kernel, [half, half, half], third, gains, to_oct, limit=4
    )
    columns = (beyond, third_near, third_far, far, near, other_near, other_far, outer_own)
    *ready, bias1 = halo(1, columns, keep1, send1, w_qkv, sel_shift, pad)
    stream, *columns = call(
        middle_kernel, [shape(T, D), half, half, half, half], stream, other, third, *ready,
        *weights, bias1, bias2, to_oct, back, scratch=kv_scratch(4), flops=1 << 31,
    )
    *ready, bias3 = halo(3, columns, keep3, send3, w_qkv, sel_shift, pad)
    stream = call(
        last_kernel, shape(T // 2, 2, D), stream, *ready, *weights, bias3, back,
        scratch=kv_scratch(2), flops=1 << 31,
    )
    return stream.reshape(6, 12, 2, D).transpose(2, 0, 1, 3)


def solution(mesh):
    in_specs = (
        P("lev", "lat", "lon", None),
        P(),
        P(),
        P(),
        P(),
        P(),
        P(None, None, "lat", None, None),
        P(None, "lat", "lon"),
    )
    return jax.shard_map(
        per_device,
        mesh=mesh,
        in_specs=in_specs,
        out_specs=P("lev", "lat", "lon", None),
        check_vma=False,
    )
```

```python
import functools

import jax
import jax.numpy as jnp
import numpy as np
from jax import lax
from jax.experimental import pallas as pl
from jax.experimental.pallas import tpu as pltpu
from jax.sharding import PartitionSpec as P

HEADS = 6
HD = 32
WZ = 2
WY = 6
WX = 12
BLOCKS = 4
D = 192
FF = 768
T = WZ * WY * WX
OFFS = 2 * WX - 1
POS = 3312
SLOT = 24
FILLED = 18
PAIR = 2 * SLOT
NEG = -1e30
MASK_AT = 192
BF = jnp.bfloat16
F32 = jnp.float32


def octant_maps():
    to_oct = np.zeros((8 * SLOT, T), np.float32)
    back = np.zeros((T, 8 * SLOT), np.float32)
    for z in range(2):
        for y in range(6):
            for x in range(12):
                yh, yl, xh, xl = y // 3, y % 3, x // 6, x % 6
                tok = (y * 12 + x) * 2 + z
                slot = yl * 6 + xl
                to_oct[((xh * 2 + yh) * 2 + z) * SLOT + slot, tok] = 1.0
                back[tok, ((z * 2 + yh) * 2 + xh) * SLOT + slot] = 1.0
    side = np.zeros((2, T // 2, T), np.float32)
    side_oct = np.zeros((4 * SLOT, T // 2), np.float32)
    for z in range(2):
        for y in range(6):
            for x in range(12):
                half = (y * 6 + x % 6) * 2 + z
                side[x // 6, half, (y * 12 + x) * 2 + z] = 1.0
                row = (y // 3 * 2 + z) * SLOT + y % 3 * 6 + x % 6
                side_oct[row, half] = 1.0
    return to_oct, back, side, side_oct


def selectors():
    regular = np.zeros((2, 256, 256), np.float32)
    for zq in range(2):
        for yq in range(6):
            for xq in range(12):
                regular[zq, yq * OFFS + 11 - xq, (yq * 12 + xq) * 2 + zq] = 1.0
    shifted = np.zeros((2, 256, 256), np.float32)
    pad = np.full((1, 256), NEG, np.float32)
    for zk in range(2):
        for yk in range(2):
            for xk in range(2):
                for yl in range(3):
                    for xl in range(6):
                        lane = ((zk * 2 + yk) * 2 + xk) * SLOT + yl * 6 + xl
                        yq, xq = yk * 3 + yl, xk * 6 + xl
                        shifted[zk, yq * OFFS + 11 - xq, lane] = 1.0
                        shifted[zk, MASK_AT + yq, lane] = 1.0
                        pad[0, lane] = 0.0
    return regular.reshape(512, 256), shifted.reshape(512, 256), pad


def dot(a, b):
    return jnp.dot(a, b, preferred_element_type=F32)


def dot_t(a, b):
    return lax.dot_general(a, b, (((1,), (1,)), ((), ())), preferred_element_type=F32)


def layer_norm(values, gain):
    center = values - jnp.mean(values, axis=-1, keepdims=True)
    spread = jnp.mean(center * center, axis=-1, keepdims=True)
    return (center * lax.rsqrt(spread + 1e-05) * gain).astype(BF)


def head_mask(rows):
    lane_head = lax.broadcasted_iota(jnp.int32, (rows, D), 1) // HD
    return [lane_head == h for h in range(HEADS)]


def spread_heads(q, masks):
    return jnp.concatenate([jnp.where(m, q, 0.0) for m in masks], axis=0).astype(BF)


def softmax_mix(scores, values, sizes):
    tops = [jnp.max(score, axis=-1, keepdims=True) for score in scores]
    terms = [jnp.exp(score - top) for score, top in zip(scores, tops)]
    totals = [1.0 / jnp.sum(term, axis=-1, keepdims=True) for term in terms]
    mixed = [dot(term.astype(BF), v) for term, v in zip(terms, values)]
    outs = []
    for part, total, rows in zip(mixed, totals, sizes):
        masks = head_mask(rows)
        part = part * total
        out = part[0:rows]
        for h in range(1, HEADS):
            out = jnp.where(masks[h], part[h * rows : (h + 1) * rows], out)
        outs.append(out)
    return outs


def feed_forward(middle, gain, w_up, w_down):
    normed = layer_norm(middle.astype(F32), gain)
    up = dot(normed, w_up)
    hidden = (0.5 * up * (1.0 + lax.erf(up * np.float32(0.5**0.5)))).astype(BF)
    return (middle.astype(F32) + dot_t(hidden, w_down)).astype(BF)


def regular_block(
    stream, queries, normed_q, gain0, gain1, w_qkv, w_out, w_up, w_down, biases, arrive=lambda: None
):
    if normed_q is None:
        normed_q = normed = layer_norm(stream.astype(F32), gain0)
    else:
        normed = layer_norm(stream.astype(F32), gain0)
        normed_q = normed_q(normed)
    q = dot(normed_q, w_qkv[:, :D]).astype(BF).astype(F32) * np.float32(HD**-0.5)
    kv = dot(normed, w_qkv[:, D:])
    scores, values, at = [], [], 0
    sizes = [bias.shape[1] // HEADS for bias in biases]
    for i, (bias, size) in enumerate(zip(biases, sizes)):
        k = kv[i * T : (i + 1) * T, :D].astype(BF)
        values.append(kv[i * T : (i + 1) * T, D:].astype(BF))
        added = jnp.concatenate([bias[0], bias[1, :, : T - 128]], axis=1)
        scores.append(dot_t(spread_heads(q[at : at + size], head_mask(size)), k) + added)
        at += size
    heads_out = jnp.concatenate(softmax_mix(scores, values, sizes), axis=0).astype(BF)
    arrive()
    attended = dot(heads_out, w_out[...]).astype(BF)
    middle = (queries.astype(F32) + attended.astype(F32)).astype(BF)
    return feed_forward(middle, gain1, w_up[...], w_down[...])


def pack(tokens):
    half = tokens.shape[0] // 2
    tails = jnp.concatenate([tokens[:half, 128:], tokens[half:, 128:]], axis=1)
    return jnp.concatenate([tokens[:, :128], tails], axis=0).astype(BF)


def unpack(packed, rows=None):
    values = packed.astype(F32)
    rows = rows or values.shape[0] // 3 * 2
    tails = values[rows : rows // 2 * 3]
    tails = jnp.concatenate([tails[:, :64], tails[:, 64:]], axis=0)
    return jnp.concatenate([values[:rows], tails], axis=1)


def keys_values(tokens, w_qkv, k_ref, v_ref):
    kv = dot(tokens.astype(BF), w_qkv[:, D:])
    k_ref[...] = kv[:, :D].astype(BF).reshape(k_ref.shape)
    v_ref[...] = kv[:, D:].astype(BF).reshape(v_ref.shape)


def own_keys_kernel(block, down, up, w_qkv, q_ref, k_ref, v_ref):
    across = k_ref.shape[2] * 2
    own = []
    for z, ref in enumerate((down, up)):
        tokens = ref[...].astype(F32)
        keys_values(tokens, w_qkv[block], k_ref.at[z], v_ref.at[z])
        for yh in range(2):
            row = ((1 + yh) * across + 1) * SLOT
            own.append(tokens[row : row + (across - 2) * SLOT])
    q = dot(jnp.concatenate(own, axis=0).astype(BF), w_qkv[block, :, :D]).astype(BF)
    q_ref[...] = q.astype(F32) * np.float32(HD**-0.5)


def level_windows(z, halo, q_ref, k_own, v_own, w_qkv, bias, k_ref, v_ref):
    pairs = k_own.shape[2]
    windows = pairs - 1
    keys_values(spaced(unpack(halo[...])), w_qkv, k_ref, v_ref)
    masks = head_mask(SLOT)
    sides = ((k_ref, v_ref), (k_own.at[z], v_own.at[z]))
    if z:
        sides = sides[::-1]
    names, scores, values = [], [], []
    for yh in range(2):
        for pair in range(pairs):
            ks, vs = [
                jnp.concatenate(
                    [side[i][2 * yh : 2 * yh + 2, pair].reshape(2 * PAIR, D) for side in sides],
                    axis=0,
                )
                for i in range(2)
            ]
            for half in (2 * pair - 1, 2 * pair):
                if half < 0 or half >= 2 * windows:
                    continue
                at = ((z * 2 + yh) * 2 * windows + half) * SLOT
                q = spread_heads(q_ref[at : at + SLOT], masks)
                at = ((z * 2 + yh) * 2 + half % 2) * 144
                added = jnp.concatenate([bias[0, at : at + 144], bias[1, at : at + 144, :64]], 1)
                names.append((half // 2, yh, half % 2))
                scores.append(dot_t(q, ks) + added)
                values.append(vs)
    outs = dict(zip(names, softmax_mix(scores, values, [SLOT] * len(scores))))
    return jnp.concatenate([outs[key] for key in sorted(outs)], axis=0).astype(BF)


def lower_kernel(block, below, q, k_own, v_own, w_qkv, bias, out, k_ref, v_ref):
    out[...] = level_windows(0, below, q, k_own, v_own, w_qkv[block], bias, k_ref, v_ref)


def shifted_block(
    stream, lower, above, q, k_own, v_own, gain1, w_qkv, w_out, w_up, w_down, bias, back,
    k_ref, v_ref,
):
    upper = level_windows(1, above, q, k_own, v_own, w_qkv, bias, k_ref, v_ref)
    rows = 4 * SLOT
    starts = range(0, upper.shape[0], rows)
    heads_out = [half[at : at + rows] for at in starts for half in (lower, upper)]
    projected = dot(jnp.concatenate(heads_out, axis=0), w_out).astype(BF)
    attended = [dot(back, projected[2 * at : 2 * at + 2 * rows]) for at in starts]
    middle = (stream.astype(F32) + jnp.concatenate(attended, axis=0)).astype(BF)
    return feed_forward(middle, gain1, w_up, w_down)


def pick_table(table_ref, block, window, table):
    rows = table_ref[block].astype(F32)
    at = lax.broadcasted_iota(jnp.int32, rows.shape, 1)
    table[...] = jnp.sum(jnp.where(at == window, rows, 0.0), axis=1)


def put(ref, rows, value):
    for k in range(2):
        ref[k, rows, :] = value[:, k * 128 : (k + 1) * 128]


def widened(table, start, extra):
    part = table[:, start : start + 6 * OFFS]
    wide = jnp.concatenate([part, jnp.zeros((HEADS, 256 - 6 * OFFS), F32)], axis=1)
    return wide if extra is None else wide + extra


def bias_rolls(parts, sel):
    lane = lax.broadcasted_iota(jnp.int32, parts[0].shape, 1)
    fixed = [jnp.where(lane >= MASK_AT, p, 0.0) for p in parts]
    moving = [jnp.where(lane < MASK_AT, p, 0.0) for p in parts]
    for xp in range(WX):
        rows = [
            (pltpu.roll(m, 256 - xp, 1) if xp else m) + f for m, f in zip(moving, fixed)
        ]
        yield xp, dot(jnp.concatenate(rows, axis=1).astype(BF), sel)


def bias_regular(table, sel, lhs, out_ref, sides=None):
    for zp in range(2):
        for zq in range(2):
            for yp in range(6):
                start = ((zp * 2 + zq) * 6 + yp) * 6 * OFFS
                rows = pl.ds(zp * 40 + yp, HEADS, stride=6)
                put(lhs.at[zq], rows, widened(table, start, None))
    parts = [jnp.concatenate([lhs[k, 0], lhs[k, 1]], axis=1) for k in range(2)]
    for xp, rows in bias_rolls(parts, sel):
        for zp in range(2):
            part = rows[zp * 40 : zp * 40 + 36]
            put(out_ref, pl.ds(2 * xp + zp, 36, stride=24), part)
            if sides is not None:
                put(sides.at[xp // 6], pl.ds(2 * (xp % 6) + zp, 36, stride=12), part)


def tables_kernel(
    table_ref, label_ref, sel_ref, bias2, sides2, keep1, send1, keep3, send3, table, lhs, half
):
    pick_table(table_ref, 2, level_at(0), table)
    lhs[...] = jnp.zeros_like(lhs)
    bias_regular(table, sel_ref[...], lhs, bias2, sides2)
    lane = lax.broadcasted_iota(jnp.int32, (8, 128), 1)
    level = lax.broadcasted_iota(jnp.int32, (8, 128), 0)
    first = MASK_AT - 128
    tags = jnp.zeros((8, 128), F32)
    for y in range(6):
        column = label_ref[y].astype(F32)[:, 0:1]
        tags = jnp.where(lane == first + y, column, tags)
    in_mask = (lane[0:1] >= first) & (lane[0:1] < first + 6)
    half[...] = jnp.zeros_like(half)
    for block, keep, send in ((1, keep1, send1), (3, keep3, send3)):
        for z in range(2):
            window = level_at(z - 1)
            pick_table(table_ref, block, window, table)
            keys = [
                jnp.sum(jnp.where(level == window * 2 + zq, tags, 0.0), axis=0, keepdims=True)
                for zq in range(2)
            ]
            zp = 1 - z
            for yp in range(6):
                mine = jnp.sum(
                    jnp.where(lane[0:1] == first + yp, keys[zp], 0.0), axis=1, keepdims=True
                )
                for zq in range(2):
                    mask = jnp.where(in_mask & (keys[zq] != mine), NEG, 0.0)
                    mask = jnp.concatenate([jnp.zeros((1, 128), F32), mask], axis=1)
                    start = ((zp * 2 + zq) * 6 + yp) * 6 * OFFS
                    rows = pl.ds(z * 24 + yp % 3, HEADS, stride=4)
                    put(half.at[yp // 3, zq], rows, widened(table, start, mask))
        keep[...] = half[0].astype(BF)
        send[...] = half[1].astype(BF).reshape(192, 128)


def bias_shifted_kernel(keep, far, near, sel_ref, pad_ref, out_ref):
    moved = choose(parity("lat"), near[-192:], far[-192:]).reshape(2, 2, 48, 128)
    parts = []
    for zq in range(2):
        rows = [jnp.concatenate([src[zq, 0], src[zq, 1]], axis=1) for src in (moved, keep)]
        parts.append(jnp.concatenate(rows, axis=0).astype(F32))
    for xp, rows in bias_rolls(parts, sel_ref[...]):
        rows = rows + pad_ref[...]
        x = (xp + 6) % 12
        xh, xl = x // 6, x % 6
        for yh in range(2):
            for z in range(2):
                base = ((z * 2 + yh) * 2 + xh) * 144 + xl
                at = (yh * 2 + z) * 24
                put(out_ref, pl.ds(base, 24, stride=6), rows[at : at + 24])


def parity(axis):
    return lax.rem(lax.axis_index(axis), 2)


def level_at(steps):
    return lax.rem(lax.axis_index("lev") + 4 + steps, 4)


def choose(odd, value_odd, value_even):
    return jnp.where(odd == 1, value_odd, value_even)


def halves(stream, gain, to_oct, odd, far, near):
    octs = dot(to_oct, layer_norm(stream.astype(F32), gain))
    west, east = pack(octs[: 4 * SLOT]), pack(octs[4 * SLOT :])
    far[...] = choose(odd, east, west)
    near[...] = choose(odd, west, east)


def first_kernel(
    x_hbm, gains_hbm, w_qkv_hbm, w_out_hbm, w_up_hbm, w_down_hbm, table_hbm, sel_hbm,
    oct_hbm, stream_out, far, near, table, lhs, bias, x, gains, w_qkv, w_out, w_up, w_down,
    rows, sel, to_oct, sems,
):
    pairs = (
        (table_hbm.at[pl.ds(0, 1)], rows), (sel_hbm, sel), (x_hbm, x), (gains_hbm, gains),
        (w_qkv_hbm.at[0], w_qkv), (w_out_hbm.at[0], w_out), (w_up_hbm.at[0], w_up),
        (w_down_hbm.at[0], w_down), (oct_hbm, to_oct),
    )
    copies = [pltpu.make_async_copy(a, b, sems.at[i]) for i, (a, b) in enumerate(pairs)]
    for copy in copies:
        copy.start()
    copies[0].wait()
    pick_table(rows, 0, level_at(0), table)
    lhs[...] = jnp.zeros_like(lhs)
    copies[1].wait()
    bias_regular(table, sel[...], lhs, bias)
    for copy in copies[2:5]:
        copy.wait()

    def arrive():
        for copy in copies[5:]:
            copy.wait()

    tokens = x[...].reshape(T, D)
    stream = regular_block(
        tokens, tokens, None, gains[0, 0:1], gains[0, 1:2], w_qkv[...],
        w_out, w_up, w_down, [bias], arrive,
    )
    packed = pack(stream.astype(F32))
    stream_out[...] = jnp.concatenate([packed, jnp.zeros((8, 128), BF)], axis=0)
    halves(stream, gains[1, 0:1], to_oct[...], parity("lon"), far, near)


def join_kernel(other, near, joined):
    joined[:144] = near[...]
    joined[144:] = other[...]


def partner_kernel(other, gains, to_oct, far, near):
    halves(unpack(other[...], T), gains[1, 0:1], to_oct[...], 1 - parity("lon"), far, near)


def middle_kernel(
    own_in, other_in, third_in, lower, above, q, k_own, v_own, gains, w_qkv, w_out, w_up, w_down,
    bias1, bias2, sides2, to_oct, back, side, side_oct, stream_out, beside_w, west, east, beside_e, k_ref, v_ref,
):
    odd = parity("lon")
    other, third = unpack(other_in[...], T), unpack(third_in[144:], T)
    stream = [choose(odd, other, third), unpack(own_in[...], T), choose(odd, third, other)]
    stream = shifted_block(
        jnp.concatenate(stream, axis=0).astype(BF), lower[...], above, q, k_own, v_own, gains[1, 1:2],
        w_qkv[1], w_out[1], w_up[1], w_down[1], bias1, back[...], k_ref, v_ref,
    )

    def worked(tokens):
        left, right = dot(side[1], tokens[:T]), dot(side[0], tokens[2 * T :])
        return jnp.concatenate([left, tokens[T : 2 * T].astype(F32), right], axis=0).astype(BF)

    stream = regular_block(
        stream, worked(stream), worked, gains[2, 0:1], gains[2, 1:2], w_qkv[2], w_out[2], w_up[2],
        w_down[2], [sides2.at[1], bias2, sides2.at[0]],
    )
    stream = stream.astype(F32)
    half = T // 2
    stream_out[...] = stream[half : half + T].astype(BF)
    normed = layer_norm(stream, gains[3, 0:1]).astype(F32)
    beside_w[...] = pack(dot(side_oct[...], normed[:half].astype(BF)))
    octs = dot(to_oct[...], normed[half : half + T].astype(BF))
    west[...] = pack(octs[: 4 * SLOT])
    east[...] = pack(octs[4 * SLOT :])
    beside_e[...] = pack(dot(side_oct[...], normed[half + T :].astype(BF)))


def last_kernel(
    stream_in, lower, above, q, k_own, v_own, gains, w_qkv, w_out, w_up, w_down, bias3, back, out,
    k_ref, v_ref,
):
    stream = shifted_block(
        stream_in[...], lower[...], above, q, k_own, v_own, gains[3, 1:2], w_qkv[3], w_out[3], w_up[3],
        w_down[3], bias3, back[...], k_ref, v_ref,
    )
    out[...] = stream.reshape(T // 2, 2, D)


def lat_pack_kernel(mirrored, *refs):
    *columns, table_rows, far, near = refs
    if mirrored:
        third, gains, to_oct, *columns = columns
    parts = [unpack(ref[...]) for ref in columns]
    if mirrored:
        octs = dot(to_oct[...], layer_norm(unpack(third[144:], T), gains[1, 0:1]))
        west, east = octs[: 4 * SLOT], octs[4 * SLOT :]
        odd = parity("lon")
        sides = [choose(odd, east, west), choose(odd, west, east)]
        parts = [unpack(third[:144]), *sides, *parts]
        count = len(parts)
        parts = [choose(parity("lon"), parts[count - 1 - i], parts[i]) for i in range(count)]
    packed = []
    for yh in range(2):
        rows = [
            part[(yh * 2 + z) * SLOT : (yh * 2 + z + 1) * SLOT] for z in range(2) for part in parts
        ]
        packed.append(pack(jnp.concatenate(rows, axis=0)))
    size = packed[0].shape[0]
    far[:size] = choose(parity("lat"), packed[1], packed[0])
    near[:size] = choose(parity("lat"), packed[0], packed[1])
    far[size:] = table_rows[...]
    near[size:] = table_rows[...]


def lev_pack_kernel(recv_far, own_far, own_near, recv_near, down, up, own_down, own_up):
    parts = [unpack(ref[:-192]) for ref in (recv_far, own_far, own_near, recv_near)]
    parts = [choose(parity("lat"), parts[3 - i], parts[i]) for i in range(4)]
    half = parts[0].shape[0] // 2
    for z, ref, own in ((0, down, own_down), (1, up, own_up)):
        tokens = jnp.concatenate([part[z * half : (z + 1) * half] for part in parts], axis=0)
        own[...] = tokens.astype(BF)
        starts = range(0, tokens.shape[0], SLOT)
        ref[...] = pack(jnp.concatenate([tokens[at : at + FILLED] for at in starts], axis=0))


def spaced(tokens):
    starts = range(0, tokens.shape[0], FILLED)
    gap = jnp.zeros((SLOT - FILLED, D), F32)
    rows = [part for at in starts for part in (tokens[at : at + FILLED], gap)]
    return jnp.concatenate(rows, axis=0)


def call(kernel, outs, *args, scratch=(), flops=0, limit=20, place=pltpu.VMEM):
    specs = [pl.BlockSpec(memory_space=place)] * len(args)
    if place == pltpu.HBM:
        args = [pltpu.with_memory_space_constraint(arg, place) for arg in args]
    return pl.pallas_call(
        kernel,
        out_shape=outs,
        in_specs=specs,
        scratch_shapes=list(scratch),
        compiler_params=pltpu.CompilerParams(vmem_limit_bytes=int(limit * (1 << 20))),
        cost_estimate=pl.CostEstimate(flops=flops, bytes_accessed=1 << 20, transcendentals=0),
    )(*args)


def shape(*dims, dtype=BF):
    return jax.ShapeDtypeStruct(dims, dtype)


def move(value, axis, steps):
    count = lax.axis_size(axis)
    return lax.ppermute(value, axis, [(i, (i + steps) % count) for i in range(count)])


def swap(value, axis, steps):
    count = lax.axis_size(axis)
    pairs = [(i, (i + (-steps if i % 2 else steps)) % count) for i in range(count)]
    return lax.ppermute(value, axis, pairs)


def kv_scratch(pairs):
    return [pltpu.VMEM((4, pairs, PAIR, D), BF)] * 2


def halo(block, columns, keep, send, w_qkv, sel_shift, pad):
    across = len(columns)
    far, near = call(
        functools.partial(lat_pack_kernel, block == 1), [shape(across * 72 + 192, 128)] * 2,
        *columns, send, limit=4,
    )
    recv_far = swap(far, "lat", -1)
    recv_near = swap(near, "lat", 1)
    down, up, own_down, own_up = call(
        lev_pack_kernel, [shape(across * 108, 128)] * 2 + [shape(across * 96, D)] * 2,
        recv_far, far, near, recv_near, limit=4,
    )
    above = move(down, "lev", -1)
    below = move(up, "lev", 1)
    kv = shape(2, 4, across // 2, PAIR, D)
    q, k, v = call(
        functools.partial(own_keys_kernel, block),
        [shape((across - 2) * 4 * SLOT, D, dtype=F32), kv, kv],
        own_down, own_up, w_qkv, flops=1 << 30, limit=8,
    )
    bias = call(
        bias_shifted_kernel, shape(2, 8 * 144, 128, dtype=F32), keep, recv_far, recv_near,
        sel_shift, pad, flops=1 << 30, limit=8,
    )
    lower = call(
        functools.partial(lower_kernel, block), shape((across - 2) * 2 * SLOT, D), below, q, k, v,
        w_qkv, bias, scratch=kv_scratch(across // 2), flops=1 << 30, limit=8,
    )
    return lower, above, q, k, v, bias


def per_device(fields, w_qkv, w_out, w_up, w_down, gains, bias_table, labels):
    to_oct, back, side, side_oct = [jnp.asarray(m, BF) for m in octant_maps()]
    sel_reg, sel_shift, pad = selectors()
    sel_reg, sel_shift = jnp.asarray(sel_reg, BF), jnp.asarray(sel_shift, BF)
    pad = jnp.asarray(pad, F32)
    tables = bias_table[:, :, 0].transpose(0, 2, 1, 3)
    tags = labels.transpose(1, 0, 2)
    weights = (gains, w_qkv, w_out, w_up, w_down.transpose(0, 2, 1))

    bias_shape = (2, HEADS * T, 128)
    table_scratch = [pltpu.VMEM((HEADS, POS), F32), pltpu.VMEM((2, 2, 80, 128), F32)]
    half = shape(144, 128)
    stream, far, near = call(
        first_kernel, [shape(224, 128), half, half], fields.transpose(1, 2, 0, 3).reshape(T // 2, 2, D), *weights,
        tables, sel_reg, to_oct,
        scratch=[
            *table_scratch, pltpu.VMEM(bias_shape, F32), pltpu.VMEM((T // 2, 2, D), BF),
            pltpu.VMEM((BLOCKS, 2, D), F32), pltpu.VMEM((D, 3 * D), BF), pltpu.VMEM((D, D), BF),
            pltpu.VMEM((D, FF), BF), pltpu.VMEM((D, FF), BF), pltpu.VMEM((1, HEADS, 4, POS), BF),
            pltpu.VMEM((512, 256), BF), pltpu.VMEM((8 * SLOT, T), BF), pltpu.SemaphoreType.DMA((9,)),
        ],
        flops=1 << 31, place=pltpu.HBM,
    )
    other = swap(stream, "lon", 1)
    outer_own = swap(far, "lon", -2)
    rows = [shape(2, 2, 48, 128), shape(192, 128)]
    bias2, sides2, keep1, send1, keep3, send3 = call(
        tables_kernel,
        [shape(*bias_shape, dtype=F32), shape(2, 2, HEADS * T // 2, 128, dtype=F32), *rows, *rows],
        tables, tags, sel_reg,
        scratch=[*table_scratch, pltpu.VMEM((2, 2, 2, 48, 128), F32)], flops=1 << 31,
    )
    other, send1, outer_own = lax.optimization_barrier((other, send1, outer_own))
    joined = call(join_kernel, shape(368, 128), other, near, limit=4)
    third = swap(joined, "lon", 2)
    other_far, other_near = call(
        partner_kernel, [half, half], other, gains, to_oct, flops=1 << 28, limit=4
    )
    columns = (third, gains, to_oct, far, near, other_near, other_far, outer_own)
    *ready, bias1 = halo(1, columns, keep1, send1, w_qkv, sel_shift, pad)
    stream, *columns = call(
        middle_kernel, [shape(T, D), half, half, half, half], stream, other, third, *ready,
        *weights, bias1, bias2, sides2, to_oct, back, side, side_oct, scratch=kv_scratch(4), flops=1 << 31,
    )
    *ready, bias3 = halo(3, columns, keep3, send3, w_qkv, sel_shift, pad)
    stream = call(
        last_kernel, shape(T // 2, 2, D), stream, *ready, *weights, bias3, back,
        scratch=kv_scratch(2), flops=1 << 31,
    )
    return stream.reshape(6, 12, 2, D).transpose(2, 0, 1, 3)


def solution(mesh):
    in_specs = (
        P("lev", "lat", "lon", None),
        P(),
        P(),
        P(),
        P(),
        P(),
        P(None, None, "lat", None, None),
        P(None, "lat", "lon"),
    )
    return jax.shard_map(
        per_device,
        mesh=mesh,
        in_specs=in_specs,
        out_specs=P("lev", "lat", "lon", None),
        check_vma=False,
    )
```

```python
import functools

import jax
import jax.numpy as jnp
import numpy as np
from jax import lax
from jax.experimental import pallas as pl
from jax.experimental.pallas import tpu as pltpu
from jax.sharding import PartitionSpec as P

HEADS = 6
HD = 32
WZ = 2
WY = 6
WX = 12
BLOCKS = 4
D = 192
FF = 768
T = WZ * WY * WX
OFFS = 2 * WX - 1
POS = 3312
SLOT = 24
FILLED = 18
PAIR = 2 * SLOT
NEG = -1e30
MASK_AT = 192
BF = jnp.bfloat16
F32 = jnp.float32


def octant_maps():
    to_oct = np.zeros((8 * SLOT, T), np.float32)
    back = np.zeros((T, 8 * SLOT), np.float32)
    for z in range(2):
        for y in range(6):
            for x in range(12):
                yh, yl, xh, xl = y // 3, y % 3, x // 6, x % 6
                tok = (y * 12 + x) * 2 + z
                slot = yl * 6 + xl
                to_oct[((xh * 2 + yh) * 2 + z) * SLOT + slot, tok] = 1.0
                back[tok, ((z * 2 + yh) * 2 + xh) * SLOT + slot] = 1.0
    side = np.zeros((2, T // 2, T), np.float32)
    side_oct = np.zeros((4 * SLOT, T // 2), np.float32)
    for z in range(2):
        for y in range(6):
            for x in range(12):
                half = (y * 6 + x % 6) * 2 + z
                side[x // 6, half, (y * 12 + x) * 2 + z] = 1.0
                row = (y // 3 * 2 + z) * SLOT + y % 3 * 6 + x % 6
                side_oct[row, half] = 1.0
    return to_oct, back, side, side_oct


def selectors():
    regular = np.zeros((2, 256, 256), np.float32)
    for zq in range(2):
        for yq in range(6):
            for xq in range(12):
                regular[zq, yq * OFFS + 11 - xq, (yq * 12 + xq) * 2 + zq] = 1.0
    shifted = np.zeros((2, 256, 256), np.float32)
    pad = np.full((1, 256), NEG, np.float32)
    for zk in range(2):
        for yk in range(2):
            for xk in range(2):
                for yl in range(3):
                    for xl in range(6):
                        lane = ((zk * 2 + yk) * 2 + xk) * SLOT + yl * 6 + xl
                        yq, xq = yk * 3 + yl, xk * 6 + xl
                        shifted[zk, yq * OFFS + 11 - xq, lane] = 1.0
                        shifted[zk, MASK_AT + yq, lane] = 1.0
                        pad[0, lane] = 0.0
    return regular.reshape(512, 256), shifted.reshape(512, 256), pad


def dot(a, b):
    return jnp.dot(a, b, preferred_element_type=F32)


def dot_t(a, b):
    return lax.dot_general(a, b, (((1,), (1,)), ((), ())), preferred_element_type=F32)


def layer_norm(values, gain):
    center = values - jnp.mean(values, axis=-1, keepdims=True)
    spread = jnp.mean(center * center, axis=-1, keepdims=True)
    return (center * lax.rsqrt(spread + 1e-05) * gain).astype(BF)


def head_mask(rows):
    lane_head = lax.broadcasted_iota(jnp.int32, (rows, D), 1) // HD
    return [lane_head == h for h in range(HEADS)]


def spread_heads(q, masks):
    return jnp.concatenate([jnp.where(m, q, 0.0) for m in masks], axis=0).astype(BF)


def softmax_mix(scores, values, sizes):
    tops = [jnp.max(score, axis=-1, keepdims=True) for score in scores]
    terms = [jnp.exp(score - top) for score, top in zip(scores, tops)]
    totals = [1.0 / jnp.sum(term, axis=-1, keepdims=True) for term in terms]
    mixed = [dot(term.astype(BF), v) for term, v in zip(terms, values)]
    outs = []
    for part, total, rows in zip(mixed, totals, sizes):
        masks = head_mask(rows)
        part = part * total
        out = part[0:rows]
        for h in range(1, HEADS):
            out = jnp.where(masks[h], part[h * rows : (h + 1) * rows], out)
        outs.append(out)
    return outs


def feed_forward(middle, gain, w_up, w_down):
    normed = layer_norm(middle.astype(F32), gain)
    up = dot(normed, w_up)
    hidden = (0.5 * up * (1.0 + lax.erf(up * np.float32(0.5**0.5)))).astype(BF)
    return (middle.astype(F32) + dot_t(hidden, w_down)).astype(BF)


def regular_block(
    stream, queries, normed_q, gain0, gain1, w_qkv, w_out, w_up, w_down, biases, arrive=lambda: None
):
    if normed_q is None:
        normed_q = normed = layer_norm(stream.astype(F32), gain0)
    else:
        normed = layer_norm(stream.astype(F32), gain0)
        normed_q = normed_q(normed)
    q = dot(normed_q, w_qkv[:, :D]).astype(BF).astype(F32) * np.float32(HD**-0.5)
    kv = dot(normed, w_qkv[:, D:])
    scores, values, at = [], [], 0
    sizes = [bias.shape[1] // HEADS for bias in biases]
    for i, (bias, size) in enumerate(zip(biases, sizes)):
        k = kv[i * T : (i + 1) * T, :D].astype(BF)
        values.append(kv[i * T : (i + 1) * T, D:].astype(BF))
        added = jnp.concatenate([bias[0], bias[1, :, : T - 128]], axis=1)
        scores.append(dot_t(spread_heads(q[at : at + size], head_mask(size)), k) + added)
        at += size
    heads_out = jnp.concatenate(softmax_mix(scores, values, sizes), axis=0).astype(BF)
    arrive()
    attended = dot(heads_out, w_out[...]).astype(BF)
    middle = (queries.astype(F32) + attended.astype(F32)).astype(BF)
    return feed_forward(middle, gain1, w_up[...], w_down[...])


def pack(tokens):
    half = tokens.shape[0] // 2
    tails = jnp.concatenate([tokens[:half, 128:], tokens[half:, 128:]], axis=1)
    return jnp.concatenate([tokens[:, :128], tails], axis=0).astype(BF)


def unpack(packed, rows=None):
    values = packed.astype(F32)
    rows = rows or values.shape[0] // 3 * 2
    tails = values[rows : rows // 2 * 3]
    tails = jnp.concatenate([tails[:, :64], tails[:, 64:]], axis=0)
    return jnp.concatenate([values[:rows], tails], axis=1)


def keys_values(tokens, w_qkv, k_ref, v_ref):
    kv = dot(tokens.astype(BF), w_qkv[:, D:])
    k_ref[...] = kv[:, :D].astype(BF).reshape(k_ref.shape)
    v_ref[...] = kv[:, D:].astype(BF).reshape(v_ref.shape)


def own_keys_kernel(block, down, up, w_qkv, q_ref, k_ref, v_ref):
    across = k_ref.shape[2] * 2
    own = []
    for z, ref in enumerate((down, up)):
        tokens = ref[...].astype(F32)
        keys_values(tokens, w_qkv[block], k_ref.at[z], v_ref.at[z])
        for yh in range(2):
            row = ((1 + yh) * across + 1) * SLOT
            own.append(tokens[row : row + (across - 2) * SLOT])
    q = dot(jnp.concatenate(own, axis=0).astype(BF), w_qkv[block, :, :D]).astype(BF)
    q_ref[...] = q.astype(F32) * np.float32(HD**-0.5)


def level_windows(z, halo, q_ref, k_own, v_own, w_qkv, bias, k_ref, v_ref):
    pairs = k_own.shape[2]
    windows = pairs - 1
    keys_values(spaced(unpack(halo[...])), w_qkv, k_ref, v_ref)
    masks = head_mask(SLOT)
    sides = ((k_ref, v_ref), (k_own.at[z], v_own.at[z]))
    if z:
        sides = sides[::-1]
    names, scores, values = [], [], []
    for yh in range(2):
        for pair in range(pairs):
            ks, vs = [
                jnp.concatenate(
                    [side[i][2 * yh : 2 * yh + 2, pair].reshape(2 * PAIR, D) for side in sides],
                    axis=0,
                )
                for i in range(2)
            ]
            for half in (2 * pair - 1, 2 * pair):
                if half < 0 or half >= 2 * windows:
                    continue
                at = ((z * 2 + yh) * 2 * windows + half) * SLOT
                q = spread_heads(q_ref[at : at + SLOT], masks)
                at = ((z * 2 + yh) * 2 + half % 2) * 144
                added = jnp.concatenate([bias[0, at : at + 144], bias[1, at : at + 144, :64]], 1)
                names.append((half // 2, yh, half % 2))
                scores.append(dot_t(q, ks) + added)
                values.append(vs)
    outs = dict(zip(names, softmax_mix(scores, values, [SLOT] * len(scores))))
    return jnp.concatenate([outs[key] for key in sorted(outs)], axis=0).astype(BF)


def lower_kernel(block, below, q, k_own, v_own, w_qkv, bias, out, k_ref, v_ref):
    out[...] = level_windows(0, below, q, k_own, v_own, w_qkv[block], bias, k_ref, v_ref)


def shifted_block(
    stream, lower, above, q, k_own, v_own, gain1, w_qkv, w_out, w_up, w_down, bias, back,
    k_ref, v_ref,
):
    upper = level_windows(1, above, q, k_own, v_own, w_qkv, bias, k_ref, v_ref)
    rows = 4 * SLOT
    starts = range(0, upper.shape[0], rows)
    heads_out = [half[at : at + rows] for at in starts for half in (lower, upper)]
    projected = dot(jnp.concatenate(heads_out, axis=0), w_out).astype(BF)
    attended = [dot(back, projected[2 * at : 2 * at + 2 * rows]) for at in starts]
    middle = (stream.astype(F32) + jnp.concatenate(attended, axis=0)).astype(BF)
    return feed_forward(middle, gain1, w_up, w_down)


def pick_table(table_ref, block, window, table):
    rows = table_ref[block].astype(F32)
    at = lax.broadcasted_iota(jnp.int32, rows.shape, 1)
    table[...] = jnp.sum(jnp.where(at == window, rows, 0.0), axis=1)


def put(ref, rows, value):
    for k in range(2):
        ref[k, rows, :] = value[:, k * 128 : (k + 1) * 128]


def widened(table, start, extra):
    part = table[:, start : start + 6 * OFFS]
    wide = jnp.concatenate([part, jnp.zeros((HEADS, 256 - 6 * OFFS), F32)], axis=1)
    return wide if extra is None else wide + extra


def bias_rolls(parts, sel):
    lane = lax.broadcasted_iota(jnp.int32, parts[0].shape, 1)
    fixed = [jnp.where(lane >= MASK_AT, p, 0.0) for p in parts]
    moving = [jnp.where(lane < MASK_AT, p, 0.0) for p in parts]
    for xp in range(WX):
        rows = [
            (pltpu.roll(m, 256 - xp, 1) if xp else m) + f for m, f in zip(moving, fixed)
        ]
        yield xp, dot(jnp.concatenate(rows, axis=1).astype(BF), sel)


def bias_regular(table, sel, lhs, out_ref, sides=None):
    for zp in range(2):
        for zq in range(2):
            for yp in range(6):
                start = ((zp * 2 + zq) * 6 + yp) * 6 * OFFS
                rows = pl.ds(zp * 40 + yp, HEADS, stride=6)
                put(lhs.at[zq], rows, widened(table, start, None))
    parts = [jnp.concatenate([lhs[k, 0], lhs[k, 1]], axis=1) for k in range(2)]
    for xp, rows in bias_rolls(parts, sel):
        for zp in range(2):
            part = rows[zp * 40 : zp * 40 + 36]
            put(out_ref, pl.ds(2 * xp + zp, 36, stride=24), part)
            if sides is not None:
                put(sides.at[xp // 6], pl.ds(2 * (xp % 6) + zp, 36, stride=12), part)


def tables_kernel(
    table_ref, label_ref, sel_ref, bias2, sides2, keep1, send1, keep3, send3, table, lhs, half
):
    pick_table(table_ref, 2, level_at(0), table)
    lhs[...] = jnp.zeros_like(lhs)
    bias_regular(table, sel_ref[...], lhs, bias2, sides2)
    lane = lax.broadcasted_iota(jnp.int32, (8, 128), 1)
    level = lax.broadcasted_iota(jnp.int32, (8, 128), 0)
    first = MASK_AT - 128
    tags = jnp.zeros((8, 128), F32)
    for y in range(6):
        column = label_ref[y].astype(F32)[:, 0:1]
        tags = jnp.where(lane == first + y, column, tags)
    in_mask = (lane[0:1] >= first) & (lane[0:1] < first + 6)
    half[...] = jnp.zeros_like(half)
    for block, keep, send in ((1, keep1, send1), (3, keep3, send3)):
        for z in range(2):
            window = level_at(z - 1)
            pick_table(table_ref, block, window, table)
            keys = [
                jnp.sum(jnp.where(level == window * 2 + zq, tags, 0.0), axis=0, keepdims=True)
                for zq in range(2)
            ]
            zp = 1 - z
            for yp in range(6):
                mine = jnp.sum(
                    jnp.where(lane[0:1] == first + yp, keys[zp], 0.0), axis=1, keepdims=True
                )
                for zq in range(2):
                    mask = jnp.where(in_mask & (keys[zq] != mine), NEG, 0.0)
                    mask = jnp.concatenate([jnp.zeros((1, 128), F32), mask], axis=1)
                    start = ((zp * 2 + zq) * 6 + yp) * 6 * OFFS
                    rows = pl.ds(z * 24 + yp % 3, HEADS, stride=4)
                    put(half.at[yp // 3, zq], rows, widened(table, start, mask))
        keep[...] = half[0].astype(BF)
        send[...] = half[1].astype(BF).reshape(192, 128)


def bias_shifted_kernel(keep, far, near, sel_ref, pad_ref, out_ref):
    moved = choose(parity("lat"), near[-192:], far[-192:]).reshape(2, 2, 48, 128)
    parts = []
    for zq in range(2):
        rows = [jnp.concatenate([src[zq, 0], src[zq, 1]], axis=1) for src in (moved, keep)]
        parts.append(jnp.concatenate(rows, axis=0).astype(F32))
    for xp, rows in bias_rolls(parts, sel_ref[...]):
        rows = rows + pad_ref[...]
        x = (xp + 6) % 12
        xh, xl = x // 6, x % 6
        for yh in range(2):
            for z in range(2):
                base = ((z * 2 + yh) * 2 + xh) * 144 + xl
                at = (yh * 2 + z) * 24
                put(out_ref, pl.ds(base, 24, stride=6), rows[at : at + 24])


def parity(axis):
    return lax.rem(lax.axis_index(axis), 2)


def level_at(steps):
    return lax.rem(lax.axis_index("lev") + 4 + steps, 4)


def choose(odd, value_odd, value_even):
    return jnp.where(odd == 1, value_odd, value_even)


def halves(stream, gain, to_oct, odd, far, near):
    octs = dot(to_oct, layer_norm(stream.astype(F32), gain))
    west, east = pack(octs[: 4 * SLOT]), pack(octs[4 * SLOT :])
    far[...] = choose(odd, east, west)
    near[...] = choose(odd, west, east)


def first_kernel(
    x_hbm, gains_hbm, w_qkv_hbm, w_out_hbm, w_up_hbm, w_down_hbm, table_hbm, sel_hbm,
    oct_hbm, stream_out, far, near, table, lhs, bias, x, gains, w_qkv, w_out, w_up, w_down,
    rows, sel, to_oct, sems,
):
    pairs = (
        (table_hbm.at[pl.ds(0, 1)], rows), (sel_hbm, sel), (x_hbm, x), (gains_hbm, gains),
        (w_qkv_hbm.at[0], w_qkv), (w_out_hbm.at[0], w_out), (w_up_hbm.at[0], w_up),
        (w_down_hbm.at[0], w_down), (oct_hbm, to_oct),
    )
    copies = [pltpu.make_async_copy(a, b, sems.at[i]) for i, (a, b) in enumerate(pairs)]
    for copy in copies:
        copy.start()
    copies[0].wait()
    pick_table(rows, 0, level_at(0), table)
    lhs[...] = jnp.zeros_like(lhs)
    copies[1].wait()
    bias_regular(table, sel[...], lhs, bias)
    for copy in copies[2:5]:
        copy.wait()

    def arrive():
        for copy in copies[5:]:
            copy.wait()

    tokens = x[...].reshape(T, D)
    stream = regular_block(
        tokens, tokens, None, gains[0, 0:1], gains[0, 1:2], w_qkv[...],
        w_out, w_up, w_down, [bias], arrive,
    )
    packed = pack(stream.astype(F32))
    stream_out[...] = jnp.concatenate([packed, jnp.zeros((8, 128), BF)], axis=0)
    halves(stream, gains[1, 0:1], to_oct[...], parity("lon"), far, near)


def join_kernel(other, near, joined):
    joined[:144] = near[...]
    joined[144:] = other[...]


def partner_kernel(other, gains, to_oct, far, near):
    halves(unpack(other[...], T), gains[1, 0:1], to_oct[...], 1 - parity("lon"), far, near)


def middle_kernel(
    own_in, other_in, third_in, lower, above, q, k_own, v_own, gains, w_qkv, w_out, w_up, w_down,
    bias1, bias2, sides2, to_oct, back, side, side_oct, stream_out, beside_w, west, east, beside_e, k_ref, v_ref,
):
    odd = parity("lon")
    other, third = unpack(other_in[...], T), unpack(third_in[144:], T)
    stream = [choose(odd, other, third), unpack(own_in[...], T), choose(odd, third, other)]
    stream = shifted_block(
        jnp.concatenate(stream, axis=0).astype(BF), lower[...], above, q, k_own, v_own, gains[1, 1:2],
        w_qkv[1], w_out[1], w_up[1], w_down[1], bias1, back[...], k_ref, v_ref,
    )

    def worked(tokens):
        left, right = dot(side[1], tokens[:T]), dot(side[0], tokens[2 * T :])
        return jnp.concatenate([left, tokens[T : 2 * T].astype(F32), right], axis=0).astype(BF)

    stream = regular_block(
        stream, worked(stream), worked, gains[2, 0:1], gains[2, 1:2], w_qkv[2], w_out[2], w_up[2],
        w_down[2], [sides2.at[1], bias2, sides2.at[0]],
    )
    stream = stream.astype(F32)
    half = T // 2
    stream_out[...] = stream[half : half + T].astype(BF)
    normed = layer_norm(stream, gains[3, 0:1]).astype(F32)
    beside_w[...] = pack(dot(side_oct[...], normed[:half].astype(BF)))
    octs = dot(to_oct[...], normed[half : half + T].astype(BF))
    west[...] = pack(octs[: 4 * SLOT])
    east[...] = pack(octs[4 * SLOT :])
    beside_e[...] = pack(dot(side_oct[...], normed[half + T :].astype(BF)))


def last_kernel(
    stream_in, lower, above, q, k_own, v_own, gains, w_qkv, w_out, w_up, w_down, bias3, back, out,
    k_ref, v_ref,
):
    stream = shifted_block(
        stream_in[...], lower[...], above, q, k_own, v_own, gains[3, 1:2], w_qkv[3], w_out[3], w_up[3],
        w_down[3], bias3, back[...], k_ref, v_ref,
    )
    out[...] = stream.reshape(T // 2, 2, D)


def lat_rows(across):
    return -(-across * 3 * FILLED // 16) * 16


def lat_pack_kernel(mirrored, *refs):
    *columns, table_rows, far, near = refs
    if mirrored:
        third, gains, to_oct, *columns = columns
    parts = [unpack(ref[...]) for ref in columns]
    if mirrored:
        octs = dot(to_oct[...], layer_norm(unpack(third[144:], T), gains[1, 0:1]))
        west, east = octs[: 4 * SLOT], octs[4 * SLOT :]
        odd = parity("lon")
        sides = [choose(odd, east, west), choose(odd, west, east)]
        parts = [unpack(third[:144]), *sides, *parts]
        count = len(parts)
        parts = [choose(parity("lon"), parts[count - 1 - i], parts[i]) for i in range(count)]
    packed = []
    for yh in range(2):
        rows = [
            part[(yh * 2 + z) * SLOT : (yh * 2 + z) * SLOT + FILLED]
            for z in range(2)
            for part in parts
        ]
        packed.append(pack(jnp.concatenate(rows, axis=0)))
    size = lat_rows(len(parts))
    gap = size - packed[0].shape[0]
    if gap:
        packed = [jnp.concatenate([p, jnp.zeros((gap, 128), BF)], axis=0) for p in packed]
    far[:size] = choose(parity("lat"), packed[1], packed[0])
    near[:size] = choose(parity("lat"), packed[0], packed[1])
    far[size:] = table_rows[...]
    near[size:] = table_rows[...]


def lev_pack_kernel(
    across, recv_far, own_far, own_near, recv_near, down, up, own_down, own_up
):
    refs = (recv_far, own_far, own_near, recv_near)
    parts = [unpack(ref[: lat_rows(across)], across * 2 * FILLED) for ref in refs]
    parts = [choose(parity("lat"), parts[3 - i], parts[i]) for i in range(4)]
    half = across * FILLED
    for z, ref, own in ((0, down, own_down), (1, up, own_up)):
        tokens = jnp.concatenate([part[z * half : (z + 1) * half] for part in parts], axis=0)
        own[...] = spaced(tokens).astype(BF)
        ref[...] = pack(tokens)


def spaced(tokens):
    starts = range(0, tokens.shape[0], FILLED)
    gap = jnp.zeros((SLOT - FILLED, D), F32)
    rows = [part for at in starts for part in (tokens[at : at + FILLED], gap)]
    return jnp.concatenate(rows, axis=0)


def call(kernel, outs, *args, scratch=(), flops=0, limit=20, place=pltpu.VMEM):
    specs = [pl.BlockSpec(memory_space=place)] * len(args)
    if place == pltpu.HBM:
        args = [pltpu.with_memory_space_constraint(arg, place) for arg in args]
    return pl.pallas_call(
        kernel,
        out_shape=outs,
        in_specs=specs,
        scratch_shapes=list(scratch),
        compiler_params=pltpu.CompilerParams(vmem_limit_bytes=int(limit * (1 << 20))),
        cost_estimate=pl.CostEstimate(flops=flops, bytes_accessed=1 << 20, transcendentals=0),
    )(*args)


def shape(*dims, dtype=BF):
    return jax.ShapeDtypeStruct(dims, dtype)


def move(value, axis, steps):
    count = lax.axis_size(axis)
    return lax.ppermute(value, axis, [(i, (i + steps) % count) for i in range(count)])


def swap(value, axis, steps):
    count = lax.axis_size(axis)
    pairs = [(i, (i + (-steps if i % 2 else steps)) % count) for i in range(count)]
    return lax.ppermute(value, axis, pairs)


def kv_scratch(pairs):
    return [pltpu.VMEM((4, pairs, PAIR, D), BF)] * 2


def halo(block, columns, keep, send, w_qkv, sel_shift, pad):
    across = len(columns)
    far, near = call(
        functools.partial(lat_pack_kernel, block == 1), [shape(lat_rows(across) + 192, 128)] * 2,
        *columns, send, limit=4,
    )
    recv_far = swap(far, "lat", -1)
    recv_near = swap(near, "lat", 1)
    down, up, own_down, own_up = call(
        functools.partial(lev_pack_kernel, across),
        [shape(across * 108, 128)] * 2 + [shape(across * 96, D)] * 2,
        recv_far, far, near, recv_near, limit=4,
    )
    above = move(down, "lev", -1)
    below = move(up, "lev", 1)
    kv = shape(2, 4, across // 2, PAIR, D)
    q, k, v = call(
        functools.partial(own_keys_kernel, block),
        [shape((across - 2) * 4 * SLOT, D, dtype=F32), kv, kv],
        own_down, own_up, w_qkv, flops=1 << 30, limit=8,
    )
    bias = call(
        bias_shifted_kernel, shape(2, 8 * 144, 128, dtype=F32), keep, recv_far, recv_near,
        sel_shift, pad, flops=1 << 30, limit=8,
    )
    lower = call(
        functools.partial(lower_kernel, block), shape((across - 2) * 2 * SLOT, D), below, q, k, v,
        w_qkv, bias, scratch=kv_scratch(across // 2), flops=1 << 30, limit=8,
    )
    return lower, above, q, k, v, bias


def per_device(fields, w_qkv, w_out, w_up, w_down, gains, bias_table, labels):
    to_oct, back, side, side_oct = [jnp.asarray(m, BF) for m in octant_maps()]
    sel_reg, sel_shift, pad = selectors()
    sel_reg, sel_shift = jnp.asarray(sel_reg, BF), jnp.asarray(sel_shift, BF)
    pad = jnp.asarray(pad, F32)
    tables = bias_table[:, :, 0].transpose(0, 2, 1, 3)
    tags = labels.transpose(1, 0, 2)
    weights = (gains, w_qkv, w_out, w_up, w_down.transpose(0, 2, 1))

    bias_shape = (2, HEADS * T, 128)
    table_scratch = [pltpu.VMEM((HEADS, POS), F32), pltpu.VMEM((2, 2, 80, 128), F32)]
    half = shape(144, 128)
    stream, far, near = call(
        first_kernel, [shape(224, 128), half, half], fields.transpose(1, 2, 0, 3).reshape(T // 2, 2, D), *weights,
        tables, sel_reg, to_oct,
        scratch=[
            *table_scratch, pltpu.VMEM(bias_shape, F32), pltpu.VMEM((T // 2, 2, D), BF),
            pltpu.VMEM((BLOCKS, 2, D), F32), pltpu.VMEM((D, 3 * D), BF), pltpu.VMEM((D, D), BF),
            pltpu.VMEM((D, FF), BF), pltpu.VMEM((D, FF), BF), pltpu.VMEM((1, HEADS, 4, POS), BF),
            pltpu.VMEM((512, 256), BF), pltpu.VMEM((8 * SLOT, T), BF), pltpu.SemaphoreType.DMA((9,)),
        ],
        flops=1 << 31, place=pltpu.HBM,
    )
    other = swap(stream, "lon", 1)
    outer_own = swap(far, "lon", -2)
    rows = [shape(2, 2, 48, 128), shape(192, 128)]
    bias2, sides2, keep1, send1, keep3, send3 = call(
        tables_kernel,
        [shape(*bias_shape, dtype=F32), shape(2, 2, HEADS * T // 2, 128, dtype=F32), *rows, *rows],
        tables, tags, sel_reg,
        scratch=[*table_scratch, pltpu.VMEM((2, 2, 2, 48, 128), F32)], flops=1 << 31,
    )
    other, send1, outer_own = lax.optimization_barrier((other, send1, outer_own))
    joined = call(join_kernel, shape(368, 128), other, near, limit=4)
    third = swap(joined, "lon", 2)
    other_far, other_near = call(
        partner_kernel, [half, half], other, gains, to_oct, flops=1 << 28, limit=4
    )
    columns = (third, gains, to_oct, far, near, other_near, other_far, outer_own)
    *ready, bias1 = halo(1, columns, keep1, send1, w_qkv, sel_shift, pad)
    stream, *columns = call(
        middle_kernel, [shape(T, D), half, half, half, half], stream, other, third, *ready,
        *weights, bias1, bias2, sides2, to_oct, back, side, side_oct, scratch=kv_scratch(4), flops=1 << 31,
    )
    *ready, bias3 = halo(3, columns, keep3, send3, w_qkv, sel_shift, pad)
    stream = call(
        last_kernel, shape(T // 2, 2, D), stream, *ready, *weights, bias3, back,
        scratch=kv_scratch(2), flops=1 << 31,
    )
    return stream.reshape(6, 12, 2, D).transpose(2, 0, 1, 3)


def solution(mesh):
    in_specs = (
        P("lev", "lat", "lon", None),
        P(),
        P(),
        P(),
        P(),
        P(),
        P(None, None, "lat", None, None),
        P(None, "lat", "lon"),
    )
    return jax.shard_map(
        per_device,
        mesh=mesh,
        in_specs=in_specs,
        out_specs=P("lev", "lat", "lon", None),
        check_vma=False,
    )
```

```python
import functools

import jax
import jax.numpy as jnp
import numpy as np
from jax import lax
from jax.experimental import pallas as pl
from jax.experimental.pallas import tpu as pltpu
from jax.sharding import PartitionSpec as P

HEADS = 6
HD = 32
WZ = 2
WY = 6
WX = 12
BLOCKS = 4
D = 192
FF = 768
T = WZ * WY * WX
OFFS = 2 * WX - 1
POS = 3312
SLOT = 24
FILLED = 18
PAIR = 2 * SLOT
NEG = -1e30
MASK_AT = 192
BF = jnp.bfloat16
F32 = jnp.float32


def octant_maps():
    to_oct = np.zeros((8 * SLOT, T), np.float32)
    back = np.zeros((T, 8 * SLOT), np.float32)
    for z in range(2):
        for y in range(6):
            for x in range(12):
                yh, yl, xh, xl = y // 3, y % 3, x // 6, x % 6
                tok = (y * 12 + x) * 2 + z
                slot = yl * 6 + xl
                to_oct[((xh * 2 + yh) * 2 + z) * SLOT + slot, tok] = 1.0
                back[tok, ((z * 2 + yh) * 2 + xh) * SLOT + slot] = 1.0
    side = np.zeros((2, T // 2, T), np.float32)
    side_oct = np.zeros((4 * SLOT, T // 2), np.float32)
    for z in range(2):
        for y in range(6):
            for x in range(12):
                half = (y * 6 + x % 6) * 2 + z
                side[x // 6, half, (y * 12 + x) * 2 + z] = 1.0
                row = (y // 3 * 2 + z) * SLOT + y % 3 * 6 + x % 6
                side_oct[row, half] = 1.0
    return to_oct, back, side, side_oct


def selectors():
    regular = np.zeros((2, 256, 256), np.float32)
    for zq in range(2):
        for yq in range(6):
            for xq in range(12):
                regular[zq, yq * OFFS + 11 - xq, (yq * 12 + xq) * 2 + zq] = 1.0
    shifted = np.zeros((2, 256, 256), np.float32)
    pad = np.full((1, 256), NEG, np.float32)
    for zk in range(2):
        for yk in range(2):
            for xk in range(2):
                for yl in range(3):
                    for xl in range(6):
                        lane = ((zk * 2 + yk) * 2 + xk) * SLOT + yl * 6 + xl
                        yq, xq = yk * 3 + yl, xk * 6 + xl
                        shifted[zk, yq * OFFS + 11 - xq, lane] = 1.0
                        shifted[zk, MASK_AT + yq, lane] = 1.0
                        pad[0, lane] = 0.0
    return regular.reshape(512, 256), shifted.reshape(512, 256), pad


def dot(a, b):
    return jnp.dot(a, b, preferred_element_type=F32)


def dot_t(a, b):
    return lax.dot_general(a, b, (((1,), (1,)), ((), ())), preferred_element_type=F32)


def layer_norm(values, gain):
    center = values - jnp.mean(values, axis=-1, keepdims=True)
    spread = jnp.mean(center * center, axis=-1, keepdims=True)
    return (center * lax.rsqrt(spread + 1e-05) * gain).astype(BF)


def head_mask(rows):
    lane_head = lax.broadcasted_iota(jnp.int32, (rows, D), 1) // HD
    return [lane_head == h for h in range(HEADS)]


def spread_heads(q, masks):
    return jnp.concatenate([jnp.where(m, q, 0.0) for m in masks], axis=0).astype(BF)


def softmax_mix(scores, values, sizes):
    tops = [jnp.max(score, axis=-1, keepdims=True) for score in scores]
    terms = [jnp.exp(score - top) for score, top in zip(scores, tops)]
    totals = [1.0 / jnp.sum(term, axis=-1, keepdims=True) for term in terms]
    mixed = [dot(term.astype(BF), v) for term, v in zip(terms, values)]
    outs = []
    for part, total, rows in zip(mixed, totals, sizes):
        masks = head_mask(rows)
        part = part * total
        out = part[0:rows]
        for h in range(1, HEADS):
            out = jnp.where(masks[h], part[h * rows : (h + 1) * rows], out)
        outs.append(out)
    return outs


def feed_forward(middle, gain, w_up, w_down):
    normed = layer_norm(middle.astype(F32), gain)
    up = dot(normed, w_up)
    hidden = (0.5 * up * (1.0 + lax.erf(up * np.float32(0.5**0.5)))).astype(BF)
    return (middle.astype(F32) + dot_t(hidden, w_down)).astype(BF)


def regular_block(
    stream, queries, normed_q, gain0, gain1, w_qkv, w_out, w_up, w_down, biases, arrive=lambda: None
):
    if normed_q is None:
        normed_q = normed = layer_norm(stream.astype(F32), gain0)
    else:
        normed = layer_norm(stream.astype(F32), gain0)
        normed_q = normed_q(normed)
    q = dot(normed_q, w_qkv[:, :D]).astype(BF).astype(F32) * np.float32(HD**-0.5)
    kv = dot(normed, w_qkv[:, D:])
    scores, values, at = [], [], 0
    sizes = [bias.shape[1] // HEADS for bias in biases]
    for i, (bias, size) in enumerate(zip(biases, sizes)):
        k = kv[i * T : (i + 1) * T, :D].astype(BF)
        values.append(kv[i * T : (i + 1) * T, D:].astype(BF))
        added = jnp.concatenate([bias[0], bias[1, :, : T - 128]], axis=1)
        scores.append(dot_t(spread_heads(q[at : at + size], head_mask(size)), k) + added)
        at += size
    heads_out = jnp.concatenate(softmax_mix(scores, values, sizes), axis=0).astype(BF)
    arrive()
    attended = dot(heads_out, w_out[...]).astype(BF)
    middle = (queries.astype(F32) + attended.astype(F32)).astype(BF)
    return feed_forward(middle, gain1, w_up[...], w_down[...])


def pack(tokens):
    half = tokens.shape[0] // 2
    tails = jnp.concatenate([tokens[:half, 128:], tokens[half:, 128:]], axis=1)
    return jnp.concatenate([tokens[:, :128], tails], axis=0).astype(BF)


def unpack(packed, rows=None):
    values = packed.astype(F32)
    rows = rows or values.shape[0] // 3 * 2
    tails = values[rows : rows // 2 * 3]
    tails = jnp.concatenate([tails[:, :64], tails[:, 64:]], axis=0)
    return jnp.concatenate([values[:rows], tails], axis=1)


def keys_values(tokens, w_qkv, k_ref, v_ref):
    kv = dot(tokens.astype(BF), w_qkv[:, D:])
    k_ref[...] = kv[:, :D].astype(BF).reshape(k_ref.shape)
    v_ref[...] = kv[:, D:].astype(BF).reshape(v_ref.shape)


def own_keys_kernel(block, down, up, w_qkv, q_ref, k_ref, v_ref):
    across = k_ref.shape[2] * 2
    own = []
    for z, ref in enumerate((down, up)):
        tokens = ref[...].astype(F32)
        keys_values(tokens, w_qkv[block], k_ref.at[z], v_ref.at[z])
        for yh in range(2):
            row = ((1 + yh) * across + 1) * SLOT
            own.append(tokens[row : row + (across - 2) * SLOT])
    q = dot(jnp.concatenate(own, axis=0).astype(BF), w_qkv[block, :, :D]).astype(BF)
    q = q.astype(F32) * np.float32(HD**-0.5)
    masks = head_mask(SLOT)
    for at in range(0, q.shape[0], SLOT):
        q_ref[at * HEADS : (at + SLOT) * HEADS] = spread_heads(q[at : at + SLOT], masks)


def level_windows(z, halo, q_ref, k_own, v_own, w_qkv, bias, k_ref, v_ref):
    pairs = k_own.shape[2]
    windows = pairs - 1
    keys_values(spaced(unpack(halo[...])), w_qkv, k_ref, v_ref)
    sides = ((k_ref, v_ref), (k_own.at[z], v_own.at[z]))
    if z:
        sides = sides[::-1]
    names, scores, values = [], [], []
    for yh in range(2):
        for pair in range(pairs):
            ks, vs = [
                jnp.concatenate(
                    [side[i][2 * yh : 2 * yh + 2, pair].reshape(2 * PAIR, D) for side in sides],
                    axis=0,
                )
                for i in range(2)
            ]
            for half in (2 * pair - 1, 2 * pair):
                if half < 0 or half >= 2 * windows:
                    continue
                at = ((z * 2 + yh) * 2 * windows + half) * SLOT
                q = q_ref[at * HEADS : (at + SLOT) * HEADS]
                at = ((z * 2 + yh) * 2 + half % 2) * 144
                added = jnp.concatenate([bias[0, at : at + 144], bias[1, at : at + 144, :64]], 1)
                names.append((half // 2, yh, half % 2))
                scores.append(dot_t(q, ks) + added)
                values.append(vs)
    outs = dict(zip(names, softmax_mix(scores, values, [SLOT] * len(scores))))
    return jnp.concatenate([outs[key] for key in sorted(outs)], axis=0).astype(BF)


def lower_kernel(block, below, q, k_own, v_own, w_qkv, bias, out, k_ref, v_ref):
    out[...] = level_windows(0, below, q, k_own, v_own, w_qkv[block], bias, k_ref, v_ref)


def shifted_block(
    stream, lower, above, q, k_own, v_own, gain1, w_qkv, w_out, w_up, w_down, bias, back,
    k_ref, v_ref,
):
    upper = level_windows(1, above, q, k_own, v_own, w_qkv, bias, k_ref, v_ref)
    rows = 4 * SLOT
    starts = range(0, upper.shape[0], rows)
    heads_out = [half[at : at + rows] for at in starts for half in (lower, upper)]
    projected = dot(jnp.concatenate(heads_out, axis=0), w_out).astype(BF)
    attended = [dot(back, projected[2 * at : 2 * at + 2 * rows]) for at in starts]
    middle = (stream.astype(F32) + jnp.concatenate(attended, axis=0)).astype(BF)
    return feed_forward(middle, gain1, w_up, w_down)


def pick_table(table_ref, block, window, table):
    rows = table_ref[block].astype(F32)
    at = lax.broadcasted_iota(jnp.int32, rows.shape, 1)
    table[...] = jnp.sum(jnp.where(at == window, rows, 0.0), axis=1)


def put(ref, rows, value):
    for k in range(2):
        ref[k, rows, :] = value[:, k * 128 : (k + 1) * 128]


def widened(table, start, extra):
    part = table[:, start : start + 6 * OFFS]
    wide = jnp.concatenate([part, jnp.zeros((HEADS, 256 - 6 * OFFS), F32)], axis=1)
    return wide if extra is None else wide + extra


def bias_rolls(parts, sel):
    lane = lax.broadcasted_iota(jnp.int32, parts[0].shape, 1)
    fixed = [jnp.where(lane >= MASK_AT, p, 0.0) for p in parts]
    moving = [jnp.where(lane < MASK_AT, p, 0.0) for p in parts]
    for xp in range(WX):
        rows = [
            (pltpu.roll(m, 256 - xp, 1) if xp else m) + f for m, f in zip(moving, fixed)
        ]
        yield xp, dot(jnp.concatenate(rows, axis=1).astype(BF), sel)


def bias_regular(table, sel, lhs, out_ref, sides=None):
    for zp in range(2):
        for zq in range(2):
            for yp in range(6):
                start = ((zp * 2 + zq) * 6 + yp) * 6 * OFFS
                rows = pl.ds(zp * 40 + yp, HEADS, stride=6)
                put(lhs.at[zq], rows, widened(table, start, None))
    parts = [jnp.concatenate([lhs[k, 0], lhs[k, 1]], axis=1) for k in range(2)]
    for xp, rows in bias_rolls(parts, sel):
        for zp in range(2):
            part = rows[zp * 40 : zp * 40 + 36]
            put(out_ref, pl.ds(2 * xp + zp, 36, stride=24), part)
            if sides is not None:
                put(sides.at[xp // 6], pl.ds(2 * (xp % 6) + zp, 36, stride=12), part)


def tables_kernel(
    table_ref, label_ref, sel_ref, bias2, sides2, keep1, send1, keep3, send3, table, lhs, half
):
    pick_table(table_ref, 2, level_at(0), table)
    lhs[...] = jnp.zeros_like(lhs)
    bias_regular(table, sel_ref[...], lhs, bias2, sides2)
    lane = lax.broadcasted_iota(jnp.int32, (8, 128), 1)
    level = lax.broadcasted_iota(jnp.int32, (8, 128), 0)
    first = MASK_AT - 128
    tags = jnp.zeros((8, 128), F32)
    for y in range(6):
        column = label_ref[y].astype(F32)[:, 0:1]
        tags = jnp.where(lane == first + y, column, tags)
    in_mask = (lane[0:1] >= first) & (lane[0:1] < first + 6)
    half[...] = jnp.zeros_like(half)
    for block, keep, send in ((1, keep1, send1), (3, keep3, send3)):
        for z in range(2):
            window = level_at(z - 1)
            pick_table(table_ref, block, window, table)
            keys = [
                jnp.sum(jnp.where(level == window * 2 + zq, tags, 0.0), axis=0, keepdims=True)
                for zq in range(2)
            ]
            zp = 1 - z
            for yp in range(6):
                mine = jnp.sum(
                    jnp.where(lane[0:1] == first + yp, keys[zp], 0.0), axis=1, keepdims=True
                )
                for zq in range(2):
                    mask = jnp.where(in_mask & (keys[zq] != mine), NEG, 0.0)
                    mask = jnp.concatenate([jnp.zeros((1, 128), F32), mask], axis=1)
                    start = ((zp * 2 + zq) * 6 + yp) * 6 * OFFS
                    rows = pl.ds(z * 24 + yp % 3, HEADS, stride=4)
                    put(half.at[yp // 3, zq], rows, widened(table, start, mask))
        keep[...] = half[0].astype(BF)
        send[...] = half[1].astype(BF).reshape(192, 128)


def bias_shifted_kernel(keep, far, near, sel_ref, pad_ref, out_ref):
    moved = choose(parity("lat"), near[-192:], far[-192:]).reshape(2, 2, 48, 128)
    parts = []
    for zq in range(2):
        rows = [jnp.concatenate([src[zq, 0], src[zq, 1]], axis=1) for src in (moved, keep)]
        parts.append(jnp.concatenate(rows, axis=0).astype(F32))
    for xp, rows in bias_rolls(parts, sel_ref[...]):
        rows = rows + pad_ref[...]
        x = (xp + 6) % 12
        xh, xl = x // 6, x % 6
        for yh in range(2):
            for z in range(2):
                base = ((z * 2 + yh) * 2 + xh) * 144 + xl
                at = (yh * 2 + z) * 24
                put(out_ref, pl.ds(base, 24, stride=6), rows[at : at + 24])


def parity(axis):
    return lax.rem(lax.axis_index(axis), 2)


def level_at(steps):
    return lax.rem(lax.axis_index("lev") + 4 + steps, 4)


def choose(odd, value_odd, value_even):
    return jnp.where(odd == 1, value_odd, value_even)


def halves(stream, gain, to_oct, odd, far, near):
    octs = dot(to_oct, layer_norm(stream.astype(F32), gain))
    west, east = pack(octs[: 4 * SLOT]), pack(octs[4 * SLOT :])
    far[...] = choose(odd, east, west)
    near[...] = choose(odd, west, east)


def first_kernel(
    x_hbm, gains_hbm, w_qkv_hbm, w_out_hbm, w_up_hbm, w_down_hbm, table_hbm, sel_hbm,
    oct_hbm, stream_out, far, near, table, lhs, bias, x, gains, w_qkv, w_out, w_up, w_down,
    rows, sel, to_oct, sems,
):
    pairs = (
        (table_hbm.at[pl.ds(0, 1)], rows), (sel_hbm, sel), (x_hbm, x), (gains_hbm, gains),
        (w_qkv_hbm.at[0], w_qkv), (w_out_hbm.at[0], w_out), (w_up_hbm.at[0], w_up),
        (w_down_hbm.at[0], w_down), (oct_hbm, to_oct),
    )
    copies = [pltpu.make_async_copy(a, b, sems.at[i]) for i, (a, b) in enumerate(pairs)]
    for copy in copies:
        copy.start()
    copies[0].wait()
    pick_table(rows, 0, level_at(0), table)
    lhs[...] = jnp.zeros_like(lhs)
    copies[1].wait()
    bias_regular(table, sel[...], lhs, bias)
    for copy in copies[2:5]:
        copy.wait()

    def arrive():
        for copy in copies[5:]:
            copy.wait()

    tokens = x[...].reshape(T, D)
    stream = regular_block(
        tokens, tokens, None, gains[0, 0:1], gains[0, 1:2], w_qkv[...],
        w_out, w_up, w_down, [bias], arrive,
    )
    packed = pack(stream.astype(F32))
    stream_out[...] = jnp.concatenate([packed, jnp.zeros((8, 128), BF)], axis=0)
    halves(stream, gains[1, 0:1], to_oct[...], parity("lon"), far, near)


def join_kernel(other, near, joined):
    joined[:144] = near[...]
    joined[144:] = other[...]


def partner_kernel(other, gains, to_oct, far, near):
    halves(unpack(other[...], T), gains[1, 0:1], to_oct[...], 1 - parity("lon"), far, near)


def middle_kernel(
    own_in, other_in, third_in, lower, above, q, k_own, v_own, gains, w_qkv, w_out, w_up, w_down,
    bias1, bias2, sides2, to_oct, back, side, side_oct, stream_out, beside_w, west, east, beside_e, k_ref, v_ref,
):
    odd = parity("lon")
    other, third = unpack(other_in[...], T), unpack(third_in[144:], T)
    stream = [choose(odd, other, third), unpack(own_in[...], T), choose(odd, third, other)]
    stream = shifted_block(
        jnp.concatenate(stream, axis=0).astype(BF), lower[...], above, q, k_own, v_own, gains[1, 1:2],
        w_qkv[1], w_out[1], w_up[1], w_down[1], bias1, back[...], k_ref, v_ref,
    )

    def worked(tokens):
        left, right = dot(side[1], tokens[:T]), dot(side[0], tokens[2 * T :])
        return jnp.concatenate([left, tokens[T : 2 * T].astype(F32), right], axis=0).astype(BF)

    stream = regular_block(
        stream, worked(stream), worked, gains[2, 0:1], gains[2, 1:2], w_qkv[2], w_out[2], w_up[2],
        w_down[2], [sides2.at[1], bias2, sides2.at[0]],
    )
    stream = stream.astype(F32)
    half = T // 2
    stream_out[...] = stream[half : half + T].astype(BF)
    normed = layer_norm(stream, gains[3, 0:1]).astype(F32)
    beside_w[...] = pack(dot(side_oct[...], normed[:half].astype(BF)))
    octs = dot(to_oct[...], normed[half : half + T].astype(BF))
    west[...] = pack(octs[: 4 * SLOT])
    east[...] = pack(octs[4 * SLOT :])
    beside_e[...] = pack(dot(side_oct[...], normed[half + T :].astype(BF)))


def last_kernel(
    stream_in, lower, above, q, k_own, v_own, gains, w_qkv, w_out, w_up, w_down, bias3, back, out,
    k_ref, v_ref,
):
    stream = shifted_block(
        stream_in[...], lower[...], above, q, k_own, v_own, gains[3, 1:2], w_qkv[3], w_out[3], w_up[3],
        w_down[3], bias3, back[...], k_ref, v_ref,
    )
    out[...] = stream.reshape(T // 2, 2, D)


def lat_rows(across):
    return -(-across * 3 * FILLED // 16) * 16


def lat_pack_kernel(mirrored, *refs):
    *columns, table_rows, far, near = refs
    if mirrored:
        third, gains, to_oct, *columns = columns
    parts = [unpack(ref[...]) for ref in columns]
    if mirrored:
        octs = dot(to_oct[...], layer_norm(unpack(third[144:], T), gains[1, 0:1]))
        west, east = octs[: 4 * SLOT], octs[4 * SLOT :]
        odd = parity("lon")
        sides = [choose(odd, east, west), choose(odd, west, east)]
        parts = [unpack(third[:144]), *sides, *parts]
        count = len(parts)
        parts = [choose(parity("lon"), parts[count - 1 - i], parts[i]) for i in range(count)]
    packed = []
    for yh in range(2):
        rows = [
            part[(yh * 2 + z) * SLOT : (yh * 2 + z) * SLOT + FILLED]
            for z in range(2)
            for part in parts
        ]
        packed.append(pack(jnp.concatenate(rows, axis=0)))
    size = lat_rows(len(parts))
    gap = size - packed[0].shape[0]
    if gap:
        packed = [jnp.concatenate([p, jnp.zeros((gap, 128), BF)], axis=0) for p in packed]
    far[:size] = choose(parity("lat"), packed[1], packed[0])
    near[:size] = choose(parity("lat"), packed[0], packed[1])
    far[size:] = table_rows[...]
    near[size:] = table_rows[...]


def lev_pack_kernel(
    across, recv_far, own_far, own_near, recv_near, down, up, own_down, own_up
):
    refs = (recv_far, own_far, own_near, recv_near)
    parts = [unpack(ref[: lat_rows(across)], across * 2 * FILLED) for ref in refs]
    parts = [choose(parity("lat"), parts[3 - i], parts[i]) for i in range(4)]
    half = across * FILLED
    for z, ref, own in ((0, down, own_down), (1, up, own_up)):
        tokens = jnp.concatenate([part[z * half : (z + 1) * half] for part in parts], axis=0)
        own[...] = spaced(tokens).astype(BF)
        ref[...] = pack(tokens)


def spaced(tokens):
    starts = range(0, tokens.shape[0], FILLED)
    gap = jnp.zeros((SLOT - FILLED, D), F32)
    rows = [part for at in starts for part in (tokens[at : at + FILLED], gap)]
    return jnp.concatenate(rows, axis=0)


def call(kernel, outs, *args, scratch=(), flops=0, limit=20, place=pltpu.VMEM):
    specs = [pl.BlockSpec(memory_space=place)] * len(args)
    if place == pltpu.HBM:
        args = [pltpu.with_memory_space_constraint(arg, place) for arg in args]
    return pl.pallas_call(
        kernel,
        out_shape=outs,
        in_specs=specs,
        scratch_shapes=list(scratch),
        compiler_params=pltpu.CompilerParams(vmem_limit_bytes=int(limit * (1 << 20))),
        cost_estimate=pl.CostEstimate(flops=flops, bytes_accessed=1 << 20, transcendentals=0),
    )(*args)


def shape(*dims, dtype=BF):
    return jax.ShapeDtypeStruct(dims, dtype)


def move(value, axis, steps):
    count = lax.axis_size(axis)
    return lax.ppermute(value, axis, [(i, (i + steps) % count) for i in range(count)])


def swap(value, axis, steps):
    count = lax.axis_size(axis)
    pairs = [(i, (i + (-steps if i % 2 else steps)) % count) for i in range(count)]
    return lax.ppermute(value, axis, pairs)


def kv_scratch(pairs):
    return [pltpu.VMEM((4, pairs, PAIR, D), BF)] * 2


def halo(block, columns, keep, send, w_qkv, sel_shift, pad):
    across = len(columns)
    far, near = call(
        functools.partial(lat_pack_kernel, block == 1), [shape(lat_rows(across) + 192, 128)] * 2,
        *columns, send, limit=4,
    )
    recv_far = swap(far, "lat", -1)
    recv_near = swap(near, "lat", 1)
    down, up, own_down, own_up = call(
        functools.partial(lev_pack_kernel, across),
        [shape(across * 108, 128)] * 2 + [shape(across * 96, D)] * 2,
        recv_far, far, near, recv_near, limit=4,
    )
    above = move(down, "lev", -1)
    below = move(up, "lev", 1)
    kv = shape(2, 4, across // 2, PAIR, D)
    q, k, v = call(
        functools.partial(own_keys_kernel, block),
        [shape((across - 2) * 4 * SLOT * HEADS, D), kv, kv],
        own_down, own_up, w_qkv, flops=1 << 30, limit=8,
    )
    bias = call(
        bias_shifted_kernel, shape(2, 8 * 144, 128, dtype=F32), keep, recv_far, recv_near,
        sel_shift, pad, flops=1 << 30, limit=8,
    )
    lower = call(
        functools.partial(lower_kernel, block), shape((across - 2) * 2 * SLOT, D), below, q, k, v,
        w_qkv, bias, scratch=kv_scratch(across // 2), flops=1 << 30, limit=8,
    )
    return lower, above, q, k, v, bias


def per_device(fields, w_qkv, w_out, w_up, w_down, gains, bias_table, labels):
    to_oct, back, side, side_oct = [jnp.asarray(m, BF) for m in octant_maps()]
    sel_reg, sel_shift, pad = selectors()
    sel_reg, sel_shift = jnp.asarray(sel_reg, BF), jnp.asarray(sel_shift, BF)
    pad = jnp.asarray(pad, F32)
    tables = bias_table[:, :, 0].transpose(0, 2, 1, 3)
    tags = labels.transpose(1, 0, 2)
    weights = (gains, w_qkv, w_out, w_up, w_down.transpose(0, 2, 1))

    bias_shape = (2, HEADS * T, 128)
    table_scratch = [pltpu.VMEM((HEADS, POS), F32), pltpu.VMEM((2, 2, 80, 128), F32)]
    half = shape(144, 128)
    stream, far, near = call(
        first_kernel, [shape(224, 128), half, half], fields.transpose(1, 2, 0, 3).reshape(T // 2, 2, D), *weights,
        tables, sel_reg, to_oct,
        scratch=[
            *table_scratch, pltpu.VMEM(bias_shape, F32), pltpu.VMEM((T // 2, 2, D), BF),
            pltpu.VMEM((BLOCKS, 2, D), F32), pltpu.VMEM((D, 3 * D), BF), pltpu.VMEM((D, D), BF),
            pltpu.VMEM((D, FF), BF), pltpu.VMEM((D, FF), BF), pltpu.VMEM((1, HEADS, 4, POS), BF),
            pltpu.VMEM((512, 256), BF), pltpu.VMEM((8 * SLOT, T), BF), pltpu.SemaphoreType.DMA((9,)),
        ],
        flops=1 << 31, place=pltpu.HBM,
    )
    other = swap(stream, "lon", 1)
    outer_own = swap(far, "lon", -2)
    rows = [shape(2, 2, 48, 128), shape(192, 128)]
    bias2, sides2, keep1, send1, keep3, send3 = call(
        tables_kernel,
        [shape(*bias_shape, dtype=F32), shape(2, 2, HEADS * T // 2, 128, dtype=F32), *rows, *rows],
        tables, tags, sel_reg,
        scratch=[*table_scratch, pltpu.VMEM((2, 2, 2, 48, 128), F32)], flops=1 << 31,
    )
    other, send1, outer_own = lax.optimization_barrier((other, send1, outer_own))
    joined = call(join_kernel, shape(368, 128), other, near, limit=4)
    third = swap(joined, "lon", 2)
    other_far, other_near = call(
        partner_kernel, [half, half], other, gains, to_oct, flops=1 << 28, limit=4
    )
    columns = (third, gains, to_oct, far, near, other_near, other_far, outer_own)
    *ready, bias1 = halo(1, columns, keep1, send1, w_qkv, sel_shift, pad)
    stream, *columns = call(
        middle_kernel, [shape(T, D), half, half, half, half], stream, other, third, *ready,
        *weights, bias1, bias2, sides2, to_oct, back, side, side_oct, scratch=kv_scratch(4), flops=1 << 31,
    )
    *ready, bias3 = halo(3, columns, keep3, send3, w_qkv, sel_shift, pad)
    stream = call(
        last_kernel, shape(T // 2, 2, D), stream, *ready, *weights, bias3, back,
        scratch=kv_scratch(2), flops=1 << 31,
    )
    return stream.reshape(6, 12, 2, D).transpose(2, 0, 1, 3)


def solution(mesh):
    in_specs = (
        P("lev", "lat", "lon", None),
        P(),
        P(),
        P(),
        P(),
        P(),
        P(None, None, "lat", None, None),
        P(None, "lat", "lon"),
    )
    return jax.shard_map(
        per_device,
        mesh=mesh,
        in_specs=in_specs,
        out_specs=P("lev", "lat", "lon", None),
        check_vma=False,
    )
```
